256 devices in a mesh: gx: 8 (over z), gy: 4 (over y_lo, core), gz: 8 (over y_hi, x).
Axes of the slice: x: 4, y: 4 (y_hi: 2, y_lo: 2; y = y_hi * 2 + y_lo), z: 8, core: 2. Of those that a mesh axis runs over, the one named last changes fastest.
Arguments:
- positions: float32 [3, 8, 4, 8, 32], P(None, 'gx', 'gy', 'gz'), may hold values from 0 to 32, as said below
- features: float32 [8, 4, 8, 32, 256], P('gx', 'gy', 'gz'), may hold values from -6 to 6
- plane_send: int32 [8, 4, 8, 2, 2, 8], P('gx', 'gy', 'gz'), may hold values from 0 to 31
- vertical_send: int32 [8, 4, 8, 2, 8], P('gx', 'gy', 'gz'), may hold values from 0 to 159, as said below
- neighbours: int32 [8, 4, 8, 32, 48], P('gx', 'gy', 'gz'), may hold values from 0 to 191, as said below
- counts: int32 [8, 4, 8, 32], P('gx', 'gy', 'gz'), may hold values from 1 to 48, as said below
- query_weight: float32 [2, 256, 256], replicated, may hold values from -0.375 to 0.375
- key_weight: float32 [2, 256, 256], replicated, may hold values from -0.375 to 0.375
- radial_weight: float32 [2, 8, 256], replicated, may hold values from -2 to 2
- mix_weight: bfloat16 [2, 256, 256], replicated, may hold values from -0.375 to 0.375
- vector_weight: bfloat16 [2, 256, 64], replicated, may hold values from -0.375 to 0.375
- head_weight: float32 [256, 256], replicated, may hold values from -0.375 to 0.375
- energy_weight: float32 [256], replicated, may hold values from -0.375 to 0.375
Outputs:
- energies: float32 [8, 4, 8, 32], P('gx', 'gy', 'gz')
- forces: float32 [3, 8, 4, 8, 32], P(None, 'gx', 'gy', 'gz')
- feature_grad: float32 [8, 4, 8, 32, 256], P('gx', 'gy', 'gz')
The draws below stay inside these ranges and needn't reach their ends.
Inputs may be any that keep to these rules, and one draw needn't show every extreme that they name: `vertical_send`: an own row, or a row of a plane cell that a neighbouring domain fills; never one of the four central cells, never a cell beyond the grid. `neighbours`: an own row other than the atom itself, a plane row as for vertical_send, or a row of z-cells 2 iz - 1 and 2 iz + 2. `counts`: every domain has an atom with all 48 slots live. `positions`: component 0 of domain (ix, iy, iz)'s atoms lies within 4 ix to 4 ix + 4, components 1 and 2 likewise with iy and iz.
All inputs are finite; a program needn't handle non-finite values.
Results may differ from the reference program's by a relative error of at most 0.011.
Values sent between devices are 32-bit elements; how exact they have to be, the bound alone decides.
A program may use at most 64 MiB of HBM per device.

```python
import math
import jax
import jax.numpy as jnp
from jax import lax

C = 256
CT = 64
NB = 8
K = 48
LAYERS = 2
A = 32
G = 8
N_GX = 8
N_GY = 4
N_GZ = 8


side = 4.0


def row_validity(total_rows):
    rows = jnp.arange(total_rows)
    cell = (rows - A) // G
    cell_x = cell // 4
    cell_y = cell % 4
    in_plane = (rows >= A) & (rows < A + 16 * G)
    border = (cell_x == 0) | (cell_x == 3) | (cell_y == 0) | (cell_y == 3)
    place_x = jnp.arange(N_GX)[:, None, None]
    place_y = jnp.arange(N_GY)[None, :, None]
    fits_x = ((cell_x != 0) | (place_x > 0)) & ((cell_x != 3) | (place_x < N_GX - 1))
    fits_y = ((cell_y != 0) | (place_y > 0)) & ((cell_y != 3) | (place_y < N_GY - 1))
    zone_cell = (rows - A - 16 * G) // G
    in_zone = (rows >= A + 16 * G) & ((zone_cell == 0) | (zone_cell == 3))
    valid = (rows < A) | in_plane & border & fits_x & fits_y | in_zone
    valid = jnp.broadcast_to(valid[:, :, None, :], (N_GX, N_GY, N_GZ, total_rows))
    return valid.astype(jnp.int32)


def pick_rows(key, valid, samples):
    total_rows = valid.shape[-1]
    rows = jnp.arange(total_rows)
    order = jnp.argsort((1 - valid) * total_rows + rows, axis=-1).astype(jnp.int32)
    lead = valid.shape[:-1]
    extra = (1,) * len(samples)
    available = jnp.sum(valid, axis=-1).reshape(lead + extra)
    raw_draw = jax.random.randint(key, lead + samples, 0, 2 ** 30)
    return (order, available, raw_draw % available)


def take_order(order, slot_pick):
    flat = slot_pick.reshape(order.shape[:-1] + (-1,))
    return jnp.take_along_axis(order, flat, axis=-1).reshape(slot_pick.shape)


def draw_vertical_send(key, part):
    key = jax.random.fold_in(key, 11)
    order, available, slot_pick = pick_rows(key, row_validity(A + 16 * G), (2, G))
    return take_order(order, slot_pick).astype(jnp.int32)


def draw_neighbours(key, part):
    key = jax.random.fold_in(key, 12)
    order, available, slot_pick = pick_rows(key, row_validity(A + 20 * G), (A, K))
    chosen = take_order(order, slot_pick)
    again = take_order(order, (slot_pick + 1) % available)
    itself = jnp.arange(A)[:, None]
    return jnp.where(chosen == itself, again, chosen).astype(jnp.int32)


def draw_counts(key, part):
    key = jax.random.fold_in(key, 13)
    key_level, key_raw, key_full = jax.random.split(key, 3)
    level = jax.random.randint(key_level, (N_GX, N_GY, N_GZ, 1), 1, 5)
    raw_count = jax.random.randint(key_raw, (N_GX, N_GY, N_GZ, A), 1, K + 1)
    scaled_count = jnp.clip(raw_count * level // 4, 1, K)
    full_at = jax.random.randint(key_full, (N_GX, N_GY, N_GZ, 1), 0, A)
    return jnp.where(jnp.arange(A) == full_at, K, scaled_count).astype(jnp.int32)


def draw_positions(key, part):
    key = jax.random.fold_in(key, 14)
    shape = (3, N_GX, N_GY, N_GZ, A)
    frac = jax.random.uniform(key, shape, jnp.float32, 0.05, 0.95)
    grid_x = jnp.broadcast_to(jnp.arange(N_GX)[:, None, None, None], shape[1:])
    grid_y = jnp.broadcast_to(jnp.arange(N_GY)[None, :, None, None], shape[1:])
    grid_z = jnp.broadcast_to(jnp.arange(N_GZ)[None, None, :, None], shape[1:])
    offset = jnp.stack([grid_x, grid_y, grid_z]).astype(jnp.float32)
    return ((offset + frac) * side).astype(jnp.float32)


def with_ends(entries, own_key, low, top_value):
    dims = entries.shape
    index_at = [jax.random.randint(jax.random.fold_in(own_key, axis), (), 0, dims[axis]) for axis in range(len(dims))]
    entries = entries.at[tuple(index_at)].set(low)
    longest = dims.index(max(dims))
    index_at[longest] = (index_at[longest] + 1) % dims[longest]
    return entries.at[tuple(index_at)].set(top_value)


def steps_of(stream_key, extent, cuts, smallest, top_value):
    def one(dim, shards_of):
        steps = jax.random.uniform(jax.random.fold_in(jax.random.fold_in(stream_key, 6), dim), (shards_of,), jnp.float32, smallest / len(cuts), top_value / len(cuts))
        return jnp.repeat(jnp.exp(steps), extent[dim] // shards_of).reshape((-1,) + (1,) * (len(extent) - dim - 1))

    level = one(*cuts[0])
    for cut in cuts[1:]:
        level = level * one(*cut)
    return level


def normal_values(stream_key, dims, spread, most, pieces=(), held_as=jnp.bfloat16):
    values = jax.random.normal(stream_key, dims, jnp.float32) * spread
    if len(pieces) > 0:
        values = steps_of(stream_key, dims, pieces, -0.22, 0.18) * values
    return jnp.clip(values, min=-most, max=most).astype(held_as)


def setup_inputs(seed: int = 0) -> dict:
    key_of = jax.random.split(jax.random.key(seed), 14)
    return {
        "positions": draw_positions(jax.random.fold_in(key_of[13], 71), 0),
        "features": normal_values(key_of[1], (N_GX, N_GY, N_GZ, A, C), 1.0, 6.0, ((0, 8), (1, 4), (2, 8)), jnp.float32),
        "plane_send": with_ends(jax.random.randint(key_of[2], (N_GX, N_GY, N_GZ, 2, 2, G), 0, A), jax.random.fold_in(key_of[2], 1), 0, A - 1).astype(jnp.int32),
        "vertical_send": draw_vertical_send(jax.random.fold_in(key_of[13], 71), 0),
        "neighbours": draw_neighbours(jax.random.fold_in(key_of[13], 71), 0),
        "counts": draw_counts(jax.random.fold_in(key_of[13], 71), 0),
        "query_weight": normal_values(key_of[6], (LAYERS, C, C), C ** -0.5, 0.375, (), jnp.float32),
        "key_weight": normal_values(key_of[7], (LAYERS, C, C), C ** -0.5, 0.375, (), jnp.float32),
        "radial_weight": normal_values(key_of[8], (LAYERS, NB, C), NB ** -0.5, 2.0, (), jnp.float32),
        "mix_weight": normal_values(key_of[9], (LAYERS, C, C), C ** -0.5, 0.375),
        "vector_weight": normal_values(key_of[10], (LAYERS, C, CT), C ** -0.5, 0.375),
        "head_weight": normal_values(key_of[11], (C, C), C ** -0.5, 0.375, (), jnp.float32),
        "energy_weight": normal_values(key_of[12], (C,), C ** -0.5, 0.375, (), jnp.float32),
    }


cutoff = 6.0
soften = 0.25
box_side = 4.0
highest = lax.Precision.HIGHEST

def edge_layer(pos_tab, key_rows, feat_own, neighbours, counts, query_weight, radial_weight, mix_weight, vector_weight):
    atom_count = feat_own.shape[0]
    slot_count = neighbours.shape[1]
    width_dim = feat_own.shape[1]
    queries = jnp.dot(feat_own, query_weight, precision=highest)
    own_places = pos_tab[:, :atom_count]
    others_pos = jnp.take(pos_tab, neighbours, axis=1)
    offsets = others_pos - own_places[:, :, None]
    distance = jnp.sqrt(lax.optimization_barrier(jnp.sum(offsets * offsets, axis=0)) + soften)
    scaled = distance / cutoff
    live_slots = (jnp.arange(slot_count)[None, :] < counts[:, None]).astype(jnp.float32)
    envelope = jnp.where(scaled < 1.0, (1.0 - scaled * scaled) ** 2, 0.0) * live_slots
    orders = jnp.arange(1, radial_weight.shape[0] + 1).astype(jnp.float32)
    basis_set = jnp.sin(jnp.pi * scaled[:, :, None] * orders) / scaled[:, :, None]
    radial = jnp.dot(basis_set.reshape(-1, basis_set.shape[2]), radial_weight, precision=highest)
    latent = queries[:, None, :] + jnp.take(key_rows, neighbours, axis=0) + radial.reshape(atom_count, slot_count, width_dim)
    active = jax.nn.silu(latent).astype(jnp.bfloat16).reshape(atom_count * slot_count, width_dim)
    mixed_rows = jnp.dot(active, mix_weight, preferred_element_type=jnp.float32).reshape(atom_count, slot_count, width_dim)
    factor = 1.0 / math.sqrt(slot_count)
    feat_new = feat_own + factor * lax.optimization_barrier(jnp.sum(envelope[:, :, None] * mixed_rows, axis=1))
    tensor = jnp.dot(active, vector_weight, preferred_element_type=jnp.float32).reshape(atom_count, slot_count, -1)
    weighted = envelope[:, :, None] * tensor
    direction = offsets / distance[None]
    vector = factor * jnp.einsum('akc,xak->xac', weighted, direction, precision=highest)
    vec_energy = lax.optimization_barrier(jnp.sum(vector * vector, axis=(0, 2))) / tensor.shape[2]
    return (feat_new, vec_energy)

def device_layer(own_pos, ghost_pos, feat_own, ghost_vals, neighbours, counts, query_weight, key_weight, radial_weight, mix_weight, vector_weight):
    key_rows = jnp.dot(jnp.concatenate([feat_own, ghost_vals], axis=0), key_weight, precision=highest)
    pos_tab = jnp.concatenate([own_pos, ghost_pos], axis=1)
    return edge_layer(pos_tab, key_rows, feat_own, neighbours, counts, query_weight, radial_weight, mix_weight, vector_weight)

def window_index(count):
    return 2 * jnp.arange(count)[:, None] + jnp.arange(4)[None, :]

def pick_blocks(values, index):
    return jax.vmap(lambda rows, where_rows: jnp.take(rows, where_rows, axis=0))(values, index)

def build_ghosts(values, plane_send, vertical_send, shift):
    size_x, size_y, size_z, own_count, feat_dim = values.shape
    block = plane_send.shape[-1]
    devices = size_x * size_y * size_z
    picked = pick_blocks(values.reshape(devices, own_count, feat_dim), plane_send.reshape(devices, 4 * block))
    cells = picked.reshape(size_x, size_y, size_z, 2, 2, block, feat_dim)
    cells = cells.transpose(0, 3, 1, 4, 2, 5, 6).reshape(2 * size_x, 2 * size_y, size_z, block, feat_dim)
    padded = jnp.pad(cells, ((1, 1), (1, 1), (0, 0), (0, 0), (0, 0)))
    plane = padded[window_index(size_x)]
    plane = plane[:, :, window_index(size_y)]
    plane = plane.transpose(0, 2, 4, 1, 3, 5, 6).reshape(size_x, size_y, size_z, 16 * block, feat_dim)
    first = jnp.concatenate([values, plane], axis=3)
    first_rows = first.shape[3]
    picked = pick_blocks(first.reshape(devices, first_rows, feat_dim), vertical_send.reshape(devices, 2 * block))
    cells = picked.reshape(size_x, size_y, 2 * size_z, block, feat_dim)
    wrapped = jnp.concatenate([cells[:, :, -1:] - shift, cells, cells[:, :, :1] + shift], axis=2)
    zone = wrapped[:, :, window_index(size_z)].reshape(size_x, size_y, size_z, 4 * block, feat_dim)
    return jnp.concatenate([plane, zone], axis=3)

def reference(positions, features, plane_send, vertical_send, neighbours, counts, query_weight, key_weight, radial_weight, mix_weight, vector_weight, head_weight, energy_weight):
    size_x, size_y, size_z, own_count, width_dim = features.shape
    devices = size_x * size_y * size_z
    zero_shift = jnp.zeros((width_dim,), jnp.float32)
    place_shift = jnp.array([0.0, 0.0, box_side * size_z], jnp.float32)
    flat_nbr = neighbours.reshape(devices, own_count, -1)
    flat_cnt = counts.reshape(devices, own_count)

    def total(places, feats):
        own_places = places.transpose(1, 2, 3, 4, 0)
        ghost_places = build_ghosts(own_places, plane_send, vertical_send, place_shift)
        ghost_flat = ghost_places.reshape(devices, -1, 3).transpose(0, 2, 1)
        own_flat = own_places.reshape(devices, own_count, 3).transpose(0, 2, 1)
        current = feats
        energy_sum = jnp.zeros((devices, own_count), jnp.float32)
        for layer_index in range(LAYERS):
            ghost_feats = build_ghosts(current, plane_send, vertical_send, zero_shift).reshape(devices, -1, width_dim)
            step = jax.checkpoint(lambda op, gp, fo, gv, nb, ct, li=layer_index: device_layer(op, gp, fo, gv, nb, ct, query_weight[li], key_weight[li], radial_weight[li], mix_weight[li], vector_weight[li]))
            new_feats, vec_energy = lax.map(lambda items: step(*items), (own_flat, ghost_flat, current.reshape(devices, own_count, width_dim), ghost_feats, flat_nbr, flat_cnt))
            energy_sum = energy_sum + vec_energy
            current = new_feats.reshape(size_x, size_y, size_z, own_count, width_dim)
        hidden = jax.nn.silu(jnp.dot(current.reshape(devices * own_count, width_dim), head_weight, precision=highest))
        head = jnp.dot(hidden, energy_weight, precision=highest)
        return (energy_sum.reshape(-1) + head).reshape(size_x, size_y, size_z, own_count)
    energies, pull_back = jax.vjp(total, positions, features)
    place_grad, feat_grad = pull_back(jnp.ones_like(energies))
    return (energies, -place_grad, feat_grad)
```

```python
import math

import jax
import jax.numpy as jnp
from jax import lax
from jax.experimental import pallas as pl
from jax.experimental.pallas import tpu as pltpu
from jax.sharding import PartitionSpec as P

A, S, C, CT, NB, G = 32, 48, 256, 64, 8, 8
LAYERS = 2
EDGES = A * S
STEP = 256
CHUNKS = EDGES // STEP
CUTOFF, SOFTEN, BOX_SIDE = 6.0, 0.25, 4.0
FACTOR = 1.0 / math.sqrt(S)
F32, BF = jnp.float32, jnp.bfloat16

MESSAGES = (
    (1, 0, ((1, 0), (1, 1))),
    (-1, 0, ((0, 0), (0, 1))),
    (0, 1, ((0, 1), (1, 1))),
    (0, -1, ((0, 0), (1, 0))),
    (1, 1, ((1, 1),)),
    (1, -1, ((1, 0),)),
    (-1, 1, ((0, 1),)),
    (-1, -1, ((0, 0),)),
)
BLOCKS = tuple((dx, dy, a, b) for dx, dy, quads in MESSAGES for a, b in quads)
PLANE = G * len(BLOCKS)
FIRST = A + PLANE
ROWS = FIRST + 2 * G
LABELS = tuple(range(0, A, G)) + tuple(
    A + ((1 - 2 * dx + a) * 4 + 1 - 2 * dy + b) * G for dx, dy, a, b in BLOCKS
) + (A + 16 * G, A + 19 * G)
SELF = ROWS + A
DEPTH = 256


def mm(a, b):
    return lax.dot_general(a, b, (((1,), (0,)), ((), ())), preferred_element_type=F32)


def mm_nt(a, b):
    return lax.dot_general(a, b, (((1,), (1,)), ((), ())), preferred_element_type=F32)


def split(x):
    hi = x.astype(BF)
    return hi, (x - hi.astype(F32)).astype(BF)


def split3(x):
    hi, rest = x.astype(BF), x - x.astype(BF).astype(F32)
    mid = rest.astype(BF)
    return hi, mid, (rest - mid.astype(F32)).astype(BF)


def exact(product, a, b):
    ah, al = split(a)
    bh, bl = split(b)
    return product(ah, bh) + (product(ah, bl) + product(al, bh))


def iota(shape, dim):
    return lax.broadcasted_iota(jnp.int32, shape, dim)


def kernel(
    pos, feat, ps, vs, nbr, cnt, wr, we, wq_in, wk_in, wm_in, wv_in, wh_in,
    en_out, force_out, grad_out,
    wq, wk, wm, wv, wh,
    key_tab, key_send, face_send, pos_tab, pos_send, pos_face,
    dkey, key_back, key_ret, key_mine, dpos, pos_back, pos_ret, pos_mine,
    edge, weight, act, slope, dlat, mt, basis_s, dbasis_s, dw, db, dr_s,
    load_sem, send_sem, recv_sem,
):
    ix, iy, iz = (lax.axis_index(n) for n in ("gx", "gy", "gz"))
    nx, ny, nz = (lax.axis_size(n) for n in ("gx", "gy", "gz"))

    def at(dx, dy, dz):
        return {
            "gx": lax.rem(ix + (dx + nx), nx),
            "gy": lax.rem(iy + (dy + ny), ny),
            "gz": lax.rem(iz + (dz + nz), nz),
        }

    loads = {}
    for n, (name, src, dst) in enumerate(
        (
            ("wk", wk_in, wk),
            ("wq", wq_in, wq),
            ("wm", wm_in, wm),
            ("wv", wv_in, wv),
            ("wh", wh_in, wh),
        )
    ):
        loads[name] = pltpu.make_async_copy(src, dst, load_sem.at[n])
        loads[name].start()

    barrier = pltpu.get_barrier_semaphore()
    around = [(dx, dy, 0) for dx, dy, _ in MESSAGES] + [(0, 0, -1), (0, 0, 1)]
    for step in around:
        pl.semaphore_signal(barrier, inc=1, device_id=at(*step), device_id_type=pl.DeviceIdType.MESH)

    def remote(stage, src, dst, where):
        pltpu.make_async_remote_copy(
            src_ref=src,
            dst_ref=dst,
            send_sem=send_sem.at[stage],
            recv_sem=recv_sem.at[stage],
            device_id=where,
            device_id_type=pl.DeviceIdType.MESH,
        ).start()

    def plane(stage, src, src_at, dst, dst_at, sign):
        row = 0
        for dx, dy, quads in MESSAGES:
            rows = G * len(quads)
            remote(
                stage,
                src.at[pl.ds(src_at + row, rows)],
                dst.at[pl.ds(dst_at + row, rows)],
                at(sign * dx, sign * dy, 0),
            )
            row += rows

    def zone(stage, src, src_at, dst, dst_at):
        remote(stage, src.at[pl.ds(src_at, G)], dst.at[pl.ds(dst_at + G, G)], at(0, 0, -1))
        remote(stage, src.at[pl.ds(src_at + G, G)], dst.at[pl.ds(dst_at, G)], at(0, 0, 1))

    def arrived(stage, buf, row, rows):
        part = buf.at[pl.ds(row, rows)]
        pltpu.make_async_copy(part, part, recv_sem.at[stage]).wait()

    def sent(stage, buf, row, rows):
        part = buf.at[pl.ds(row, rows)]
        pltpu.make_async_copy(part, part, send_sem.at[stage]).wait()

    sub8, lane8 = iota((G, G), 0), iota((G, G), 1)

    def column(row):
        return jnp.sum(jnp.where(sub8 == lane8, row.astype(F32), 0.0), axis=1, keepdims=True)

    quads = [column(ps[q : q + 1, :]) for q in range(4)]
    lane32 = iota((G, A), 1).astype(F32)
    picks = [jnp.where(quads[2 * a + b] == lane32, 1.0, 0.0) for _, _, a, b in BLOCKS]
    eye = jnp.where(iota((A, A), 0) == iota((A, A), 1), 1.0, 0.0)
    pick_f = jnp.concatenate([eye] + picks, axis=0)
    pick = pick_f.astype(BF)

    own_parts = split3(pos[...])

    def place_rows(part):
        wide = jnp.concatenate([part.astype(F32), jnp.zeros((128 - 3, A), F32)], axis=0)
        return mm_nt(pick, wide.astype(BF))

    place = place_rows(own_parts[0]) + place_rows(own_parts[1]) + place_rows(own_parts[2])
    pos_tab[pl.ds(0, A), :] = place[:A]
    pos_send[...] = place[A:]

    pl.semaphore_wait(barrier, len(around))
    plane(0, pos_send, 0, pos_tab, A, 1)

    loads["wk"].wait()
    h0 = feat[...]

    def send_keys(layer, h):
        keys = exact(mm, h, wk[layer])
        rows = mm(pick, keys.astype(BF))
        key_tab[layer, pl.ds(0, A), :] = rows[:A]
        key_send[layer] = rows[A:]
        plane(2 + 2 * layer, key_send.at[layer], 0, key_tab.at[layer], A, 1)

    send_keys(0, h0)

    lane_first = iota((1, FIRST), 1)
    label_row = lane_first
    for n in range(A // G, FIRST // G):
        label_row = label_row + jnp.where(lane_first // G == n, LABELS[n] - n * G, 0)
    label_row = label_row.astype(F32)
    face_f = jnp.concatenate(
        [jnp.where(column(vs[f : f + 1, :]) == label_row, 1.0, 0.0) for f in range(2)], axis=0
    )
    face = face_f.astype(BF)
    face_t = jnp.concatenate([face_f, face_f], axis=0).T.astype(BF)
    pick_q = pick_f[A:]
    pick_t = jnp.concatenate([pick_q, pick_q], axis=0).T.astype(BF)

    atom = iota((A, EDGES), 1) & (A - 1)
    mine = atom == iota((A, EDGES), 0)
    slot_pick = jnp.where((iota((S, EDGES), 1) >> 5) == iota((S, EDGES), 0), 1.0, 0.0).astype(BF)
    nbr_all = mm(nbr[...].astype(F32).astype(BF), slot_pick)
    nbr_row = jnp.sum(jnp.where(mine, nbr_all, 0.0), axis=0, keepdims=True)
    mine_f = jnp.where(mine, 1.0, 0.0)
    mine_b = mine_f.astype(BF)
    cnt_rows = jnp.broadcast_to(cnt[...].astype(F32), (16, A)).astype(BF)
    cnt_row = mm(cnt_rows, mine_b)[0:1]
    live = jnp.where((iota((1, EDGES), 1) >> 5).astype(F32) < cnt_row, 1.0, 0.0)
    tile = iota((16, EDGES), 0)
    for n in range(ROWS // 16):
        low, high = LABELS[2 * n], LABELS[2 * n + 1]
        label = jnp.where(tile < G, tile + low, tile + (high - G)).astype(F32)
        edge[pl.ds(16 * n, 16), :] = jnp.where(nbr_row == label, 1.0, 0.0).astype(BF)
    edge[pl.ds(ROWS, A), :] = mine_b
    edge[pl.ds(SELF, DEPTH - SELF), :] = jnp.zeros((DEPTH - SELF, EDGES), BF)
    dr_s[...] = jnp.zeros_like(dr_s)

    arrived(0, pos_tab, A, PLANE)
    first = pos_tab[pl.ds(0, FIRST), :]
    rows = sum(mm(face, part) for part in split3(first))
    span = BOX_SIDE * nz
    low_shift = jnp.where(iz == 0, span, 0.0).astype(F32)
    high_shift = jnp.where(iz == nz - 1, -span, 0.0).astype(F32)
    shift = jnp.where(iota((2 * G, 128), 0) < G, low_shift, high_shift)
    pos_face[...] = rows + jnp.where(iota((2 * G, 128), 1) == 2, shift, 0.0)
    zone(1, pos_face, 0, pos_tab, FIRST)

    def send_faces(layer):
        arrived(2 + 2 * layer, key_tab.at[layer], A, PLANE)
        first_keys = key_tab[layer, pl.ds(0, FIRST), :].astype(BF)
        face_send[layer] = mm(face, first_keys)
        zone(3 + 2 * layer, face_send.at[layer], 0, key_tab.at[layer], FIRST)

    send_faces(0)

    arrived(1, pos_tab, FIRST, 2 * G)
    place = jnp.concatenate([pos_tab[...], -pos_tab[pl.ds(0, A), :]], axis=0)
    place = jnp.concatenate([place, jnp.zeros((DEPTH - SELF, 128), F32)], axis=0)
    place_t = place.T[0:G, :]
    parts = [part.astype(F32) for part in split3(place_t)] + [jnp.zeros((G, DEPTH), F32)]
    offset = mm(jnp.concatenate(parts, axis=0).astype(BF), edge[...])
    offset = offset[0:G] + (offset[G : 2 * G] + offset[2 * G : 3 * G])
    dist2 = jnp.sum(offset * offset, axis=0, keepdims=True) + SOFTEN
    dist = jnp.sqrt(dist2)
    inv = 1.0 / dist
    scaled = dist * (1.0 / CUTOFF)
    gap = 1.0 - scaled * scaled
    inside = jnp.where(scaled < 1.0, live, 0.0)
    envelope = inside * gap * gap
    direction = offset * inv
    order = (iota((NB, EDGES), 0) + 1).astype(F32)
    turn = order * scaled
    whole = jnp.floor(turn + 0.5)
    angle = (turn - whole) * math.pi
    sign = 1.0 - 2.0 * (whole - 2.0 * jnp.floor(0.5 * whole))
    sq = angle * angle
    sine, cosine = jnp.zeros_like(sq), jnp.zeros_like(sq)
    for n in range(6, -1, -1):
        sine = sine * sq + (-1.0) ** n / math.factorial(2 * n + 1)
        cosine = cosine * sq + (-1.0) ** n / math.factorial(2 * n)
    inv_scaled = CUTOFF * inv
    basis = sign * sine * angle * inv_scaled
    basis_s[...] = basis
    dbasis_s[...] = (order * math.pi * sign * cosine - basis) * inv_scaled
    basis_h, basis_l = split(basis)
    basis_h, basis_l = basis_h.astype(F32), basis_l.astype(F32)
    edge[pl.ds(SELF, 32), :] = jnp.concatenate(
        [basis_h, basis_l, basis_h, jnp.zeros_like(basis)], axis=0
    ).astype(BF)
    for q in range(4):
        row = envelope if q == 0 else envelope * direction[q - 1 : q]
        w_h, w_l = split(row * mine_f)
        weight[pl.ds(A * q, A), :] = w_h
        weight[pl.ds(4 * A + A * q, A), :] = w_l

    def forward(layer, h, queries):
        radial = wr[layer]
        radial_h, radial_l = split(radial)
        radial_h, radial_l = radial_h.astype(F32), radial_l.astype(F32)
        arrived(3 + 2 * layer, key_tab.at[layer], FIRST, 2 * G)
        rows = jnp.concatenate(
            [
                key_tab[layer],
                queries,
                radial_h,
                radial_h,
                radial_l,
                jnp.zeros((DEPTH - SELF - 3 * NB, C), F32),
            ],
            axis=0,
        )
        mt[...] = rows.T.astype(BF)

        def step(n, carry):
            part = pl.ds(pl.multiple_of(n * STEP, STEP), STEP)
            latent = mm(mt[...], edge[:, part])
            gate = 0.5 * jnp.tanh(0.5 * latent) + 0.5
            active = latent * gate
            act[layer, :, part] = active.astype(BF)
            slope[layer, :, part] = gate + active * (1.0 - gate)
            return carry

        lax.fori_loop(0, CHUNKS, step, 0)
        total = mm_nt(weight[...], act[layer])
        total = total[: 4 * A] + total[4 * A :]
        gather_h, gather_l = split(total[:A])
        new = h + FACTOR * (mm(gather_h, wm[layer]) + mm(gather_l, wm[layer]))
        vec_h, vec_l = split(total[A:])
        vector = FACTOR * (mm(vec_h, wv[layer]) + mm(vec_l, wv[layer]))
        return new, vector

    loads["wq"].wait()
    q0 = exact(mm, h0, wq[0])
    loads["wm"].wait()
    loads["wv"].wait()
    h1, v0 = forward(0, h0, q0)
    send_keys(1, h1)
    q1 = exact(mm, h1, wq[1])
    send_faces(1)
    loads["wh"].wait()
    h2, v1 = forward(1, h1, q1)

    lat = exact(mm, h2, wh[...])
    gate = 0.5 * jnp.tanh(0.5 * lat) + 0.5
    hidden = lat * gate
    readout = we[...]
    square = v0 * v0 + v1 * v1
    square = square[:A] + (square[A : 2 * A] + square[2 * A :])
    energy = jnp.sum(hidden * readout, axis=1, keepdims=True) + jnp.sum(
        square, axis=1, keepdims=True
    ) * (1.0 / CT)
    en_out[...] = jnp.sum(eye * energy, axis=0, keepdims=True)
    dh2 = exact(mm_nt, readout * (gate + hidden * (1.0 - gate)), wh[...])

    chunk_mine = mine_f[:, :STEP]

    def backward(layer, dh, vector):
        dh_h, dh_l = split(dh)
        g0 = FACTOR * (mm_nt(dh_h, wm[layer]) + mm_nt(dh_l, wm[layer]))
        dv_h, dv_l = split(vector * (2.0 / CT))
        gx = FACTOR * (mm_nt(dv_h, wv[layer]) + mm_nt(dv_l, wv[layer]))
        pull = jnp.concatenate([g0, gx], axis=0)
        pull_b = pull.astype(BF)
        mt[...] = jnp.concatenate([pull, pull], axis=0).T.astype(BF)
        radial_h, radial_l = split(wr[layer])
        radial = jnp.concatenate([radial_h.astype(F32), radial_l.astype(F32)], axis=0).astype(BF)

        def step(n, carry):
            part = pl.ds(pl.multiple_of(n * STEP, STEP), STEP)
            dl = (mm(mt[...], weight[:, part]) * slope[layer, :, part]).astype(BF)
            dlat[:, part] = dl
            cross = mm(pull_b, act[layer, :, part])
            rows = [
                jnp.sum(cross[A * q : A * q + A] * chunk_mine, axis=0, keepdims=True)
                for q in range(4)
            ]
            rows = jnp.concatenate(rows + [jnp.zeros((4, STEP), F32)], axis=0)
            got = mm(radial, dl)
            got = got[:NB] + got[NB:]
            if layer == LAYERS - 1:
                dw[:, part] = rows
                db[:, part] = got
            else:
                dw[:, part] += rows
                db[:, part] += got
            return carry

        lax.fori_loop(0, CHUNKS, step, 0)
        drows = mm_nt(edge[pl.ds(0, SELF), :], dlat[...])
        dkey[layer] = drows[:ROWS]
        zone(6 + 2 * layer, dkey.at[layer], FIRST, key_back.at[layer], 0)
        return drows[ROWS:]

    def add_faces(first, back):
        back_h, back_l = split(back)
        return first + mm(face_t, jnp.concatenate([back_h, back_l], axis=0))

    def add_quads(own, back):
        back_h, back_l = split(back)
        return own + mm(pick_t, jnp.concatenate([back_h, back_l], axis=0))

    def return_planes(layer):
        arrived(6 + 2 * layer, key_back.at[layer], 0, 2 * G)
        total = add_faces(dkey[layer, pl.ds(0, FIRST), :], key_back[layer])
        key_ret[layer] = total[A:]
        plane(7 + 2 * layer, key_ret.at[layer], 0, key_mine.at[layer], 0, -1)
        return total[:A]

    def finish(layer, own, dh, dquery):
        arrived(7 + 2 * layer, key_mine.at[layer], 0, PLANE)
        own = add_quads(own, key_mine[layer])
        return dh + dquery + exact(mm_nt, own, wk[layer])

    dq1 = backward(1, dh2, v1)
    dq1 = exact(mm_nt, dq1, wq[1])
    own1 = return_planes(1)
    dh1 = finish(1, own1, dh2, dq1)
    dq0 = backward(0, dh1, v0)

    de = dw[0:1]
    unit = direction
    for q in range(3):
        de = de + dw[q + 1 : q + 2] * unit[q : q + 1]
    lanes = iota((G, EDGES), 0)
    du = jnp.zeros((G, EDGES), F32)
    for q in range(3):
        du = jnp.where(lanes == q, dw[q + 1 : q + 2], du)
    du = du * envelope
    dscaled = -4.0 * inside * gap * scaled * de + jnp.sum(
        db[...] * dbasis_s[...], axis=0, keepdims=True
    )
    ddist = dscaled * (1.0 / CUTOFF) - inv * jnp.sum(du * unit, axis=0, keepdims=True)
    dr_h, dr_l = split(du * inv + unit * ddist)
    dr_s[pl.ds(0, 16), :] = jnp.concatenate([dr_h.astype(F32), dr_l.astype(F32)], axis=0).astype(BF)
    rows = mm_nt(edge[pl.ds(0, SELF), :], dr_s[...])
    dpos[...] = rows[:ROWS]
    zone(10, dpos, FIRST, pos_back, 0)
    pos_own = rows[:A] - rows[ROWS:]

    own0 = return_planes(0)
    dq0 = exact(mm_nt, dq0, wq[0])
    arrived(10, pos_back, 0, 2 * G)
    total = add_faces(dpos[pl.ds(0, FIRST), :], pos_back[...])
    pos_ret[...] = total[A:]
    plane(11, pos_ret, 0, pos_mine, 0, -1)
    pos_own = total[:A] - rows[ROWS:]
    grad_out[...] = finish(0, own0, dh1, dq0)
    arrived(11, pos_mine, 0, PLANE)
    pos_own = add_quads(pos_own, pos_mine[...])
    pos_own = jnp.concatenate([pos_own, jnp.zeros((128 - A, 128), F32)], axis=0).T
    force_out[...] = -(pos_own[0:3, :A] + pos_own[G : G + 3, :A])

    sent(0, pos_send, 0, PLANE)
    sent(1, pos_face, 0, 2 * G)
    for layer in range(LAYERS):
        sent(2 + 2 * layer, key_send.at[layer], 0, PLANE)
        sent(3 + 2 * layer, face_send.at[layer], 0, 2 * G)
        sent(6 + 2 * layer, dkey.at[layer], FIRST, 2 * G)
        sent(7 + 2 * layer, key_ret.at[layer], 0, PLANE)
    sent(10, dpos, FIRST, 2 * G)
    sent(11, pos_ret, 0, PLANE)


def per_device(
    positions, features, plane_send, vertical_send, neighbours, counts,
    query_weight, key_weight, radial_weight, mix_weight, vector_weight, head_weight, energy_weight,
):
    vmem = pl.BlockSpec(memory_space=pltpu.VMEM)
    hbm = pl.BlockSpec(memory_space=pl.ANY)
    energies, forces, grad = pl.pallas_call(
        kernel,
        out_shape=(
            jax.ShapeDtypeStruct((1, A), F32),
            jax.ShapeDtypeStruct((3, A), F32),
            jax.ShapeDtypeStruct((A, C), F32),
        ),
        in_specs=[vmem] * 8 + [hbm] * 5,
        out_specs=(vmem,) * 3,
        scratch_shapes=[
            pltpu.VMEM((LAYERS, C, C), F32),
            pltpu.VMEM((LAYERS, C, C), F32),
            pltpu.VMEM((LAYERS, C, C), BF),
            pltpu.VMEM((LAYERS, C, CT), BF),
            pltpu.VMEM((C, C), F32),
            pltpu.VMEM((LAYERS, ROWS, C), F32),
            pltpu.VMEM((LAYERS, PLANE, C), F32),
            pltpu.VMEM((LAYERS, 2 * G, C), F32),
            pltpu.VMEM((ROWS, 128), F32),
            pltpu.VMEM((PLANE, 128), F32),
            pltpu.VMEM((2 * G, 128), F32),
            pltpu.VMEM((LAYERS, ROWS, C), F32),
            pltpu.VMEM((LAYERS, 2 * G, C), F32),
            pltpu.VMEM((LAYERS, PLANE, C), F32),
            pltpu.VMEM((LAYERS, PLANE, C), F32),
            pltpu.VMEM((ROWS, 128), F32),
            pltpu.VMEM((2 * G, 128), F32),
            pltpu.VMEM((PLANE, 128), F32),
            pltpu.VMEM((PLANE, 128), F32),
            pltpu.VMEM((DEPTH, EDGES), BF),
            pltpu.VMEM((8 * A, EDGES), BF),
            pltpu.VMEM((LAYERS, C, EDGES), BF),
            pltpu.VMEM((LAYERS, C, EDGES), F32),
            pltpu.VMEM((C, EDGES), BF),
            pltpu.VMEM((C, C), BF),
            pltpu.VMEM((NB, EDGES), F32),
            pltpu.VMEM((NB, EDGES), F32),
            pltpu.VMEM((8, EDGES), F32),
            pltpu.VMEM((NB, EDGES), F32),
            pltpu.VMEM((128, EDGES), BF),
            pltpu.SemaphoreType.DMA((5,)),
            pltpu.SemaphoreType.DMA((12,)),
            pltpu.SemaphoreType.DMA((12,)),
        ],
        compiler_params=pltpu.CompilerParams(
            collective_id=0, has_side_effects=True, vmem_limit_bytes=32 * 1024 * 1024
        ),
        cost_estimate=pl.CostEstimate(
            flops=2_500_000_000, bytes_accessed=2_000_000, transcendentals=800_000
        ),
    )(
        positions.reshape(3, A),
        features.reshape(A, C),
        plane_send.reshape(4, G),
        vertical_send.reshape(2, G),
        neighbours.reshape(A, S),
        counts.reshape(1, A),
        radial_weight,
        energy_weight.reshape(1, C),
        query_weight,
        key_weight,
        mix_weight,
        vector_weight,
        head_weight,
    )
    return (
        energies.reshape(1, 1, 1, A),
        forces.reshape(3, 1, 1, 1, A),
        grad.reshape(1, 1, 1, A, C),
    )


def solution(mesh):
    return jax.shard_map(
        per_device,
        mesh=mesh,
        in_specs=(
            P(None, "gx", "gy", "gz", None),
            P("gx", "gy", "gz", None, None),
            P("gx", "gy", "gz", None, None, None),
            P("gx", "gy", "gz", None, None),
            P("gx", "gy", "gz", None, None),
            P("gx", "gy", "gz", None),
            P(),
            P(),
            P(),
            P(),
            P(),
            P(),
            P(),
        ),
        out_specs=(
            P("gx", "gy", "gz", None),
            P(None, "gx", "gy", "gz", None),
            P("gx", "gy", "gz", None, None),
        ),
        check_vma=False,
    )
```

```python
import math

import jax
import jax.numpy as jnp
from jax import lax
from jax.experimental import pallas as pl
from jax.experimental.pallas import tpu as pltpu
from jax.sharding import PartitionSpec as P

A, S, C, CT, NB, G = 32, 48, 256, 64, 8, 8
LAYERS = 2
EDGES = A * S
STEP = 256
CHUNKS = EDGES // STEP
CUTOFF, SOFTEN, BOX_SIDE = 6.0, 0.25, 4.0
FACTOR = 1.0 / math.sqrt(S)
F32, BF = jnp.float32, jnp.bfloat16

MESSAGES = (
    (1, 0, ((1, 0), (1, 1))),
    (-1, 0, ((0, 0), (0, 1))),
    (0, 1, ((0, 1), (1, 1))),
    (0, -1, ((0, 0), (1, 0))),
    (1, 1, ((1, 1),)),
    (1, -1, ((1, 0),)),
    (-1, 1, ((0, 1),)),
    (-1, -1, ((0, 0),)),
)
BLOCKS = tuple((dx, dy, a, b) for dx, dy, quads in MESSAGES for a, b in quads)
PLANE = G * len(BLOCKS)
FIRST = A + PLANE
ROWS = FIRST + 2 * G
LABELS = tuple(range(0, A, G)) + tuple(
    A + ((1 - 2 * dx + a) * 4 + 1 - 2 * dy + b) * G for dx, dy, a, b in BLOCKS
) + (A + 16 * G, A + 19 * G)
SELF = ROWS + A
DEPTH = 256
PLACES = tuple((dx, dy) for dx, dy, _ in MESSAGES) + ((0, 0),)
ZONE = 2 * G * len(PLACES)
BACK = PLANE + ZONE


def mm(a, b):
    return lax.dot_general(a, b, (((1,), (0,)), ((), ())), preferred_element_type=F32)


def mm_nt(a, b):
    return lax.dot_general(a, b, (((1,), (1,)), ((), ())), preferred_element_type=F32)


def split(x):
    hi = x.astype(BF)
    return hi, (x - hi.astype(F32)).astype(BF)


def split3(x):
    hi, rest = x.astype(BF), x - x.astype(BF).astype(F32)
    mid = rest.astype(BF)
    return hi, mid, (rest - mid.astype(F32)).astype(BF)


def exact(product, a, b):
    ah, al = split(a)
    bh, bl = split(b)
    return product(ah, bh) + (product(ah, bl) + product(al, bh))


def iota(shape, dim):
    return lax.broadcasted_iota(jnp.int32, shape, dim)


def kernel(
    pos_in, feat_in, ps_in, vs_in, nbr_in, cnt_in, wq_in, wk_in, wr_in, wm_in, wv_in, wh_in, we_in,
    en_out, force_out, grad_out,
    pos, feat, ps, vs, nbr, cnt, wq, wk, wr, wm, wv, wh, we,
    face_mine, face_all, pos_tab, pos_send, pos_face, pos_grad, pos_back,
    key_tab, key_send, face_send, zone_in, dkey, key_back,
    pick_all, pick_back, mine_s, geo, unit_s, dbasis_s, edge, weight, act, slope, dlat,
    mt, mp, dw, db, dr_s, h1_s, h2_s, dh_s, dq_s, own_s, query_s, vec_s,
    load_sem, send_sem, recv_sem,
):
    ix, iy, iz = (lax.axis_index(n) for n in ("gx", "gy", "gz"))
    nx, ny, nz = (lax.axis_size(n) for n in ("gx", "gy", "gz"))

    def at(dx, dy, dz):
        return {
            "gx": lax.rem(ix + (dx + nx), nx),
            "gy": lax.rem(iy + (dy + ny), ny),
            "gz": lax.rem(iz + (dz + nz), nz),
        }

    loads = {}
    for n, (name, src, dst) in enumerate(
        (
            ("ps", ps_in, ps),
            ("pos", pos_in, pos),
            ("feat", feat_in, feat),
            ("wk", wk_in, wk),
            ("vs", vs_in, vs),
            ("nbr", nbr_in, nbr),
            ("cnt", cnt_in, cnt),
            ("wr", wr_in, wr),
            ("wq", wq_in, wq),
            ("wm", wm_in, wm),
            ("wv", wv_in, wv),
            ("wh", wh_in, wh),
            ("we", we_in, we),
        )
    ):
        loads[name] = pltpu.make_async_copy(src, dst, load_sem.at[n])
        loads[name].start()

    barrier = pltpu.get_barrier_semaphore()
    around = [(dx, dy, 0) for dx, dy, _ in MESSAGES] + [(0, 0, -1), (0, 0, 1)]
    for step in around:
        pl.semaphore_signal(barrier, inc=1, device_id=at(*step), device_id_type=pl.DeviceIdType.MESH)

    def remote(stage, src, dst, where):
        pltpu.make_async_remote_copy(
            src_ref=src,
            dst_ref=dst,
            send_sem=send_sem.at[stage],
            recv_sem=recv_sem.at[stage],
            device_id=where,
            device_id_type=pl.DeviceIdType.MESH,
        ).start()

    def plane(stage, src, src_at, dst, dst_at, sign):
        row = 0
        for dx, dy, quads in MESSAGES:
            rows = G * len(quads)
            remote(
                stage,
                src.at[pl.ds(src_at + row, rows)],
                dst.at[pl.ds(dst_at + row, rows)],
                at(sign * dx, sign * dy, 0),
            )
            row += rows

    def zone(stage, src, src_at, dst, dst_at):
        remote(stage, src.at[pl.ds(src_at, G)], dst.at[pl.ds(dst_at + G, G)], at(0, 0, -1))
        remote(stage, src.at[pl.ds(src_at + G, G)], dst.at[pl.ds(dst_at, G)], at(0, 0, 1))

    def zone_out(stage, src, src_at, dst):
        for m, (dx, dy) in enumerate(PLACES):
            for f, dz in ((0, -1), (1, 1)):
                remote(
                    stage,
                    src.at[pl.ds(src_at + (2 * m + f) * G, G)],
                    dst.at[pl.ds((2 * m + 1 - f) * G, G)],
                    at(-dx, -dy, dz),
                )

    def give_back(stage, src, dst):
        for m, (dx, dy) in enumerate(PLACES):
            for b, dz in ((0, -1), (1, 1)):
                remote(
                    stage,
                    src.at[pl.ds(FIRST + b * G, G)],
                    dst.at[pl.ds(PLANE + (2 * m + 1 - b) * G, G)],
                    at(dx, dy, dz),
                )
        plane(stage, src, A, dst, 0, -1)

    def arrived(stage, buf, row, rows):
        part = buf.at[pl.ds(row, rows)]

        @pl.when(ix >= 0)
        def _():
            pltpu.make_async_copy(part, part, recv_sem.at[stage]).wait()

    def sent(stage, buf, row, rows):
        part = buf.at[pl.ds(row, rows)]
        pltpu.make_async_copy(part, part, send_sem.at[stage]).wait()

    sub8, lane8 = iota((G, G), 0), iota((G, G), 1)

    def column(row):
        return jnp.sum(jnp.where(sub8 == lane8, row.astype(F32), 0.0), axis=1, keepdims=True)

    loads["ps"].wait()
    lane32 = iota((G, A), 1).astype(F32)
    quads = {
        (a, b): jnp.where(column(ps[0, 0, 0, a, b : b + 1, :]) == lane32, 1.0, 0.0)
        for a in range(2)
        for b in range(2)
    }
    eye = jnp.where(iota((A, A), 0) == iota((A, A), 1), 1.0, 0.0)
    pick_f = jnp.concatenate([eye] + [quads[a, b] for _, _, a, b in BLOCKS], axis=0)
    pick = pick_f.astype(BF)
    pick_all[pl.ds(0, FIRST), :] = pick

    loads["pos"].wait()
    own_parts = split3(jnp.concatenate([pos[q, 0, 0] for q in range(3)], axis=0))

    def place_rows(part):
        wide = jnp.concatenate([part.astype(F32), jnp.zeros((128 - 3, A), F32)], axis=0)
        return mm_nt(pick, wide.astype(BF))

    place = place_rows(own_parts[0]) + place_rows(own_parts[1]) + place_rows(own_parts[2])
    pos_tab[pl.ds(0, A), :] = place[:A]
    pos_send[...] = place[A:]

    def own_keys(layer, h):
        return exact(mm, h, wk[layer]).astype(BF)

    loads["feat"].wait()
    loads["wk"].wait()
    rows = mm(pick, own_keys(0, feat[0, 0, 0]))
    key_tab[0, pl.ds(0, A), :] = rows[:A]
    key_send[pl.ds(0, PLANE), :] = rows[A:]

    pl.semaphore_wait(barrier, len(around))
    plane(0, pos_send, 0, pos_tab, A, 1)
    plane(2, key_send, 0, key_tab.at[0], A, 1)

    loads["vs"].wait()
    lane_first = iota((1, FIRST), 1)
    label_row = lane_first
    for n in range(A // G, FIRST // G):
        label_row = label_row + jnp.where(lane_first >> 3 == n, LABELS[n] - n * G, 0)
    label_row = label_row.astype(F32)
    face_f = jnp.concatenate(
        [jnp.where(column(vs[0, 0, 0, f : f + 1, :]) == label_row, 1.0, 0.0) for f in range(2)],
        axis=0,
    )
    face = face_f.astype(BF)
    face_mine[...] = face_f
    for m, (dx, dy, _) in enumerate(MESSAGES):
        remote(4, face_mine, face_all.at[m], at(dx, dy, 0))

    mine = (iota((A, EDGES), 1) & (A - 1)) == iota((A, EDGES), 0)
    mine_f = jnp.where(mine, 1.0, 0.0)
    mine_b = mine_f.astype(BF)
    mine_s[...] = mine_f
    edge[pl.ds(ROWS, A), :] = mine_b
    edge[pl.ds(SELF, DEPTH - SELF), :] = jnp.zeros((DEPTH - SELF, EDGES), BF)
    dr_s[...] = jnp.zeros_like(dr_s)
    key_back[:, pl.ds(BACK, DEPTH - BACK), :] = jnp.zeros((LAYERS, DEPTH - BACK, C), F32)
    pos_back[pl.ds(BACK, DEPTH - BACK), :] = jnp.zeros((DEPTH - BACK, 128), F32)
    slot_pick = jnp.where((iota((S, EDGES), 1) >> 5) == iota((S, EDGES), 0), 1.0, 0.0).astype(BF)
    loads["nbr"].wait()
    nbr_all = mm(nbr[0, 0, 0].astype(F32).astype(BF), slot_pick)
    nbr_row = jnp.sum(jnp.where(mine, nbr_all, 0.0), axis=0, keepdims=True)
    loads["cnt"].wait()
    cnt_rows = jnp.broadcast_to(cnt[0, 0].astype(F32), (16, A)).astype(BF)
    cnt_row = mm(cnt_rows, mine_b)[0:1]
    live = jnp.where((iota((1, EDGES), 1) >> 5).astype(F32) < cnt_row, 1.0, 0.0)
    tile = iota((16, EDGES), 0)
    for n in range(ROWS // 16):
        low, high = LABELS[2 * n], LABELS[2 * n + 1]
        label = jnp.where(tile < G, tile + low, tile + (high - G)).astype(F32)
        edge[pl.ds(16 * n, 16), :] = jnp.where(nbr_row == label, 1.0, 0.0).astype(BF)

    arrived(0, pos_tab, A, PLANE)
    first = pos_tab[pl.ds(0, FIRST), :]
    rows = sum(mm(face, part) for part in split3(first))
    span = BOX_SIDE * nz
    low_shift = jnp.where(iz == 0, span, 0.0).astype(F32)
    high_shift = jnp.where(iz == nz - 1, -span, 0.0).astype(F32)
    shift = jnp.where(iota((2 * G, 128), 0) < G, low_shift, high_shift)
    pos_face[...] = rows + jnp.where(iota((2 * G, 128), 1) == 2, shift, 0.0)
    zone(1, pos_face, 0, pos_tab, FIRST)

    arrived(2, key_tab.at[0], A, PLANE)
    face_send[...] = mm(face, key_tab[0, pl.ds(0, FIRST), :].astype(BF))
    zone(3, face_send, 0, key_tab.at[0], FIRST)

    arrived(4, face_all, 0, len(MESSAGES))
    lane = iota((2 * G, FIRST), 1)
    parts, starts = [], [A]
    for _, _, quads in MESSAGES:
        starts.append(starts[-1] + G * len(quads))
    for m, (dx, dy) in enumerate(PLACES):
        if (dx, dy) == (0, 0):
            parts.append(jnp.where(lane < A, face_f, 0.0))
        else:
            to = PLACES.index((-dx, -dy))
            within = (lane >= starts[to]) & (lane < starts[to + 1])
            parts.append(jnp.where(within, face_all[m], 0.0))
    given = mm(jnp.concatenate(parts, axis=0).astype(BF), pick)
    pick_all[pl.ds(FIRST, ZONE), :] = given.astype(BF)
    pick_back[...] = jnp.concatenate(
        [pick_f[A:], given, jnp.zeros((DEPTH - BACK, A), F32)], axis=0
    ).T.astype(BF)

    loads["wq"].wait()
    query_s[0] = exact(mm, feat[0, 0, 0], wq[0])
    loads["wr"].wait()

    arrived(1, pos_tab, FIRST, 2 * G)
    place = jnp.concatenate(
        [pos_tab[...], -pos_tab[pl.ds(0, A), :], jnp.zeros((DEPTH - SELF, 128), F32)], axis=0
    )
    place_t = place.T[0:G, :]
    parts = [part.astype(F32) for part in split3(place_t)] + [jnp.zeros((G, DEPTH), F32)]
    offset = mm(jnp.concatenate(parts, axis=0).astype(BF), edge[...])
    offset = offset[0:G] + (offset[G : 2 * G] + offset[2 * G : 3 * G])
    dist = jnp.sqrt(jnp.sum(offset * offset, axis=0, keepdims=True) + SOFTEN)
    inv = 1.0 / dist
    scaled = dist * (1.0 / CUTOFF)
    gap = 1.0 - scaled * scaled
    inside = jnp.where(scaled < 1.0, live, 0.0)
    envelope = inside * gap * gap
    unit = offset * inv
    order = (iota((NB, EDGES), 0) + 1).astype(F32)
    turn = order * scaled
    whole = jnp.floor(turn + 0.5)
    angle = (turn - whole) * math.pi
    sign = 1.0 - 2.0 * (whole - 2.0 * jnp.floor(0.5 * whole))
    sq = angle * angle
    sine, cosine = jnp.zeros_like(sq), jnp.zeros_like(sq)
    for n in range(6, -1, -1):
        sine = sine * sq + (-1.0) ** n / math.factorial(2 * n + 1)
        cosine = cosine * sq + (-1.0) ** n / math.factorial(2 * n)
    inv_scaled = CUTOFF * inv
    basis = sign * sine * angle * inv_scaled
    dbasis_s[...] = (order * math.pi * sign * cosine - basis) * inv_scaled
    unit_s[...] = unit
    geo[...] = jnp.concatenate(
        [envelope, inv, -4.0 * inside * gap * scaled, jnp.zeros((5, EDGES), F32)], axis=0
    )
    basis_h, basis_l = split(basis)
    basis_h, basis_l = basis_h.astype(F32), basis_l.astype(F32)
    edge[pl.ds(SELF, 32), :] = jnp.concatenate(
        [basis_h, basis_l, basis_h, jnp.zeros_like(basis)], axis=0
    ).astype(BF)
    for q in range(4):
        row = envelope if q == 0 else envelope * unit[q - 1 : q]
        w_h, w_l = split(row * mine_s[...])
        weight[pl.ds(A * q, A), :] = w_h
        weight[pl.ds(4 * A + A * q, A), :] = w_l

    def forward(layer, h):
        radial_h, radial_l = split(wr[layer])
        radial_h, radial_l = radial_h.astype(F32), radial_l.astype(F32)
        rows = jnp.concatenate(
            [
                key_tab[layer],
                query_s[layer],
                radial_h,
                radial_h,
                radial_l,
                jnp.zeros((DEPTH - SELF - 3 * NB, C), F32),
            ],
            axis=0,
        )
        mt[...] = (0.5 * rows).T.astype(BF)
        for n in range(CHUNKS):
            part = pl.ds(n * STEP, STEP)
            half = mm(mt[...], edge[:, part])
            turned = jnp.tanh(half)
            more = 1.0 + turned
            act[layer, :, part] = (half * more).astype(BF)
            slope[layer, :, part] = more * (1.0 + half * (1.0 - turned))
        total = mm_nt(weight[...], act[layer])
        total = total[: 4 * A] + total[4 * A :]
        gather_h, gather_l = split(total[:A])
        vec_h, vec_l = split(total[A:])
        vec_s[layer] = FACTOR * (mm_nt(vec_h, wv[layer]) + mm_nt(vec_l, wv[layer]))
        return h + FACTOR * (mm(gather_h, wm[layer]) + mm(gather_l, wm[layer]))

    loads["wm"].wait()
    loads["wv"].wait()
    arrived(3, key_tab.at[0], FIRST, 2 * G)
    h1 = forward(0, feat[0, 0, 0])
    h1_s[...] = h1
    sent(2, key_send, 0, PLANE)
    rows = mm(pick_all[...], own_keys(1, h1))
    key_tab[1, pl.ds(0, A), :] = rows[:A]
    key_send[...] = rows[A:]
    zone_out(6, key_send, PLANE, zone_in)
    plane(5, key_send, 0, key_tab.at[1], A, 1)
    query_s[1] = exact(mm, h1_s[...], wq[1])
    loads["wh"].wait()
    loads["we"].wait()
    arrived(5, key_tab.at[1], A, PLANE)
    arrived(6, zone_in, 0, ZONE)
    zone_rows = zone_in[pl.ds(0, 2 * G), :]
    for m in range(1, len(PLACES)):
        zone_rows = zone_rows + zone_in[pl.ds(2 * G * m, 2 * G), :]
    key_tab[1, pl.ds(FIRST, 2 * G), :] = zone_rows
    h2 = forward(1, h1_s[...])
    h2_s[...] = h2

    lat = exact(mm, h2_s[...], wh[...])
    gate = 0.5 * jnp.tanh(0.5 * lat) + 0.5
    hidden = lat * gate
    readout = we[...]
    square = vec_s[0] * vec_s[0] + vec_s[1] * vec_s[1]
    square = square[:A] + (square[A : 2 * A] + square[2 * A :])
    energy = jnp.sum(hidden * readout, axis=1, keepdims=True) + jnp.sum(
        square, axis=1, keepdims=True
    ) * (1.0 / CT)
    en_out[0, 0] = jnp.sum(
        jnp.where(iota((A, A), 0) == iota((A, A), 1), energy, 0.0), axis=0, keepdims=True
    )
    dh_s[...] = exact(mm_nt, readout * (gate + hidden * (1.0 - gate)), wh[...])

    def backward(layer):
        dh_h, dh_l = split(dh_s[...])
        g0 = FACTOR * (mm_nt(dh_h, wm[layer]) + mm_nt(dh_l, wm[layer]))
        dv_h, dv_l = split(vec_s[layer] * (2.0 / CT))
        gx = FACTOR * (mm(dv_h, wv[layer]) + mm(dv_l, wv[layer]))
        pull = jnp.concatenate([g0, gx], axis=0)
        pull_b = pull.astype(BF)
        mp[...] = jnp.concatenate([0.5 * pull, 0.5 * pull], axis=0).T.astype(BF)
        radial_h, radial_l = split(wr[layer])
        radial = jnp.concatenate([radial_h.astype(F32), radial_l.astype(F32)], axis=0).astype(BF)
        for n in range(CHUNKS):
            part = pl.ds(n * STEP, STEP)
            dl = (mm(mp[...], weight[:, part]) * slope[layer, :, part]).astype(BF)
            dlat[:, part] = dl
            cross = mm(pull_b, act[layer, :, part])
            rows = [
                jnp.sum(cross[A * q : A * q + A] * mine_s[:, :STEP], axis=0, keepdims=True)
                for q in range(4)
            ]
            rows = jnp.concatenate(rows + [jnp.zeros((4, STEP), F32)], axis=0)
            got = mm(radial, dl)
            got = got[:NB] + got[NB:]
            if layer == LAYERS - 1:
                dw[:, part] = rows
                db[:, part] = got
            else:
                dw[:, part] += rows
                db[:, part] += got
        drows = mm_nt(edge[pl.ds(0, SELF), :], dlat[...])
        dkey[layer] = drows[:ROWS]
        give_back(7 + layer, dkey.at[layer], key_back.at[layer])
        dq_s[...] = dh_s[...] + exact(mm_nt, drows[ROWS:], wq[layer])

    def collect(own, back):
        back_h, back_l = split(back)
        return own + (mm(pick_back[...], back_h) + mm(pick_back[...], back_l))

    def finish(layer):
        arrived(7 + layer, key_back.at[layer], 0, BACK)
        own = collect(dkey[layer, pl.ds(0, A), :], key_back[layer])
        return dq_s[...] + exact(mm_nt, own, wk[layer])

    backward(1)
    dh_s[...] = finish(1)
    backward(0)

    envelope, inv, bend = geo[0:1], geo[1:2], geo[2:3]
    unit = unit_s[...]
    lanes = iota((G, EDGES), 0)
    du = jnp.zeros((G, EDGES), F32)
    for q in range(3):
        du = jnp.where(lanes == q, dw[q + 1 : q + 2], du)
    along = jnp.sum(du * unit, axis=0, keepdims=True)
    dscaled = bend * (dw[0:1] + along) + jnp.sum(db[...] * dbasis_s[...], axis=0, keepdims=True)
    ddist = dscaled * (1.0 / CUTOFF) - inv * envelope * along
    dr_h, dr_l = split(du * (envelope * inv) + unit * ddist)
    dr_s[pl.ds(0, 16), :] = jnp.concatenate([dr_h.astype(F32), dr_l.astype(F32)], axis=0).astype(BF)
    rows = mm_nt(edge[pl.ds(0, SELF), :], dr_s[...])
    pos_grad[...] = rows[:ROWS]
    give_back(9, pos_grad, pos_back)
    own_s[...] = rows[:A] - rows[ROWS:]

    grad_out[0, 0, 0] = finish(0)
    arrived(9, pos_back, 0, BACK)
    pos_own = collect(own_s[...], pos_back[...])
    pos_own = jnp.concatenate([pos_own, jnp.zeros((128 - A, 128), F32)], axis=0).T
    pos_own = -(pos_own[0:G, :A] + pos_own[G : 2 * G, :A])
    for q in range(3):
        force_out[q, 0, 0] = pos_own[q : q + 1]

    sent(0, pos_send, 0, PLANE)
    sent(1, pos_face, 0, 2 * G)
    sent(3, face_send, 0, 2 * G)
    sent(4, face_all, 0, len(MESSAGES))
    sent(5, key_send, 0, PLANE)
    sent(6, key_send, PLANE, ZONE)
    for layer in range(LAYERS):
        sent(7 + layer, key_back.at[layer], 0, BACK)
    sent(9, pos_back, 0, BACK)


def per_device(*args):
    hbm = pl.BlockSpec(memory_space=pltpu.HBM)
    vmem = pl.BlockSpec(memory_space=pltpu.VMEM)
    args = list(args)
    args[10] = args[10].swapaxes(1, 2)
    args[12] = args[12].reshape(1, C)
    f32, bf = (lambda *shape: pltpu.VMEM(shape, F32)), (lambda *shape: pltpu.VMEM(shape, BF))
    return pl.pallas_call(
        kernel,
        out_shape=(
            jax.ShapeDtypeStruct((1, 1, 1, A), F32),
            jax.ShapeDtypeStruct((3, 1, 1, 1, A), F32),
            jax.ShapeDtypeStruct((1, 1, 1, A, C), F32),
        ),
        in_specs=[hbm] * len(args),
        out_specs=(vmem,) * 3,
        scratch_shapes=[pltpu.VMEM(a.shape, a.dtype) for a in args]
        + [
            f32(2 * G, 128), f32(len(MESSAGES), 2 * G, 128), f32(ROWS, 128), f32(PLANE, 128),
            f32(2 * G, 128), f32(ROWS, 128), f32(DEPTH, 128),
            f32(LAYERS, ROWS, C), f32(BACK, C), f32(2 * G, C), f32(ZONE, C),
            f32(LAYERS, ROWS, C), f32(LAYERS, DEPTH, C),
            bf(FIRST + ZONE, A), bf(A, DEPTH), f32(A, EDGES), f32(8, EDGES), f32(G, EDGES),
            f32(NB, EDGES), bf(DEPTH, EDGES), bf(8 * A, EDGES), bf(LAYERS, C, EDGES),
            f32(LAYERS, C, EDGES), bf(C, EDGES),
            bf(C, C), bf(C, C), f32(8, EDGES), f32(NB, EDGES), bf(128, EDGES),
            f32(A, C), f32(A, C), f32(A, C), f32(A, C), f32(A, 128), f32(LAYERS, A, C),
            f32(LAYERS, 3 * A, CT),
            pltpu.SemaphoreType.DMA((13,)),
            pltpu.SemaphoreType.DMA((10,)),
            pltpu.SemaphoreType.DMA((10,)),
        ],
        compiler_params=pltpu.CompilerParams(
            collective_id=0, has_side_effects=True, vmem_limit_bytes=60 * 1024 * 1024
        ),
        cost_estimate=pl.CostEstimate(
            flops=2_500_000_000, bytes_accessed=2_000_000, transcendentals=800_000
        ),
    )(*args)


def solution(mesh):
    return jax.shard_map(
        per_device,
        mesh=mesh,
        in_specs=(
            P(None, "gx", "gy", "gz", None),
            P("gx", "gy", "gz", None, None),
            P("gx", "gy", "gz", None, None, None),
            P("gx", "gy", "gz", None, None),
            P("gx", "gy", "gz", None, None),
            P("gx", "gy", "gz", None),
            P(),
            P(),
            P(),
            P(),
            P(),
            P(),
            P(),
        ),
        out_specs=(
            P("gx", "gy", "gz", None),
            P(None, "gx", "gy", "gz", None),
            P("gx", "gy", "gz", None, None),
        ),
        check_vma=False,
    )
```

```python
import math

import jax
import jax.numpy as jnp
from jax import lax
from jax.experimental import pallas as pl
from jax.experimental.pallas import tpu as pltpu
from jax.sharding import PartitionSpec as P

A, S, C, CT, NB, G = 32, 48, 256, 64, 8, 8
LAYERS = 2
EDGES = A * S
STEP = 256
CHUNKS = EDGES // STEP
CUTOFF, SOFTEN, BOX_SIDE = 6.0, 0.25, 4.0
FACTOR = 1.0 / math.sqrt(S)
F32, BF = jnp.float32, jnp.bfloat16

MESSAGES = (
    (1, 0, ((1, 0), (1, 1))),
    (-1, 0, ((0, 0), (0, 1))),
    (0, 1, ((0, 1), (1, 1))),
    (0, -1, ((0, 0), (1, 0))),
    (1, 1, ((1, 1),)),
    (1, -1, ((1, 0),)),
    (-1, 1, ((0, 1),)),
    (-1, -1, ((0, 0),)),
)
BLOCKS = tuple((dx, dy, a, b) for dx, dy, quads in MESSAGES for a, b in quads)
PLANE = G * len(BLOCKS)
FIRST = A + PLANE
ROWS = FIRST + 2 * G
LABELS = tuple(range(0, A, G)) + tuple(
    A + ((1 - 2 * dx + a) * 4 + 1 - 2 * dy + b) * G for dx, dy, a, b in BLOCKS
) + (A + 16 * G, A + 19 * G)
SELF = ROWS + A
DEPTH = 256
PLACES = tuple((dx, dy) for dx, dy, _ in MESSAGES) + ((0, 0),)
ZONE = 2 * G * len(PLACES)
BACK = PLANE + ZONE


def mm(a, b):
    return lax.dot_general(a, b, (((1,), (0,)), ((), ())), preferred_element_type=F32)


def mm_nt(a, b):
    return lax.dot_general(a, b, (((1,), (1,)), ((), ())), preferred_element_type=F32)


def split(x):
    hi = x.astype(BF)
    return hi, (x - hi.astype(F32)).astype(BF)


def split3(x):
    hi, rest = x.astype(BF), x - x.astype(BF).astype(F32)
    mid = rest.astype(BF)
    return hi, mid, (rest - mid.astype(F32)).astype(BF)


def exact(product, a, b):
    ah, al = split(a)
    bh, bl = split(b)
    return product(ah, bh) + (product(ah, bl) + product(al, bh))


def iota(shape, dim):
    return lax.broadcasted_iota(jnp.int32, shape, dim)


def kernel(
    pos_in, feat_in, ps_in, vs_in, nbr_in, cnt_in, wq_in, wk_in, wr_in, wm_in, wv_in, wh_in, we_in,
    en_out, force_out, grad_out,
    pos, feat, ps, vs, nbr, cnt, wq, wk, wr, wm, wv, wh, we,
    face_mine, face_all, pos_tab, pos_send, pos_face,
    key_tab, key_send, face_send, zone_in, dkey_0, dkey_1, back_0, back_1,
    pick_all, pick_back, mine_s, geo, unit_s, dbasis_s, edge, weight, act, slope, dlat,
    mt, mp, dw, db, base_s, base_t, dh_s, own_s, query_s, head_s, hidden_s,
    pos_own_s, rest_s, gather_s, pull_s, joint, vec_s,
    load_sem, send_sem, recv_sem,
):
    ix, iy, iz = (lax.axis_index(n) for n in ("gx", "gy", "gz"))
    nx, ny, nz = (lax.axis_size(n) for n in ("gx", "gy", "gz"))

    def at(dx, dy, dz):
        return {
            "gx": lax.rem(ix + (dx + nx), nx),
            "gy": lax.rem(iy + (dy + ny), ny),
            "gz": lax.rem(iz + (dz + nz), nz),
        }

    loads = {}
    for n, (name, src, dst) in enumerate(
        (
            ("ps", ps_in, ps),
            ("pos", pos_in, pos),
            ("feat", feat_in, feat),
            ("wk", wk_in, wk),
            ("vs", vs_in, vs),
            ("nbr", nbr_in, nbr),
            ("cnt", cnt_in, cnt),
            ("wr", wr_in, wr),
            ("wq", wq_in, wq),
            ("wm", wm_in, wm),
            ("wv", wv_in, wv),
            ("wh", wh_in, wh),
            ("we", we_in, we),
        )
    ):
        loads[name] = pltpu.make_async_copy(src, dst, load_sem.at[n])
        loads[name].start()

    barrier = pltpu.get_barrier_semaphore()
    around = [(dx, dy, 0) for dx, dy, _ in MESSAGES] + [(0, 0, -1), (0, 0, 1)]
    for step in around:
        pl.semaphore_signal(barrier, inc=1, device_id=at(*step), device_id_type=pl.DeviceIdType.MESH)

    def remote(stage, src, dst, where):
        pltpu.make_async_remote_copy(
            src_ref=src,
            dst_ref=dst,
            send_sem=send_sem.at[stage],
            recv_sem=recv_sem.at[stage],
            device_id=where,
            device_id_type=pl.DeviceIdType.MESH,
        ).start()

    def plane(stage, src, src_at, dst, dst_at, sign):
        row = 0
        for dx, dy, quads in MESSAGES:
            rows = G * len(quads)
            remote(
                stage,
                src.at[pl.ds(src_at + row, rows)],
                dst.at[pl.ds(dst_at + row, rows)],
                at(sign * dx, sign * dy, 0),
            )
            row += rows

    def zone(stage, src, src_at, dst, dst_at):
        remote(stage, src.at[pl.ds(src_at, G)], dst.at[pl.ds(dst_at + G, G)], at(0, 0, -1))
        remote(stage, src.at[pl.ds(src_at + G, G)], dst.at[pl.ds(dst_at, G)], at(0, 0, 1))

    def zone_out(stage, src, src_at, dst):
        for m, (dx, dy) in enumerate(PLACES):
            for f, dz in ((0, -1), (1, 1)):
                remote(
                    stage,
                    src.at[pl.ds(src_at + (2 * m + f) * G, G)],
                    dst.at[pl.ds((2 * m + 1 - f) * G, G)],
                    at(-dx, -dy, dz),
                )

    def give_back(stage, src, dst):
        for m, (dx, dy) in enumerate(PLACES):
            for b, dz in ((0, -1), (1, 1)):
                remote(
                    stage,
                    src.at[pl.ds(FIRST + b * G, G)],
                    dst.at[pl.ds(PLANE + (2 * m + 1 - b) * G, G)],
                    at(dx, dy, dz),
                )
        plane(stage, src, A, dst, 0, -1)

    def arrived(stage, buf, row, rows):
        part = buf.at[pl.ds(row, rows)]

        @pl.when(ix >= 0)
        def _():
            pltpu.make_async_copy(part, part, recv_sem.at[stage]).wait()

    def sent(stage, buf, row, rows):
        part = buf.at[pl.ds(row, rows)]
        pltpu.make_async_copy(part, part, send_sem.at[stage]).wait()

    sub8, lane8 = iota((G, G), 0), iota((G, G), 1)

    def column(row):
        return jnp.sum(jnp.where(sub8 == lane8, row.astype(F32), 0.0), axis=1, keepdims=True)

    loads["ps"].wait()
    lane32 = iota((G, A), 1).astype(F32)
    quads = {
        (a, b): jnp.where(column(ps[0, 0, 0, a, b : b + 1, :]) == lane32, 1.0, 0.0)
        for a in range(2)
        for b in range(2)
    }
    eye = jnp.where(iota((A, A), 0) == iota((A, A), 1), 1.0, 0.0)
    pick_f = jnp.concatenate([eye] + [quads[a, b] for _, _, a, b in BLOCKS], axis=0)
    pick = pick_f.astype(BF)
    pick_all[pl.ds(0, FIRST), :] = pick

    loads["pos"].wait()
    own_parts = split3(jnp.concatenate([pos[q, 0, 0] for q in range(3)], axis=0))

    def place_rows(part):
        wide = jnp.concatenate([part.astype(F32), jnp.zeros((128 - 3, A), F32)], axis=0)
        return mm_nt(pick, wide.astype(BF))

    place = place_rows(own_parts[0]) + place_rows(own_parts[1]) + place_rows(own_parts[2])
    pos_tab[pl.ds(0, A), :] = place[:A]
    pos_send[...] = place[A:]

    def own_keys(layer, h):
        return exact(mm, h, wk[layer]).astype(BF)

    loads["feat"].wait()
    loads["wk"].wait()
    rows = mm(pick, own_keys(0, feat[0, 0, 0]))
    key_tab[0, pl.ds(0, A), :] = rows[:A]
    key_send[pl.ds(0, PLANE), :] = rows[A:]

    pl.semaphore_wait(barrier, len(around))
    plane(0, pos_send, 0, pos_tab, A, 1)
    plane(2, key_send, 0, key_tab.at[0], A, 1)

    loads["vs"].wait()
    lane_first = iota((1, FIRST), 1)
    label_row = lane_first
    for n in range(A // G, FIRST // G):
        label_row = label_row + jnp.where(lane_first >> 3 == n, LABELS[n] - n * G, 0)
    label_row = label_row.astype(F32)
    face_f = jnp.concatenate(
        [jnp.where(column(vs[0, 0, 0, f : f + 1, :]) == label_row, 1.0, 0.0) for f in range(2)],
        axis=0,
    )
    face = face_f.astype(BF)
    face_mine[...] = face_f
    for m, (dx, dy, _) in enumerate(MESSAGES):
        remote(4, face_mine, face_all.at[m], at(dx, dy, 0))

    mine = (iota((A, EDGES), 1) & (A - 1)) == iota((A, EDGES), 0)
    mine_f = jnp.where(mine, 1.0, 0.0)
    mine_b = mine_f.astype(BF)
    mine_s[...] = mine_f
    edge[pl.ds(ROWS, A), :] = mine_b
    edge[pl.ds(SELF, DEPTH - SELF), :] = jnp.zeros((DEPTH - SELF, EDGES), BF)
    dlat[pl.ds(C, 128), :] = jnp.zeros((128, EDGES), BF)
    for back in (back_0, back_1):
        back[pl.ds(BACK, DEPTH - BACK), :] = jnp.zeros((DEPTH - BACK, back.shape[1]), F32)
    slot_pick = jnp.where((iota((S, EDGES), 1) >> 5) == iota((S, EDGES), 0), 1.0, 0.0).astype(BF)
    loads["nbr"].wait()
    nbr_all = mm(nbr[0, 0, 0].astype(F32).astype(BF), slot_pick)
    nbr_row = jnp.sum(jnp.where(mine, nbr_all, 0.0), axis=0, keepdims=True)
    loads["cnt"].wait()
    cnt_rows = jnp.broadcast_to(cnt[0, 0].astype(F32), (16, A)).astype(BF)
    cnt_row = mm(cnt_rows, mine_b)[0:1]
    live = jnp.where((iota((1, EDGES), 1) >> 5).astype(F32) < cnt_row, 1.0, 0.0)
    def rest(layer, queries):
        radial_h, radial_l = split(wr[layer])
        radial_h, radial_l = radial_h.astype(F32), radial_l.astype(F32)
        zeros = jnp.zeros((DEPTH - SELF - 3 * NB, C), F32)
        rest_s[layer] = jnp.concatenate([queries, radial_h, radial_h, radial_l, zeros], axis=0)

    loads["wq"].wait()
    loads["wr"].wait()
    loads["wm"].wait()
    loads["wv"].wait()
    loads["wh"].wait()
    loads["we"].wait()
    h0 = feat[0, 0, 0]
    rest(0, exact(mm, h0, wq[0]))
    base_s[...] = exact(mm, h0, wk[1])
    for n, (mixing, after) in enumerate(((wm[0], wk[1]), (wm[1], wh[...]))):
        after_h, after_l = split(after)
        joint_h, joint_l = split(FACTOR * (mm(mixing, after_h) + mm(mixing, after_l)))
        joint[2 * n] = joint_h
        joint[2 * n + 1] = joint_l
    arrived(0, pos_tab, A, PLANE)
    first = pos_tab[pl.ds(0, FIRST), :]
    rows = sum(mm(face, part) for part in split3(first))
    span = BOX_SIDE * nz
    low_shift = jnp.where(iz == 0, span, 0.0).astype(F32)
    high_shift = jnp.where(iz == nz - 1, -span, 0.0).astype(F32)
    shift = jnp.where(iota((2 * G, 128), 0) < G, low_shift, high_shift)
    pos_face[...] = rows + jnp.where(iota((2 * G, 128), 1) == 2, shift, 0.0)
    zone(1, pos_face, 0, pos_tab, FIRST)

    arrived(2, key_tab.at[0], A, PLANE)
    face_send[...] = mm(face, key_tab[0, pl.ds(0, FIRST), :].astype(BF))
    zone(3, face_send, 0, key_tab.at[0], FIRST)

    tile = iota((16, EDGES), 0)
    for n in range(ROWS // 16):
        low, high = LABELS[2 * n], LABELS[2 * n + 1]
        label = jnp.where(tile < G, tile + low, tile + (high - G)).astype(F32)
        edge[pl.ds(16 * n, 16), :] = jnp.where(nbr_row == label, 1.0, 0.0).astype(BF)

    arrived(4, face_all, 0, len(MESSAGES))
    lane = iota((2 * G, FIRST), 1)
    parts, starts = [], [A]
    for _, _, quads in MESSAGES:
        starts.append(starts[-1] + G * len(quads))
    for m, (dx, dy) in enumerate(PLACES):
        if (dx, dy) == (0, 0):
            parts.append(jnp.where(lane < A, face_f, 0.0))
        else:
            to = PLACES.index((-dx, -dy))
            within = (lane >= starts[to]) & (lane < starts[to + 1])
            parts.append(jnp.where(within, face_all[m], 0.0))
    given = mm(jnp.concatenate(parts, axis=0).astype(BF), pick)
    pick_all[pl.ds(FIRST, ZONE), :] = given.astype(BF)
    pick_back[...] = jnp.concatenate(
        [pick_f[A:], given, jnp.zeros((DEPTH - BACK, A), F32)], axis=0
    ).T.astype(BF)

    arrived(1, pos_tab, FIRST, 2 * G)
    place = jnp.concatenate(
        [pos_tab[...], -pos_tab[pl.ds(0, A), :], jnp.zeros((DEPTH - SELF, 128), F32)], axis=0
    )
    place_t = place.T[0:G, :]
    parts = [part.astype(F32) for part in split3(place_t)] + [jnp.zeros((G, DEPTH), F32)]
    offset = mm(jnp.concatenate(parts, axis=0).astype(BF), edge[...])
    offset = offset[0:G] + (offset[G : 2 * G] + offset[2 * G : 3 * G])
    dist = jnp.sqrt(jnp.sum(offset * offset, axis=0, keepdims=True) + SOFTEN)
    inv = 1.0 / dist
    scaled = dist * (1.0 / CUTOFF)
    gap = 1.0 - scaled * scaled
    inside = jnp.where(scaled < 1.0, live, 0.0)
    envelope = inside * gap * gap
    unit = offset * inv
    order = (iota((NB, EDGES), 0) + 1).astype(F32)
    turn = order * scaled
    whole = jnp.floor(turn + 0.5)
    angle = (turn - whole) * math.pi
    sign = 1.0 - 2.0 * (whole - 2.0 * jnp.floor(0.5 * whole))
    sq = angle * angle
    sine, cosine = jnp.zeros_like(sq), jnp.zeros_like(sq)
    for n in range(6, -1, -1):
        sine = sine * sq + (-1.0) ** n / math.factorial(2 * n + 1)
        cosine = cosine * sq + (-1.0) ** n / math.factorial(2 * n)
    inv_scaled = CUTOFF * inv
    basis = sign * sine * angle * inv_scaled
    dbasis_s[...] = (order * math.pi * sign * cosine - basis) * inv_scaled
    unit_s[...] = unit
    geo[...] = jnp.concatenate(
        [envelope, inv, -4.0 * inside * gap * scaled, jnp.zeros((5, EDGES), F32)], axis=0
    )
    basis_h, basis_l = split(basis)
    basis_h, basis_l = basis_h.astype(F32), basis_l.astype(F32)
    edge[pl.ds(SELF, 32), :] = jnp.concatenate(
        [basis_h, basis_l, basis_h, jnp.zeros_like(basis)], axis=0
    ).astype(BF)
    for q in range(4):
        row = envelope if q == 0 else envelope * unit[q - 1 : q]
        w_h, w_l = split(row * mine_s[...])
        weight[pl.ds(A * q, A), :] = w_h
        weight[pl.ds(4 * A + A * q, A), :] = w_l

    def near_keys(layer):
        mt[:, pl.ds(0, FIRST)] = (0.5 * key_tab[layer, pl.ds(0, FIRST), :]).T.astype(BF)

    def forward(layer, zone_rows):
        rows = jnp.concatenate([zone_rows, rest_s[layer]], axis=0)
        mt[:, pl.ds(FIRST, DEPTH - FIRST)] = (0.5 * rows).T.astype(BF)
        for n in range(CHUNKS):
            part = pl.ds(n * STEP, STEP)
            half = mm(mt[...], edge[:, part])
            turned = jnp.tanh(half)
            more = 1.0 + turned
            active = (half * more).astype(BF)
            act[layer, :, part] = active
            slope[layer, :, part] = more * (1.0 + half * (1.0 - turned))
        total = mm_nt(weight[...], act[layer])
        total = total[: 4 * A] + total[4 * A :]
        gather_s[...] = total
        return total

    def vectors(layer):
        vec_h, vec_l = split(gather_s[pl.ds(A, 3 * A), :])
        vector = FACTOR * (mm_nt(vec_h, wv[layer]) + mm_nt(vec_l, wv[layer]))
        vec_s[layer] = vector
        dv_h, dv_l = split(vector * (2.0 / CT))
        gx = FACTOR * (mm(dv_h, wv[layer]) + mm(dv_l, wv[layer]))
        pull_s[layer, pl.ds(A, 3 * A), :] = gx.astype(BF)
        flipped = jnp.concatenate([jnp.zeros((A, C), F32), 0.5 * gx], axis=0).T.astype(BF)
        mp[layer, :, pl.ds(0, 4 * A)] = flipped
        mp[layer, :, pl.ds(4 * A, 4 * A)] = flipped

    def thrice(product, a, b_h, b_l):
        a_h, a_l = split(a)
        return product(a_h, b_h) + (product(a_h, b_l) + product(a_l, b_h))

    near_keys(0)

    arrived(3, key_tab.at[0], FIRST, 2 * G)
    total = forward(0, key_tab[0, pl.ds(FIRST, 2 * G), :])
    keys = base_s[...] + thrice(mm, total[:A], joint[0], joint[1])
    rows = mm(pick_all[...], keys.astype(BF))
    key_tab[1, pl.ds(0, A), :] = rows[:A]
    sent(2, key_send, 0, PLANE)
    key_send[...] = rows[A:]
    zone_out(6, key_send, PLANE, zone_in)
    plane(5, key_send, 0, key_tab.at[1], A, 1)

    gather_h, gather_l = split(gather_s[pl.ds(0, A), :])
    h1 = feat[0, 0, 0] + FACTOR * (mm(gather_h, wm[0]) + mm(gather_l, wm[0]))
    rest(1, exact(mm, h1, wq[1]))
    base_s[...] = exact(mm, h1, wh[...])
    vectors(0)
    arrived(5, key_tab.at[1], A, PLANE)
    near_keys(1)
    arrived(6, zone_in, 0, ZONE)
    zone_rows = zone_in[pl.ds(0, 2 * G), :]
    for m in range(1, len(PLACES)):
        zone_rows = zone_rows + zone_in[pl.ds(2 * G * m, 2 * G), :]
    total = forward(1, zone_rows)

    lat = base_s[...] + thrice(mm, total[:A], joint[2], joint[3])
    gate = 0.5 * jnp.tanh(0.5 * lat) + 0.5
    hidden = lat * gate
    readout = we[...]
    dhead = readout * (gate + hidden * (1.0 - gate))
    head_s[...] = dhead
    hidden_s[...] = hidden * readout
    vectors(1)

    def set_pull(layer, g0, g0_t):
        pull_s[layer, pl.ds(0, A), :] = g0.astype(BF)
        half = (0.5 * g0_t).astype(BF)
        mp[layer, :, pl.ds(0, A)] = half
        mp[layer, :, pl.ds(4 * A, A)] = half

    def flip(a, b):
        return mm_nt(b, a)

    def places(part, du, dbasis):
        unit, inv = unit_s[:, part], geo[1:2, part]
        along = jnp.sum(du * unit, axis=0, keepdims=True)
        dscaled = geo[2:3, part] * (du[3:4] + along) + jnp.sum(
            dbasis * dbasis_s[:, part], axis=0, keepdims=True
        )
        spread = geo[0:1, part] * inv
        return du * spread + unit * (dscaled * (1.0 / CUTOFF) - spread * along)

    def backward(layer):
        radial_h, radial_l = split(wr[layer])
        radial = jnp.concatenate([radial_h.astype(F32), radial_l.astype(F32)], axis=0).astype(BF)
        for n in range(CHUNKS):
            part = pl.ds(n * STEP, STEP)
            dl = (mm(mp[layer], weight[:, part]) * slope[layer, :, part]).astype(BF)
            dlat[pl.ds(0, C), part] = dl
            cross = mm(pull_s[layer], act[layer, :, part])
            rows = [
                jnp.sum(cross[A * q : A * q + A] * mine_s[:, :STEP], axis=0, keepdims=True)
                for q in range(4)
            ]
            rows = jnp.concatenate(rows[1:] + rows[:1] + [jnp.zeros((4, STEP), F32)], axis=0)
            got = mm(radial, dl)
            got = got[:NB] + got[NB:]
            if layer == LAYERS - 1:
                dw[:, part] = rows
                db[:, part] = got
            else:
                dr_h, dr_l = split(places(part, dw[:, part] + rows, db[:, part] + got))
                both = jnp.concatenate([dr_h.astype(F32), dr_l.astype(F32)], axis=0)
                dlat[pl.ds(C, 2 * G), part] = both.astype(BF)
        mine, back = (dkey_0, back_0) if layer == 0 else (dkey_1, back_1)
        drows = mm_nt(edge[pl.ds(0, SELF), :], dlat[pl.ds(0, mine.shape[1]), :])
        mine[...] = drows[:ROWS]
        give_back(7 + layer, mine, back)
        query_s[...] = drows[ROWS:, :C]
        if layer == 0:
            pos_own_s[...] = drows[ROWS:, C:]

    def collect(own, back):
        back_h, back_l = split(back)
        return own + (mm(pick_back[...], back_h) + mm(pick_back[...], back_l))

    def returned(layer):
        mine, back = (dkey_0, back_0) if layer == 0 else (dkey_1, back_1)
        arrived(7 + layer, back, 0, BACK)
        return collect(mine[pl.ds(0, A), :], back[...])

    set_pull(1, thrice(mm_nt, dhead, joint[2], joint[3]), thrice(flip, dhead, joint[2], joint[3]))
    backward(1)

    square = vec_s[0] * vec_s[0] + vec_s[1] * vec_s[1]
    square = square[:A] + (square[A : 2 * A] + square[2 * A :])
    energy = jnp.sum(hidden_s[...], axis=1, keepdims=True) + jnp.sum(
        square, axis=1, keepdims=True
    ) * (1.0 / CT)
    en_out[0, 0] = jnp.sum(
        jnp.where(iota((A, A), 0) == iota((A, A), 1), energy, 0.0), axis=0, keepdims=True
    )
    dh = exact(mm_nt, head_s[...], wh[...]) + exact(mm_nt, query_s[...], wq[1])
    dh_s[...] = dh
    dh_h, dh_l = split(FACTOR * dh)
    base_s[...] = mm_nt(dh_h, wm[0]) + mm_nt(dh_l, wm[0])
    base_t[...] = mm_nt(wm[0], dh_h) + mm_nt(wm[0], dh_l)

    own = returned(1)
    set_pull(
        0,
        base_s[...] + thrice(mm_nt, own, joint[0], joint[1]),
        base_t[...] + thrice(flip, own, joint[0], joint[1]),
    )
    own_s[...] = own
    backward(0)

    dh = dh_s[...] + exact(mm_nt, own_s[...], wk[1])
    dh_s[...] = dh + exact(mm_nt, query_s[...], wq[0])
    own = returned(0)
    grad_out[0, 0, 0] = dh_s[...] + exact(mm_nt, own[:, :C], wk[0])
    pos_own = own[:, C:] - pos_own_s[...]
    pos_own = jnp.concatenate([pos_own, jnp.zeros((128 - A, 128), F32)], axis=0).T
    pos_own = -(pos_own[0:G, :A] + pos_own[G : 2 * G, :A])
    for q in range(3):
        force_out[q, 0, 0] = pos_own[q : q + 1]

    sent(0, pos_send, 0, PLANE)
    sent(1, pos_face, 0, 2 * G)
    sent(3, face_send, 0, 2 * G)
    sent(4, face_all, 0, len(MESSAGES))
    sent(5, key_send, 0, PLANE)
    sent(6, key_send, PLANE, ZONE)
    sent(7, back_0, 0, BACK)
    sent(8, back_1, 0, BACK)


def hand_on(en_in, force_in, grad_in, en_out, force_out, grad_out, sem):
    grad_out[...] = grad_in[...]
    force_out[...] = force_in[...]
    en_out[...] = en_in[...]


def per_device(*args):
    hbm = pl.BlockSpec(memory_space=pltpu.HBM)
    vmem = pl.BlockSpec(memory_space=pltpu.VMEM)
    args = list(args)
    args[10] = args[10].swapaxes(1, 2)
    args[12] = args[12].reshape(1, C)
    f32, bf = (lambda *shape: pltpu.VMEM(shape, F32)), (lambda *shape: pltpu.VMEM(shape, BF))
    out_shape = (
        jax.ShapeDtypeStruct((1, 1, 1, A), F32),
        jax.ShapeDtypeStruct((3, 1, 1, 1, A), F32),
        jax.ShapeDtypeStruct((1, 1, 1, A, C), F32),
    )
    results = pl.pallas_call(
        kernel,
        out_shape=out_shape,
        in_specs=[hbm] * len(args),
        out_specs=(vmem,) * 3,
        scratch_shapes=[pltpu.VMEM(a.shape, a.dtype) for a in args]
        + [
            f32(2 * G, 128), f32(len(MESSAGES), 2 * G, 128), f32(ROWS, 128), f32(PLANE, 128),
            f32(2 * G, 128),
            f32(LAYERS, ROWS, C), f32(BACK, C), f32(2 * G, C), f32(ZONE, C),
            f32(ROWS, C + 128), f32(ROWS, C), f32(DEPTH, C + 128), f32(DEPTH, C),
            bf(FIRST + ZONE, A), bf(A, DEPTH), f32(A, EDGES), f32(8, EDGES), f32(G, EDGES),
            f32(NB, EDGES), bf(DEPTH, EDGES), bf(8 * A, EDGES), bf(LAYERS, C, EDGES),
            f32(LAYERS, C, EDGES), bf(C + 128, EDGES),
            bf(C, DEPTH), bf(LAYERS, C, 8 * A), f32(8, EDGES), f32(NB, EDGES),
            f32(A, C), f32(C, A), f32(A, C), f32(A, C), f32(A, C), f32(A, C), f32(A, C),
            f32(A, 128), f32(LAYERS, DEPTH - ROWS, C), f32(4 * A, C), bf(LAYERS, 4 * A, C),
            bf(4, C, C), f32(LAYERS, 3 * A, CT),
            pltpu.SemaphoreType.DMA((13,)),
            pltpu.SemaphoreType.DMA((9,)),
            pltpu.SemaphoreType.DMA((9,)),
        ],
        compiler_params=pltpu.CompilerParams(
            collective_id=0, has_side_effects=True, vmem_limit_bytes=60 * 1024 * 1024
        ),
        cost_estimate=pl.CostEstimate(
            flops=2_500_000_000, bytes_accessed=2_000_000, transcendentals=800_000
        ),
    )(*args)
    return pl.pallas_call(
        hand_on,
        out_shape=out_shape,
        in_specs=[vmem] * 3,
        out_specs=(vmem,) * 3,
        scratch_shapes=[pltpu.SemaphoreType.DMA((3,))],
        compiler_params=pltpu.CompilerParams(vmem_limit_bytes=60 * 1024 * 1024),
    )(*results)


def solution(mesh):
    return jax.shard_map(
        per_device,
        mesh=mesh,
        in_specs=(
            P(None, "gx", "gy", "gz", None),
            P("gx", "gy", "gz", None, None),
            P("gx", "gy", "gz", None, None, None),
            P("gx", "gy", "gz", None, None),
            P("gx", "gy", "gz", None, None),
            P("gx", "gy", "gz", None),
            P(),
            P(),
            P(),
            P(),
            P(),
            P(),
            P(),
        ),
        out_specs=(
            P("gx", "gy", "gz", None),
            P(None, "gx", "gy", "gz", None),
            P("gx", "gy", "gz", None, None),
        ),
        check_vma=False,
    )
```

```python
import math

import jax
import jax.numpy as jnp
from jax import lax
from jax.experimental import pallas as pl
from jax.experimental.pallas import tpu as pltpu
from jax.sharding import PartitionSpec as P

A, S, C, CT, NB, G = 32, 48, 256, 64, 8, 8
LAYERS = 2
EDGES = A * S
STEP = 256
CHUNKS = EDGES // STEP
CUTOFF, SOFTEN, BOX_SIDE = 6.0, 0.25, 4.0
FACTOR = 1.0 / math.sqrt(S)
F32, BF = jnp.float32, jnp.bfloat16

MESSAGES = (
    (1, 0, ((1, 0), (1, 1))),
    (1, 1, ((1, 1),)),
    (1, -1, ((1, 0),)),
    (-1, 0, ((0, 0), (0, 1))),
    (-1, 1, ((0, 1),)),
    (-1, -1, ((0, 0),)),
    (0, 1, ((0, 1), (1, 1))),
    (0, -1, ((0, 0), (1, 0))),
)
SIDES = (1, -1, 0)
BLOCKS = tuple((dx, dy, a, b) for dx, dy, quads in MESSAGES for a, b in quads)
PLANE = G * len(BLOCKS)
FIRST = A + PLANE
ROWS = FIRST + 2 * G
LABELS = tuple(range(0, A, G)) + tuple(
    A + ((1 - 2 * dx + a) * 4 + 1 - 2 * dy + b) * G for dx, dy, a, b in BLOCKS
) + (A + 16 * G, A + 19 * G)
SELF = ROWS + A
DEPTH = 256
PLACES = tuple((dx, dy) for dx, dy, _ in MESSAGES) + ((0, 0),)
ZONE = 2 * G * len(PLACES)
BACK = PLANE + ZONE
PLANE_PART, ZONE_PART = PLANE // 3, ZONE // 3


def mm(a, b):
    return lax.dot_general(a, b, (((1,), (0,)), ((), ())), preferred_element_type=F32)


def mm_nt(a, b):
    return lax.dot_general(a, b, (((1,), (1,)), ((), ())), preferred_element_type=F32)


def split(x):
    hi = x.astype(BF)
    return hi, (x - hi.astype(F32)).astype(BF)


def split3(x):
    hi, rest = x.astype(BF), x - x.astype(BF).astype(F32)
    mid = rest.astype(BF)
    return hi, mid, (rest - mid.astype(F32)).astype(BF)


def exact(product, a, b):
    ah, al = split(a)
    bh, bl = split(b)
    return product(ah, bh) + (product(ah, bl) + product(al, bh))


def iota(shape, dim):
    return lax.broadcasted_iota(jnp.int32, shape, dim)


def kernel(
    pos_in, feat_in, ps_in, vs_in, nbr_in, cnt_in, wq_in, wk_in, wr_in, wm_in, wv_in, wh_in, we_in,
    en_out, force_out, grad_out,
    pos, feat, ps, vs, nbr, cnt, wq, wk, wr, wm, wv, wh, we,
    face_mine, face_all, pos_tab, pos_send, pos_face,
    key_tab, key_send, face_send, zone_in, dkey_0, dkey_1, back_0, back_1,
    pick_all, pick_back, mine_s, geo, unit_s, dbasis_s, edge, weight, act, slope, dlat,
    mt, mp, dw, db, base_s, base_t, dh_s, own_s, query_s, head_s, hidden_s,
    pos_own_s, rest_s, gather_s, pull_s, joint, vec_s,
    load_sem, send_sem, recv_sem,
):
    ix, iy, iz = (lax.axis_index(n) for n in ("gx", "gy", "gz"))
    nx, ny, nz = (lax.axis_size(n) for n in ("gx", "gy", "gz"))

    def at(dx, dy, dz):
        return {
            "gx": lax.rem(ix + (dx + nx), nx),
            "gy": lax.rem(iy + (dy + ny), ny),
            "gz": lax.rem(iz + (dz + nz), nz),
        }

    def beside(side, action):
        if side == 0:
            pl.when(ix >= 0)(action)
        elif side == 1:
            pl.when(ix < nx - 1)(action)
        else:
            pl.when(ix > 0)(action)

    barrier = pltpu.get_barrier_semaphore()

    def greet(where):
        pl.semaphore_signal(barrier, inc=1, device_id=where, device_id_type=pl.DeviceIdType.MESH)

    greet(at(0, 0, -1))
    greet(at(0, 0, 1))
    for side in SIDES:

        def greet_side(side=side):
            for dx, dy, _ in MESSAGES:
                if dx == side:
                    greet(at(dx, dy, 0))

        beside(side, greet_side)
    greeted = 4 + 3 * (ix > 0).astype(jnp.int32) + 3 * (ix < nx - 1).astype(jnp.int32)

    loads = {}
    for n, (name, src, dst) in enumerate(
        (
            ("ps", ps_in, ps),
            ("pos", pos_in, pos),
            ("feat", feat_in, feat),
            ("wk", wk_in, wk),
            ("vs", vs_in, vs),
            ("nbr", nbr_in, nbr),
            ("cnt", cnt_in, cnt),
            ("wr", wr_in, wr),
            ("wq", wq_in, wq),
            ("wm", wm_in, wm),
            ("wv", wv_in, wv),
            ("wh", wh_in, wh),
            ("we", we_in, we),
        )
    ):
        loads[name] = pltpu.make_async_copy(src, dst, load_sem.at[n])
        loads[name].start()

    def remote(stage, group, src, dst, where):
        pltpu.make_async_remote_copy(
            src_ref=src,
            dst_ref=dst,
            send_sem=send_sem.at[stage, group],
            recv_sem=recv_sem.at[stage, group],
            device_id=where,
            device_id_type=pl.DeviceIdType.MESH,
        ).start()

    def plane(stage, src, src_at, dst, dst_at, sign):
        for group, side in enumerate(SIDES):

            def send(group=group, side=side):
                row = 0
                for dx, dy, quads in MESSAGES:
                    rows = G * len(quads)
                    if dx == side:
                        remote(
                            stage,
                            group,
                            src.at[pl.ds(src_at + row, rows)],
                            dst.at[pl.ds(dst_at + row, rows)],
                            at(sign * dx, sign * dy, 0),
                        )
                    row += rows

            beside(sign * side, send)

    def zone(stage, src, src_at, dst, dst_at):
        remote(stage, 0, src.at[pl.ds(src_at, G)], dst.at[pl.ds(dst_at + G, G)], at(0, 0, -1))
        remote(stage, 0, src.at[pl.ds(src_at + G, G)], dst.at[pl.ds(dst_at, G)], at(0, 0, 1))

    def zone_out(stage, src, src_at, dst):
        for group, side in enumerate(SIDES):

            def send(group=group, side=side):
                for m, (dx, dy) in enumerate(PLACES):
                    for f, dz in ((0, -1), (1, 1)):
                        if dx == side:
                            remote(
                                stage,
                                group,
                                src.at[pl.ds(src_at + (2 * m + f) * G, G)],
                                dst.at[pl.ds((2 * m + 1 - f) * G, G)],
                                at(-dx, -dy, dz),
                            )

            beside(-side, send)

    def give_back(stage, src, dst):
        for group, side in enumerate(SIDES):

            def send(group=group, side=side):
                for m, (dx, dy) in enumerate(PLACES):
                    for b, dz in ((0, -1), (1, 1)):
                        if dx == side:
                            remote(
                                stage,
                                group,
                                src.at[pl.ds(FIRST + b * G, G)],
                                dst.at[pl.ds(PLANE + (2 * m + 1 - b) * G, G)],
                                at(dx, dy, dz),
                            )

            beside(side, send)
        plane(stage + 1, src, A, dst, 0, -1)

    def arrived(stage, buf, row, rows, sign):
        for group, side in enumerate(SIDES):
            part = buf.at[pl.ds(row + rows * group, rows)]

            def wait(group=group, part=part):
                pltpu.make_async_copy(part, part, recv_sem.at[stage, group]).wait()

            beside(sign * side, wait)

    def sent(stage, buf, row, rows, sign):
        for group, side in enumerate(SIDES):
            part = buf.at[pl.ds(row + rows * group, rows)]

            def wait(group=group, part=part):
                pltpu.make_async_copy(part, part, send_sem.at[stage, group]).wait()

            beside(sign * side, wait)

    def arrived_zone(stage, buf):
        part = buf.at[pl.ds(FIRST, 2 * G)]

        @pl.when(ix >= 0)
        def _():
            pltpu.make_async_copy(part, part, recv_sem.at[stage, 0]).wait()

    def sent_zone(stage, buf):
        part = buf.at[pl.ds(0, 2 * G)]
        pltpu.make_async_copy(part, part, send_sem.at[stage, 0]).wait()

    def clear(group):
        def fill(buf, row, rows):
            buf[pl.ds(row, rows)] = jnp.zeros((rows,) + buf.shape[1:], F32)

        fill(pos_tab, A + PLANE_PART * group, PLANE_PART)
        fill(face_all, 3 * group, 3)
        fill(zone_in, ZONE_PART * (1 - group), ZONE_PART)
        for layer in range(LAYERS):
            fill(key_tab.at[layer], A + PLANE_PART * group, PLANE_PART)
        for back in (back_0, back_1):
            fill(back, PLANE + ZONE_PART * group, ZONE_PART)
            fill(back, PLANE_PART * (1 - group), PLANE_PART)

    pl.when(ix == 0)(lambda: clear(0))
    pl.when(ix == nx - 1)(lambda: clear(1))

    sub8, lane8 = iota((G, G), 0), iota((G, G), 1)

    def column(row):
        return jnp.sum(jnp.where(sub8 == lane8, row.astype(F32), 0.0), axis=1, keepdims=True)

    loads["ps"].wait()
    lane32 = iota((G, A), 1).astype(F32)
    quads = {
        (a, b): jnp.where(column(ps[0, 0, 0, a, b : b + 1, :]) == lane32, 1.0, 0.0)
        for a in range(2)
        for b in range(2)
    }
    eye = jnp.where(iota((A, A), 0) == iota((A, A), 1), 1.0, 0.0)
    pick_f = jnp.concatenate([eye] + [quads[a, b] for _, _, a, b in BLOCKS], axis=0)
    pick = pick_f.astype(BF)
    pick_all[pl.ds(0, FIRST), :] = pick

    loads["pos"].wait()
    own_parts = split3(jnp.concatenate([pos[q, 0, 0] for q in range(3)], axis=0))

    def place_rows(part):
        wide = jnp.concatenate([part.astype(F32), jnp.zeros((128 - 3, A), F32)], axis=0)
        return mm_nt(pick, wide.astype(BF))

    place = place_rows(own_parts[0]) + place_rows(own_parts[1]) + place_rows(own_parts[2])
    pos_tab[pl.ds(0, A), :] = place[:A]
    pos_send[...] = place[A:]

    def own_keys(layer, h):
        return exact(mm, h, wk[layer]).astype(BF)

    loads["feat"].wait()
    loads["wk"].wait()
    rows = mm(pick, own_keys(0, feat[0, 0, 0]))
    key_tab[0, pl.ds(0, A), :] = rows[:A]
    key_send[pl.ds(0, PLANE), :] = rows[A:]

    pl.semaphore_wait(barrier, greeted)
    plane(0, pos_send, 0, pos_tab, A, 1)
    plane(2, key_send, 0, key_tab.at[0], A, 1)

    loads["vs"].wait()
    lane_first = iota((1, FIRST), 1)
    label_row = lane_first
    for n in range(A // G, FIRST // G):
        label_row = label_row + jnp.where(lane_first >> 3 == n, LABELS[n] - n * G, 0)
    label_row = label_row.astype(F32)
    face_f = jnp.concatenate(
        [jnp.where(column(vs[0, 0, 0, f : f + 1, :]) == label_row, 1.0, 0.0) for f in range(2)],
        axis=0,
    )
    face = face_f.astype(BF)
    face_mine[...] = face_f
    for group, side in enumerate(SIDES):

        def send_face(group=group, side=side):
            for m, (dx, dy, _) in enumerate(MESSAGES):
                if dx == side:
                    remote(4, group, face_mine, face_all.at[m], at(dx, dy, 0))

        beside(side, send_face)

    mine = (iota((A, EDGES), 1) & (A - 1)) == iota((A, EDGES), 0)
    mine_f = jnp.where(mine, 1.0, 0.0)
    mine_b = mine_f.astype(BF)
    mine_s[...] = mine_f
    edge[pl.ds(ROWS, A), :] = mine_b
    edge[pl.ds(SELF, DEPTH - SELF), :] = jnp.zeros((DEPTH - SELF, EDGES), BF)
    dlat[pl.ds(C, 128), :] = jnp.zeros((128, EDGES), BF)
    for back in (back_0, back_1):
        back[pl.ds(BACK, DEPTH - BACK), :] = jnp.zeros((DEPTH - BACK, back.shape[1]), F32)
    slot_pick = jnp.where((iota((S, EDGES), 1) >> 5) == iota((S, EDGES), 0), 1.0, 0.0).astype(BF)
    loads["nbr"].wait()
    nbr_all = mm(nbr[0, 0, 0].astype(F32).astype(BF), slot_pick)
    nbr_row = jnp.sum(jnp.where(mine, nbr_all, 0.0), axis=0, keepdims=True)
    loads["cnt"].wait()
    cnt_rows = jnp.broadcast_to(cnt[0, 0].astype(F32), (16, A)).astype(BF)
    cnt_row = mm(cnt_rows, mine_b)[0:1]
    live = jnp.where((iota((1, EDGES), 1) >> 5).astype(F32) < cnt_row, 1.0, 0.0)
    def rest(layer, queries):
        radial_h, radial_l = split(wr[layer])
        radial_h, radial_l = radial_h.astype(F32), radial_l.astype(F32)
        zeros = jnp.zeros((DEPTH - SELF - 3 * NB, C), F32)
        rest_s[layer] = jnp.concatenate([queries, radial_h, radial_h, radial_l, zeros], axis=0)

    loads["wq"].wait()
    loads["wr"].wait()
    loads["wm"].wait()
    loads["wv"].wait()
    loads["wh"].wait()
    loads["we"].wait()
    h0 = feat[0, 0, 0]
    rest(0, exact(mm, h0, wq[0]))
    base_s[...] = exact(mm, h0, wk[1])
    for n, (mixing, after) in enumerate(((wm[0], wk[1]), (wm[1], wh[...]))):
        after_h, after_l = split(after)
        joint_h, joint_l = split(FACTOR * (mm(mixing, after_h) + mm(mixing, after_l)))
        joint[2 * n] = joint_h
        joint[2 * n + 1] = joint_l
    arrived(0, pos_tab, A, PLANE_PART, -1)
    first = pos_tab[pl.ds(0, FIRST), :]
    rows = sum(mm(face, part) for part in split3(first))
    span = BOX_SIDE * nz
    low_shift = jnp.where(iz == 0, span, 0.0).astype(F32)
    high_shift = jnp.where(iz == nz - 1, -span, 0.0).astype(F32)
    shift = jnp.where(iota((2 * G, 128), 0) < G, low_shift, high_shift)
    pos_face[...] = rows + jnp.where(iota((2 * G, 128), 1) == 2, shift, 0.0)
    zone(1, pos_face, 0, pos_tab, FIRST)

    arrived(2, key_tab.at[0], A, PLANE_PART, -1)
    face_send[...] = mm(face, key_tab[0, pl.ds(0, FIRST), :].astype(BF))
    zone(3, face_send, 0, key_tab.at[0], FIRST)

    tile = iota((16, EDGES), 0)
    for n in range(ROWS // 16):
        low, high = LABELS[2 * n], LABELS[2 * n + 1]
        label = jnp.where(tile < G, tile + low, tile + (high - G)).astype(F32)
        edge[pl.ds(16 * n, 16), :] = jnp.where(nbr_row == label, 1.0, 0.0).astype(BF)

    for group, side in enumerate(SIDES):
        slots = face_all.at[pl.ds(3 * group, 2 if side == 0 else 3)]

        def wait_face(group=group, slots=slots):
            pltpu.make_async_copy(slots, slots, recv_sem.at[4, group]).wait()

        beside(-side, wait_face)
    lane = iota((2 * G, FIRST), 1)
    parts, starts = [], [A]
    for _, _, quads in MESSAGES:
        starts.append(starts[-1] + G * len(quads))
    for m, (dx, dy) in enumerate(PLACES):
        if (dx, dy) == (0, 0):
            parts.append(jnp.where(lane < A, face_f, 0.0))
        else:
            to = PLACES.index((-dx, -dy))
            within = (lane >= starts[to]) & (lane < starts[to + 1])
            parts.append(jnp.where(within, face_all[m], 0.0))
    given = mm(jnp.concatenate(parts, axis=0).astype(BF), pick)
    pick_all[pl.ds(FIRST, ZONE), :] = given.astype(BF)
    pick_back[...] = jnp.concatenate(
        [pick_f[A:], given, jnp.zeros((DEPTH - BACK, A), F32)], axis=0
    ).T.astype(BF)

    arrived_zone(1, pos_tab)
    place = jnp.concatenate(
        [pos_tab[...], -pos_tab[pl.ds(0, A), :], jnp.zeros((DEPTH - SELF, 128), F32)], axis=0
    )
    place_t = place.T[0:G, :]
    parts = [part.astype(F32) for part in split3(place_t)] + [jnp.zeros((G, DEPTH), F32)]
    offset = mm(jnp.concatenate(parts, axis=0).astype(BF), edge[...])
    offset = offset[0:G] + (offset[G : 2 * G] + offset[2 * G : 3 * G])
    dist = jnp.sqrt(jnp.sum(offset * offset, axis=0, keepdims=True) + SOFTEN)
    inv = 1.0 / dist
    scaled = dist * (1.0 / CUTOFF)
    gap = 1.0 - scaled * scaled
    inside = jnp.where(scaled < 1.0, live, 0.0)
    envelope = inside * gap * gap
    unit = offset * inv
    order = (iota((NB, EDGES), 0) + 1).astype(F32)
    turn = order * scaled
    whole = jnp.floor(turn + 0.5)
    angle = (turn - whole) * math.pi
    sign = 1.0 - 2.0 * (whole - 2.0 * jnp.floor(0.5 * whole))
    sq = angle * angle
    sine, cosine = jnp.zeros_like(sq), jnp.zeros_like(sq)
    for n in range(6, -1, -1):
        sine = sine * sq + (-1.0) ** n / math.factorial(2 * n + 1)
        cosine = cosine * sq + (-1.0) ** n / math.factorial(2 * n)
    inv_scaled = CUTOFF * inv
    basis = sign * sine * angle * inv_scaled
    dbasis_s[...] = (order * math.pi * sign * cosine - basis) * inv_scaled
    unit_s[...] = unit
    geo[...] = jnp.concatenate(
        [envelope, inv, -4.0 * inside * gap * scaled, jnp.zeros((5, EDGES), F32)], axis=0
    )
    basis_h, basis_l = split(basis)
    basis_h, basis_l = basis_h.astype(F32), basis_l.astype(F32)
    edge[pl.ds(SELF, 32), :] = jnp.concatenate(
        [basis_h, basis_l, basis_h, jnp.zeros_like(basis)], axis=0
    ).astype(BF)
    for q in range(4):
        row = envelope if q == 0 else envelope * unit[q - 1 : q]
        w_h, w_l = split(row * mine_s[...])
        weight[pl.ds(A * q, A), :] = w_h
        weight[pl.ds(4 * A + A * q, A), :] = w_l

    def near_keys(layer):
        mt[:, pl.ds(0, FIRST)] = (0.5 * key_tab[layer, pl.ds(0, FIRST), :]).T.astype(BF)

    def forward(layer, zone_rows):
        rows = jnp.concatenate([zone_rows, rest_s[layer]], axis=0)
        mt[:, pl.ds(FIRST, DEPTH - FIRST)] = (0.5 * rows).T.astype(BF)
        for n in range(CHUNKS):
            part = pl.ds(n * STEP, STEP)
            half = mm(mt[...], edge[:, part])
            turned = jnp.tanh(half)
            more = 1.0 + turned
            active = (half * more).astype(BF)
            act[layer, :, part] = active
            slope[layer, :, part] = more * (1.0 + half * (1.0 - turned))
        total = mm_nt(weight[...], act[layer])
        total = total[: 4 * A] + total[4 * A :]
        gather_s[...] = total
        return total

    def vectors(layer):
        vec_h, vec_l = split(gather_s[pl.ds(A, 3 * A), :])
        vector = FACTOR * (mm_nt(vec_h, wv[layer]) + mm_nt(vec_l, wv[layer]))
        vec_s[layer] = vector
        dv_h, dv_l = split(vector * (2.0 / CT))
        gx = FACTOR * (mm(dv_h, wv[layer]) + mm(dv_l, wv[layer]))
        pull_s[layer, pl.ds(A, 3 * A), :] = gx.astype(BF)
        flipped = jnp.concatenate([jnp.zeros((A, C), F32), 0.5 * gx], axis=0).T.astype(BF)
        mp[layer, :, pl.ds(0, 4 * A)] = flipped
        mp[layer, :, pl.ds(4 * A, 4 * A)] = flipped

    def thrice(product, a, b_h, b_l):
        a_h, a_l = split(a)
        return product(a_h, b_h) + (product(a_h, b_l) + product(a_l, b_h))

    near_keys(0)

    arrived_zone(3, key_tab.at[0])
    total = forward(0, key_tab[0, pl.ds(FIRST, 2 * G), :])
    keys = base_s[...] + thrice(mm, total[:A], joint[0], joint[1])
    rows = mm(pick_all[...], keys.astype(BF))
    key_tab[1, pl.ds(0, A), :] = rows[:A]
    sent(2, key_send, 0, PLANE_PART, 1)
    key_send[...] = rows[A:]
    zone_out(6, key_send, PLANE, zone_in)
    plane(5, key_send, 0, key_tab.at[1], A, 1)

    gather_h, gather_l = split(gather_s[pl.ds(0, A), :])
    h1 = feat[0, 0, 0] + FACTOR * (mm(gather_h, wm[0]) + mm(gather_l, wm[0]))
    rest(1, exact(mm, h1, wq[1]))
    base_s[...] = exact(mm, h1, wh[...])
    vectors(0)
    arrived(5, key_tab.at[1], A, PLANE_PART, -1)
    near_keys(1)
    arrived(6, zone_in, 0, ZONE_PART, 1)
    zone_rows = zone_in[pl.ds(0, 2 * G), :]
    for m in range(1, len(PLACES)):
        zone_rows = zone_rows + zone_in[pl.ds(2 * G * m, 2 * G), :]
    total = forward(1, zone_rows)

    lat = base_s[...] + thrice(mm, total[:A], joint[2], joint[3])
    gate = 0.5 * jnp.tanh(0.5 * lat) + 0.5
    hidden = lat * gate
    readout = we[...]
    dhead = readout * (gate + hidden * (1.0 - gate))
    head_s[...] = dhead
    hidden_s[...] = hidden * readout
    vectors(1)

    def set_pull(layer, g0, g0_t):
        pull_s[layer, pl.ds(0, A), :] = g0.astype(BF)
        half = (0.5 * g0_t).astype(BF)
        mp[layer, :, pl.ds(0, A)] = half
        mp[layer, :, pl.ds(4 * A, A)] = half

    def flip(a, b):
        return mm_nt(b, a)

    def places(part, du, dbasis):
        unit, inv = unit_s[:, part], geo[1:2, part]
        along = jnp.sum(du * unit, axis=0, keepdims=True)
        dscaled = geo[2:3, part] * (du[3:4] + along) + jnp.sum(
            dbasis * dbasis_s[:, part], axis=0, keepdims=True
        )
        spread = geo[0:1, part] * inv
        return du * spread + unit * (dscaled * (1.0 / CUTOFF) - spread * along)

    def backward(layer):
        radial_h, radial_l = split(wr[layer])
        radial = jnp.concatenate([radial_h.astype(F32), radial_l.astype(F32)], axis=0).astype(BF)
        for n in range(CHUNKS):
            part = pl.ds(n * STEP, STEP)
            dl = (mm(mp[layer], weight[:, part]) * slope[layer, :, part]).astype(BF)
            dlat[pl.ds(0, C), part] = dl
            cross = mm(pull_s[layer], act[layer, :, part])
            rows = [
                jnp.sum(cross[A * q : A * q + A] * mine_s[:, :STEP], axis=0, keepdims=True)
                for q in range(4)
            ]
            rows = jnp.concatenate(rows[1:] + rows[:1] + [jnp.zeros((4, STEP), F32)], axis=0)
            got = mm(radial, dl)
            got = got[:NB] + got[NB:]
            if layer == LAYERS - 1:
                dw[:, part] = rows
                db[:, part] = got
            else:
                dr_h, dr_l = split(places(part, dw[:, part] + rows, db[:, part] + got))
                both = jnp.concatenate([dr_h.astype(F32), dr_l.astype(F32)], axis=0)
                dlat[pl.ds(C, 2 * G), part] = both.astype(BF)
        mine, back = (dkey_0, back_0) if layer == 0 else (dkey_1, back_1)
        drows = mm_nt(edge[pl.ds(0, SELF), :], dlat[pl.ds(0, mine.shape[1]), :])
        mine[...] = drows[:ROWS]
        give_back(7 + 2 * layer, mine, back)
        query_s[...] = drows[ROWS:, :C]
        if layer == 0:
            pos_own_s[...] = drows[ROWS:, C:]

    def collect(own, back):
        back_h, back_l = split(back)
        return own + (mm(pick_back[...], back_h) + mm(pick_back[...], back_l))

    def returned(layer):
        mine, back = (dkey_0, back_0) if layer == 0 else (dkey_1, back_1)
        arrived(8 + 2 * layer, back, 0, PLANE_PART, 1)
        arrived(7 + 2 * layer, back, PLANE, ZONE_PART, -1)
        return collect(mine[pl.ds(0, A), :], back[...])

    set_pull(1, thrice(mm_nt, dhead, joint[2], joint[3]), thrice(flip, dhead, joint[2], joint[3]))
    backward(1)

    square = vec_s[0] * vec_s[0] + vec_s[1] * vec_s[1]
    square = square[:A] + (square[A : 2 * A] + square[2 * A :])
    energy = jnp.sum(hidden_s[...], axis=1, keepdims=True) + jnp.sum(
        square, axis=1, keepdims=True
    ) * (1.0 / CT)
    en_out[0, 0] = jnp.sum(
        jnp.where(iota((A, A), 0) == iota((A, A), 1), energy, 0.0), axis=0, keepdims=True
    )
    dh = exact(mm_nt, head_s[...], wh[...]) + exact(mm_nt, query_s[...], wq[1])
    dh_s[...] = dh
    dh_h, dh_l = split(FACTOR * dh)
    base_s[...] = mm_nt(dh_h, wm[0]) + mm_nt(dh_l, wm[0])
    base_t[...] = mm_nt(wm[0], dh_h) + mm_nt(wm[0], dh_l)

    own = returned(1)
    set_pull(
        0,
        base_s[...] + thrice(mm_nt, own, joint[0], joint[1]),
        base_t[...] + thrice(flip, own, joint[0], joint[1]),
    )
    own_s[...] = own
    backward(0)

    dh = dh_s[...] + exact(mm_nt, own_s[...], wk[1])
    dh_s[...] = dh + exact(mm_nt, query_s[...], wq[0])
    own = returned(0)
    grad_out[0, 0, 0] = dh_s[...] + exact(mm_nt, own[:, :C], wk[0])
    pos_own = own[:, C:] - pos_own_s[...]
    pos_own = jnp.concatenate([pos_own, jnp.zeros((128 - A, 128), F32)], axis=0).T
    pos_own = -(pos_own[0:G, :A] + pos_own[G : 2 * G, :A])
    for q in range(3):
        force_out[q, 0, 0] = pos_own[q : q + 1]

    sent(0, pos_send, 0, PLANE_PART, 1)
    sent_zone(1, pos_face)
    sent_zone(3, face_send)
    for group, side in enumerate(SIDES):
        slots = face_all.at[pl.ds(3 * group, 2 if side == 0 else 3)]

        def wait_given(group=group, slots=slots):
            pltpu.make_async_copy(slots, slots, send_sem.at[4, group]).wait()

        beside(side, wait_given)
    sent(5, key_send, 0, PLANE_PART, 1)
    sent(6, key_send, PLANE, ZONE_PART, -1)
    for layer, back in enumerate((back_0, back_1)):
        sent(7 + 2 * layer, back, PLANE, ZONE_PART, 1)
        sent(8 + 2 * layer, back, 0, PLANE_PART, -1)


def hand_on(en_in, force_in, grad_in, en_out, force_out, grad_out, sem):
    grad_out[...] = grad_in[...]
    force_out[...] = force_in[...]
    en_out[...] = en_in[...]


def per_device(*args):
    hbm = pl.BlockSpec(memory_space=pltpu.HBM)
    vmem = pl.BlockSpec(memory_space=pltpu.VMEM)
    args = list(args)
    args[10] = args[10].swapaxes(1, 2)
    args[12] = args[12].reshape(1, C)
    f32, bf = (lambda *shape: pltpu.VMEM(shape, F32)), (lambda *shape: pltpu.VMEM(shape, BF))
    out_shape = (
        jax.ShapeDtypeStruct((1, 1, 1, A), F32),
        jax.ShapeDtypeStruct((3, 1, 1, 1, A), F32),
        jax.ShapeDtypeStruct((1, 1, 1, A, C), F32),
    )
    results = pl.pallas_call(
        kernel,
        out_shape=out_shape,
        in_specs=[hbm] * len(args),
        out_specs=(vmem,) * 3,
        scratch_shapes=[pltpu.VMEM(a.shape, a.dtype) for a in args]
        + [
            f32(2 * G, 128), f32(len(MESSAGES), 2 * G, 128), f32(ROWS, 128), f32(PLANE, 128),
            f32(2 * G, 128),
            f32(LAYERS, ROWS, C), f32(BACK, C), f32(2 * G, C), f32(ZONE, C),
            f32(ROWS, C + 128), f32(ROWS, C), f32(DEPTH, C + 128), f32(DEPTH, C),
            bf(FIRST + ZONE, A), bf(A, DEPTH), f32(A, EDGES), f32(8, EDGES), f32(G, EDGES),
            f32(NB, EDGES), bf(DEPTH, EDGES), bf(8 * A, EDGES), bf(LAYERS, C, EDGES),
            f32(LAYERS, C, EDGES), bf(C + 128, EDGES),
            bf(C, DEPTH), bf(LAYERS, C, 8 * A), f32(8, EDGES), f32(NB, EDGES),
            f32(A, C), f32(C, A), f32(A, C), f32(A, C), f32(A, C), f32(A, C), f32(A, C),
            f32(A, 128), f32(LAYERS, DEPTH - ROWS, C), f32(4 * A, C), bf(LAYERS, 4 * A, C),
            bf(4, C, C), f32(LAYERS, 3 * A, CT),
            pltpu.SemaphoreType.DMA((13,)),
            pltpu.SemaphoreType.DMA((11, 3)),
            pltpu.SemaphoreType.DMA((11, 3)),
        ],
        compiler_params=pltpu.CompilerParams(
            collective_id=0, has_side_effects=True, vmem_limit_bytes=60 * 1024 * 1024
        ),
        cost_estimate=pl.CostEstimate(
            flops=2_500_000_000, bytes_accessed=2_000_000, transcendentals=800_000
        ),
    )(*args)
    return pl.pallas_call(
        hand_on,
        out_shape=out_shape,
        in_specs=[vmem] * 3,
        out_specs=(vmem,) * 3,
        scratch_shapes=[pltpu.SemaphoreType.DMA((3,))],
        compiler_params=pltpu.CompilerParams(vmem_limit_bytes=60 * 1024 * 1024),
    )(*results)


def solution(mesh):
    return jax.shard_map(
        per_device,
        mesh=mesh,
        in_specs=(
            P(None, "gx", "gy", "gz", None),
            P("gx", "gy", "gz", None, None),
            P("gx", "gy", "gz", None, None, None),
            P("gx", "gy", "gz", None, None),
            P("gx", "gy", "gz", None, None),
            P("gx", "gy", "gz", None),
            P(),
            P(),
            P(),
            P(),
            P(),
            P(),
            P(),
        ),
        out_specs=(
            P("gx", "gy", "gz", None),
            P(None, "gx", "gy", "gz", None),
            P("gx", "gy", "gz", None, None),
        ),
        check_vma=False,
    )
```

```python
import math

import jax
import jax.numpy as jnp
from jax import lax
from jax.experimental import pallas as pl
from jax.experimental.pallas import tpu as pltpu
from jax.sharding import PartitionSpec as P

A, S, C, CT, NB, G = 32, 48, 256, 64, 8, 8
LAYERS = 2
EDGES = A * S
STEP = 256
CHUNKS = EDGES // STEP
CUTOFF, SOFTEN, BOX_SIDE = 6.0, 0.25, 4.0
FACTOR = 1.0 / math.sqrt(S)
F32, BF = jnp.float32, jnp.bfloat16

MESSAGES = (
    (1, 0, ((1, 0), (1, 1))),
    (1, 1, ((1, 1),)),
    (1, -1, ((1, 0),)),
    (-1, 0, ((0, 0), (0, 1))),
    (-1, 1, ((0, 1),)),
    (-1, -1, ((0, 0),)),
    (0, 1, ((0, 1), (1, 1))),
    (0, -1, ((0, 0), (1, 0))),
)
SIDES = (1, -1, 0)
BLOCKS = tuple((dx, dy, a, b) for dx, dy, quads in MESSAGES for a, b in quads)
PLANE = G * len(BLOCKS)
FIRST = A + PLANE
ROWS = FIRST + 2 * G
LABELS = tuple(range(0, A, G)) + tuple(
    A + ((1 - 2 * dx + a) * 4 + 1 - 2 * dy + b) * G for dx, dy, a, b in BLOCKS
) + (A + 16 * G, A + 19 * G)
SELF = ROWS + A
DEPTH = 256
PLACES = tuple((dx, dy) for dx, dy, _ in MESSAGES) + ((0, 0),)
ZONE = 2 * G * len(PLACES)
BACK = PLANE + ZONE
PLANE_PART, ZONE_PART = PLANE // 3, ZONE // 3


def mm(a, b):
    return lax.dot_general(a, b, (((1,), (0,)), ((), ())), preferred_element_type=F32)


def mm_nt(a, b):
    return lax.dot_general(a, b, (((1,), (1,)), ((), ())), preferred_element_type=F32)


def split(x):
    hi = x.astype(BF)
    return hi, (x - hi.astype(F32)).astype(BF)


def split3(x):
    hi, rest = x.astype(BF), x - x.astype(BF).astype(F32)
    mid = rest.astype(BF)
    return hi, mid, (rest - mid.astype(F32)).astype(BF)


def exact(product, a, b):
    ah, al = split(a)
    bh, bl = split(b)
    return product(ah, bh) + (product(ah, bl) + product(al, bh))


def corners_first(place):
    return -abs(place[1][0]) - abs(place[1][1])


def iota(shape, dim):
    return lax.broadcasted_iota(jnp.int32, shape, dim)


def kernel(
    pos_in, feat_in, ps_in, vs_in, nbr_in, cnt_in, wq_in, wk_in, wr_in, wm_in, wv_in, wh_in, we_in,
    en_out, force_out, grad_out,
    pos, feat, ps, vs, nbr, cnt, wq, wk, wr, wm, wv, wh, we,
    face_mine, face_all, pos_tab, pos_send, pos_face,
    key_tab, key_send, face_send, zone_in, dkey_0, dkey_1, back_0, back_1,
    pick_all, pick_back, mine_s, geo, unit_s, dbasis_s, edge, weight, act, slope, dlat,
    mt, mp, dw, db, base_s, base_t, dh_s, own_s, query_s, head_s, hidden_s,
    pos_own_s, rest_s, gather_s, pull_s, joint, vec_s,
    load_sem, send_sem, recv_sem,
):
    ix, iy, iz = (lax.axis_index(n) for n in ("gx", "gy", "gz"))
    nx, ny, nz = (lax.axis_size(n) for n in ("gx", "gy", "gz"))

    near_x = {d: ix + d if d else ix for d in (-1, 0, 1)}
    near_y = {d: lax.rem(iy + (d + ny), ny) if d else iy for d in (-1, 0, 1)}
    near_z = {d: lax.rem(iz + (d + nz), nz) if d else iz for d in (-1, 0, 1)}

    def at(dx, dy, dz):
        return {"gx": near_x[dx], "gy": near_y[dy], "gz": near_z[dz]}

    def beside(side, action):
        if side == 0:
            pl.when(ix >= 0)(action)
        elif side == 1:
            pl.when(ix < nx - 1)(action)
        else:
            pl.when(ix > 0)(action)

    barrier = pltpu.get_barrier_semaphore()

    def greet(where):
        pl.semaphore_signal(barrier, inc=1, device_id=where, device_id_type=pl.DeviceIdType.MESH)

    greet(at(0, 0, -1))
    greet(at(0, 0, 1))
    for side in SIDES:

        def greet_side(side=side):
            for dx, dy, _ in MESSAGES:
                if dx == side:
                    greet(at(dx, dy, 0))

        beside(side, greet_side)
    greeted = 4 + 3 * (ix > 0).astype(jnp.int32) + 3 * (ix < nx - 1).astype(jnp.int32)

    loads = {}
    for n, (name, src, dst) in enumerate(
        (
            ("ps", ps_in, ps),
            ("pos", pos_in, pos),
            ("feat", feat_in, feat),
            ("wk", wk_in, wk),
            ("vs", vs_in, vs),
            ("nbr", nbr_in, nbr),
            ("cnt", cnt_in, cnt),
            ("wr", wr_in, wr),
            ("wq", wq_in, wq),
            ("wm", wm_in, wm),
            ("wv", wv_in, wv),
            ("wh", wh_in, wh),
            ("we", we_in, we),
        )
    ):
        loads[name] = pltpu.make_async_copy(src, dst, load_sem.at[n])
        loads[name].start()

    def remote(stage, group, src, dst, where):
        pltpu.make_async_remote_copy(
            src_ref=src,
            dst_ref=dst,
            send_sem=send_sem.at[stage, group],
            recv_sem=recv_sem.at[stage, group],
            device_id=where,
            device_id_type=pl.DeviceIdType.MESH,
        ).start()

    def plane(stage, src, src_at, dst, dst_at, sign):
        for group, side in enumerate(SIDES):

            def send(group=group, side=side):
                row = 0
                for dx, dy, quads in MESSAGES:
                    rows = G * len(quads)
                    if dx == side:
                        remote(
                            stage,
                            group,
                            src.at[pl.ds(src_at + row, rows)],
                            dst.at[pl.ds(dst_at + row, rows)],
                            at(sign * dx, sign * dy, 0),
                        )
                    row += rows

            beside(sign * side, send)

    def zone(stage, src, src_at, dst, dst_at):
        remote(stage, 0, src.at[pl.ds(src_at, G)], dst.at[pl.ds(dst_at + G, G)], at(0, 0, -1))
        remote(stage, 0, src.at[pl.ds(src_at + G, G)], dst.at[pl.ds(dst_at, G)], at(0, 0, 1))

    def zone_out(stage, src, src_at, dst):
        for group, side in enumerate(SIDES):

            def send(group=group, side=side):
                for m, (dx, dy) in sorted(enumerate(PLACES), key=corners_first):
                    for f, dz in ((0, -1), (1, 1)):
                        if dx == side:
                            remote(
                                stage,
                                group,
                                src.at[pl.ds(src_at + (2 * m + f) * G, G)],
                                dst.at[pl.ds((2 * m + 1 - f) * G, G)],
                                at(-dx, -dy, dz),
                            )

            beside(-side, send)

    def give_back(stage, src, dst):
        for group, side in enumerate(SIDES):

            def send(group=group, side=side):
                for m, (dx, dy) in sorted(enumerate(PLACES), key=corners_first):
                    for b, dz in ((0, -1), (1, 1)):
                        if dx == side:
                            remote(
                                stage,
                                group,
                                src.at[pl.ds(FIRST + b * G, G)],
                                dst.at[pl.ds(PLANE + (2 * m + 1 - b) * G, G)],
                                at(dx, dy, dz),
                            )

            beside(side, send)
        plane(stage + 1, src, A, dst, 0, -1)

    def arrived(stage, buf, row, rows, sign):
        for group, side in enumerate(SIDES):
            part = buf.at[pl.ds(row + rows * group, rows)]

            def wait(group=group, part=part):
                pltpu.make_async_copy(part, part, recv_sem.at[stage, group]).wait()

            beside(sign * side, wait)

    def sent(stage, buf, row, rows, sign):
        for group, side in enumerate(SIDES):
            part = buf.at[pl.ds(row + rows * group, rows)]

            def wait(group=group, part=part):
                pltpu.make_async_copy(part, part, send_sem.at[stage, group]).wait()

            beside(sign * side, wait)

    def arrived_zone(stage, buf):
        part = buf.at[pl.ds(FIRST, 2 * G)]

        @pl.when(ix >= 0)
        def _():
            pltpu.make_async_copy(part, part, recv_sem.at[stage, 0]).wait()

    def sent_zone(stage, buf):
        part = buf.at[pl.ds(0, 2 * G)]
        pltpu.make_async_copy(part, part, send_sem.at[stage, 0]).wait()

    def clear(group):
        def fill(buf, row, rows):
            buf[pl.ds(row, rows)] = jnp.zeros((rows,) + buf.shape[1:], F32)

        fill(pos_tab, A + PLANE_PART * group, PLANE_PART)
        fill(face_all, 3 * group, 3)
        fill(zone_in, ZONE_PART * (1 - group), ZONE_PART)
        for layer in range(LAYERS):
            fill(key_tab.at[layer], A + PLANE_PART * group, PLANE_PART)
        for back in (back_0, back_1):
            fill(back, PLANE + ZONE_PART * group, ZONE_PART)
            fill(back, PLANE_PART * (1 - group), PLANE_PART)

    pl.when(ix == 0)(lambda: clear(0))
    pl.when(ix == nx - 1)(lambda: clear(1))

    sub8, lane8 = iota((G, G), 0), iota((G, G), 1)

    def column(row):
        return jnp.sum(jnp.where(sub8 == lane8, row.astype(F32), 0.0), axis=1, keepdims=True)

    loads["ps"].wait()
    lane32 = iota((G, A), 1).astype(F32)
    quads = {
        (a, b): jnp.where(column(ps[0, 0, 0, a, b : b + 1, :]) == lane32, 1.0, 0.0)
        for a in range(2)
        for b in range(2)
    }
    eye = jnp.where(iota((A, A), 0) == iota((A, A), 1), 1.0, 0.0)
    pick_f = jnp.concatenate([eye] + [quads[a, b] for _, _, a, b in BLOCKS], axis=0)
    pick = pick_f.astype(BF)
    pick_all[pl.ds(0, FIRST), :] = pick

    loads["pos"].wait()
    own_parts = split3(jnp.concatenate([pos[q, 0, 0] for q in range(3)], axis=0))

    def place_rows(part):
        wide = jnp.concatenate([part.astype(F32), jnp.zeros((128 - 3, A), F32)], axis=0)
        return mm_nt(pick, wide.astype(BF))

    place = place_rows(own_parts[0]) + place_rows(own_parts[1]) + place_rows(own_parts[2])
    pos_tab[pl.ds(0, A), :] = place[:A]
    pos_send[...] = place[A:]

    def own_keys(layer, h):
        return exact(mm, h, wk[layer]).astype(BF)

    loads["feat"].wait()
    loads["wk"].wait()
    rows = mm(pick, own_keys(0, feat[0, 0, 0]))
    key_tab[0, pl.ds(0, A), :] = rows[:A]
    key_send[pl.ds(0, PLANE), :] = rows[A:]

    pl.semaphore_wait(barrier, greeted)
    plane(0, pos_send, 0, pos_tab, A, 1)
    plane(2, key_send, 0, key_tab.at[0], A, 1)

    loads["vs"].wait()
    lane_first = iota((1, FIRST), 1)
    label_row = lane_first
    for n in range(A // G, FIRST // G):
        label_row = label_row + jnp.where(lane_first >> 3 == n, LABELS[n] - n * G, 0)
    label_row = label_row.astype(F32)
    face_f = jnp.concatenate(
        [jnp.where(column(vs[0, 0, 0, f : f + 1, :]) == label_row, 1.0, 0.0) for f in range(2)],
        axis=0,
    )
    face = face_f.astype(BF)
    face_mine[...] = face_f
    for group, side in enumerate(SIDES):

        def send_face(group=group, side=side):
            for m, (dx, dy, _) in enumerate(MESSAGES):
                if dx == side:
                    remote(4, group, face_mine, face_all.at[m], at(dx, dy, 0))

        beside(side, send_face)

    mine = (iota((A, EDGES), 1) & (A - 1)) == iota((A, EDGES), 0)
    mine_f = jnp.where(mine, 1.0, 0.0)
    mine_b = mine_f.astype(BF)
    mine_s[...] = mine_f
    edge[pl.ds(ROWS, A), :] = mine_b
    edge[pl.ds(SELF, DEPTH - SELF), :] = jnp.zeros((DEPTH - SELF, EDGES), BF)
    dlat[pl.ds(C, 128), :] = jnp.zeros((128, EDGES), BF)
    for back in (back_0, back_1):
        back[pl.ds(BACK, DEPTH - BACK), :] = jnp.zeros((DEPTH - BACK, back.shape[1]), F32)
    slot_pick = jnp.where((iota((S, EDGES), 1) >> 5) == iota((S, EDGES), 0), 1.0, 0.0).astype(BF)
    loads["nbr"].wait()
    nbr_all = mm(nbr[0, 0, 0].astype(F32).astype(BF), slot_pick)
    nbr_row = jnp.sum(jnp.where(mine, nbr_all, 0.0), axis=0, keepdims=True)
    loads["cnt"].wait()
    cnt_rows = jnp.broadcast_to(cnt[0, 0].astype(F32), (16, A)).astype(BF)
    cnt_row = mm(cnt_rows, mine_b)[0:1]
    live = jnp.where((iota((1, EDGES), 1) >> 5).astype(F32) < cnt_row, 1.0, 0.0)
    def rest(layer, queries):
        radial_h, radial_l = split(wr[layer])
        radial_h, radial_l = radial_h.astype(F32), radial_l.astype(F32)
        zeros = jnp.zeros((DEPTH - SELF - 3 * NB, C), F32)
        rest_s[layer] = jnp.concatenate([queries, radial_h, radial_h, radial_l, zeros], axis=0)

    loads["wq"].wait()
    loads["wr"].wait()
    loads["wm"].wait()
    loads["wv"].wait()
    loads["wh"].wait()
    loads["we"].wait()
    h0 = feat[0, 0, 0]
    rest(0, exact(mm, h0, wq[0]))
    base_s[...] = exact(mm, h0, wk[1])
    joint[4], joint[5] = split(wk[0])
    for n, (mixing, after) in enumerate(((wm[0], wk[1]), (wm[1], wh[...]))):
        after_h, after_l = split(after)
        joint_h, joint_l = split(FACTOR * (mm(mixing, after_h) + mm(mixing, after_l)))
        joint[2 * n] = joint_h
        joint[2 * n + 1] = joint_l
    arrived(0, pos_tab, A, PLANE_PART, -1)
    first = pos_tab[pl.ds(0, FIRST), :]
    rows = sum(mm(face, part) for part in split3(first))
    span = BOX_SIDE * nz
    low_shift = jnp.where(iz == 0, span, 0.0).astype(F32)
    high_shift = jnp.where(iz == nz - 1, -span, 0.0).astype(F32)
    shift = jnp.where(iota((2 * G, 128), 0) < G, low_shift, high_shift)
    pos_face[...] = rows + jnp.where(iota((2 * G, 128), 1) == 2, shift, 0.0)
    zone(1, pos_face, 0, pos_tab, FIRST)

    arrived(2, key_tab.at[0], A, PLANE_PART, -1)
    face_send[...] = mm(face, key_tab[0, pl.ds(0, FIRST), :].astype(BF))
    zone(3, face_send, 0, key_tab.at[0], FIRST)

    tile = iota((16, EDGES), 0)
    for n in range(ROWS // 16):
        low, high = LABELS[2 * n], LABELS[2 * n + 1]
        label = jnp.where(tile < G, tile + low, tile + (high - G)).astype(F32)
        edge[pl.ds(16 * n, 16), :] = jnp.where(nbr_row == label, 1.0, 0.0).astype(BF)

    for group, side in enumerate(SIDES):
        slots = face_all.at[pl.ds(3 * group, 2 if side == 0 else 3)]

        def wait_face(group=group, slots=slots):
            pltpu.make_async_copy(slots, slots, recv_sem.at[4, group]).wait()

        beside(-side, wait_face)
    lane = iota((2 * G, FIRST), 1)
    parts, starts = [], [A]
    for _, _, quads in MESSAGES:
        starts.append(starts[-1] + G * len(quads))
    for m, (dx, dy) in enumerate(PLACES):
        if (dx, dy) == (0, 0):
            parts.append(jnp.where(lane < A, face_f, 0.0))
        else:
            to = PLACES.index((-dx, -dy))
            within = (lane >= starts[to]) & (lane < starts[to + 1])
            parts.append(jnp.where(within, face_all[m], 0.0))
    given = mm(jnp.concatenate(parts, axis=0).astype(BF), pick)
    pick_all[pl.ds(FIRST, ZONE), :] = given.astype(BF)
    pick_back[...] = jnp.concatenate(
        [pick_f[A:], given, jnp.zeros((DEPTH - BACK, A), F32)], axis=0
    ).T.astype(BF)

    arrived_zone(1, pos_tab)
    place = jnp.concatenate(
        [pos_tab[...], -pos_tab[pl.ds(0, A), :], jnp.zeros((DEPTH - SELF, 128), F32)], axis=0
    )
    place_t = place.T[0:G, :]
    parts = [part.astype(F32) for part in split3(place_t)] + [jnp.zeros((G, DEPTH), F32)]
    offset = mm(jnp.concatenate(parts, axis=0).astype(BF), edge[...])
    offset = offset[0:G] + (offset[G : 2 * G] + offset[2 * G : 3 * G])
    dist = jnp.sqrt(jnp.sum(offset * offset, axis=0, keepdims=True) + SOFTEN)
    inv = 1.0 / dist
    scaled = dist * (1.0 / CUTOFF)
    gap = 1.0 - scaled * scaled
    inside = jnp.where(scaled < 1.0, live, 0.0)
    envelope = inside * gap * gap
    unit = offset * inv
    order = (iota((NB, EDGES), 0) + 1).astype(F32)
    turn = order * scaled
    whole = jnp.floor(turn + 0.5)
    angle = (turn - whole) * math.pi
    sign = 1.0 - 2.0 * (whole - 2.0 * jnp.floor(0.5 * whole))
    sq = angle * angle
    sine, cosine = jnp.zeros_like(sq), jnp.zeros_like(sq)
    for n in range(6, -1, -1):
        sine = sine * sq + (-1.0) ** n / math.factorial(2 * n + 1)
        cosine = cosine * sq + (-1.0) ** n / math.factorial(2 * n)
    inv_scaled = CUTOFF * inv
    basis = sign * sine * angle * inv_scaled
    dbasis_s[...] = (order * math.pi * sign * cosine - basis) * inv_scaled
    unit_s[...] = unit
    geo[...] = jnp.concatenate(
        [envelope, inv, -4.0 * inside * gap * scaled, jnp.zeros((5, EDGES), F32)], axis=0
    )
    basis_h, basis_l = split(basis)
    basis_h, basis_l = basis_h.astype(F32), basis_l.astype(F32)
    edge[pl.ds(SELF, 32), :] = jnp.concatenate(
        [basis_h, basis_l, basis_h, jnp.zeros_like(basis)], axis=0
    ).astype(BF)
    for q in range(4):
        row = envelope if q == 0 else envelope * unit[q - 1 : q]
        w_h, w_l = split(row * mine_s[...])
        weight[pl.ds(A * q, A), :] = w_h
        weight[pl.ds(4 * A + A * q, A), :] = w_l

    def near_keys(layer):
        mt[:, pl.ds(0, FIRST)] = (0.5 * key_tab[layer, pl.ds(0, FIRST), :]).T.astype(BF)

    def forward(layer, zone_rows):
        rows = jnp.concatenate([zone_rows, rest_s[layer]], axis=0)
        mt[:, pl.ds(FIRST, DEPTH - FIRST)] = (0.5 * rows).T.astype(BF)
        for n in range(CHUNKS):
            part = pl.ds(n * STEP, STEP)
            half = mm(mt[...], edge[:, part])
            turned = jnp.tanh(half)
            more = 1.0 + turned
            active = (half * more).astype(BF)
            act[layer, :, part] = active
            slope[layer, :, part] = more * (1.0 + half * (1.0 - turned))
        total = mm_nt(weight[...], act[layer])
        total = total[: 4 * A] + total[4 * A :]
        gather_s[...] = total
        return total

    def vectors(layer):
        vec_h, vec_l = split(gather_s[pl.ds(A, 3 * A), :])
        vector = FACTOR * (mm_nt(vec_h, wv[layer]) + mm_nt(vec_l, wv[layer]))
        vec_s[layer] = vector
        dv_h, dv_l = split(vector * (2.0 / CT))
        gx = FACTOR * (mm(dv_h, wv[layer]) + mm(dv_l, wv[layer]))
        pull_s[layer, pl.ds(A, 3 * A), :] = gx.astype(BF)
        flipped = jnp.concatenate([jnp.zeros((A, C), F32), 0.5 * gx], axis=0).T.astype(BF)
        mp[layer, :, pl.ds(0, 4 * A)] = flipped
        mp[layer, :, pl.ds(4 * A, 4 * A)] = flipped

    def thrice(product, a, b_h, b_l):
        a_h, a_l = split(a)
        return product(a_h, b_h) + (product(a_h, b_l) + product(a_l, b_h))

    near_keys(0)

    arrived_zone(3, key_tab.at[0])
    total = forward(0, key_tab[0, pl.ds(FIRST, 2 * G), :])
    keys = base_s[...] + thrice(mm, total[:A], joint[0], joint[1])
    rows = mm(pick_all[...], keys.astype(BF))
    key_tab[1, pl.ds(0, A), :] = rows[:A]
    sent(2, key_send, 0, PLANE_PART, 1)
    key_send[...] = rows[A:]
    zone_out(6, key_send, PLANE, zone_in)
    plane(5, key_send, 0, key_tab.at[1], A, 1)

    gather_h, gather_l = split(gather_s[pl.ds(0, A), :])
    h1 = feat[0, 0, 0] + FACTOR * (mm(gather_h, wm[0]) + mm(gather_l, wm[0]))
    rest(1, exact(mm, h1, wq[1]))
    base_s[...] = exact(mm, h1, wh[...])
    vectors(0)
    arrived(5, key_tab.at[1], A, PLANE_PART, -1)
    near_keys(1)
    arrived(6, zone_in, 0, ZONE_PART, 1)
    zone_rows = zone_in[pl.ds(0, 2 * G), :]
    for m in range(1, len(PLACES)):
        zone_rows = zone_rows + zone_in[pl.ds(2 * G * m, 2 * G), :]
    total = forward(1, zone_rows)

    lat = base_s[...] + thrice(mm, total[:A], joint[2], joint[3])
    gate = 0.5 * jnp.tanh(0.5 * lat) + 0.5
    hidden = lat * gate
    readout = we[...]
    dhead = readout * (gate + hidden * (1.0 - gate))
    head_s[...] = dhead
    hidden_s[...] = hidden * readout
    vectors(1)

    def set_pull(layer, g0, g0_t):
        pull_s[layer, pl.ds(0, A), :] = g0.astype(BF)
        half = (0.5 * g0_t).astype(BF)
        mp[layer, :, pl.ds(0, A)] = half
        mp[layer, :, pl.ds(4 * A, A)] = half

    def flip(a, b):
        return mm_nt(b, a)

    def places(part, du, dbasis):
        unit, inv = unit_s[:, part], geo[1:2, part]
        along = jnp.sum(du * unit, axis=0, keepdims=True)
        dscaled = geo[2:3, part] * (du[3:4] + along) + jnp.sum(
            dbasis * dbasis_s[:, part], axis=0, keepdims=True
        )
        spread = geo[0:1, part] * inv
        return du * spread + unit * (dscaled * (1.0 / CUTOFF) - spread * along)

    def backward(layer):
        radial_h, radial_l = split(wr[layer])
        radial = jnp.concatenate([radial_h.astype(F32), radial_l.astype(F32)], axis=0).astype(BF)
        for n in range(CHUNKS):
            part = pl.ds(n * STEP, STEP)
            dl = (mm(mp[layer], weight[:, part]) * slope[layer, :, part]).astype(BF)
            dlat[pl.ds(0, C), part] = dl
            cross = mm(pull_s[layer], act[layer, :, part])
            rows = [
                jnp.sum(cross[A * q : A * q + A] * mine_s[:, :STEP], axis=0, keepdims=True)
                for q in range(4)
            ]
            rows = jnp.concatenate(rows[1:] + rows[:1] + [jnp.zeros((4, STEP), F32)], axis=0)
            got = mm(radial, dl)
            got = got[:NB] + got[NB:]
            if layer == LAYERS - 1:
                dw[:, part] = rows
                db[:, part] = got
            else:
                dr_h, dr_l = split(places(part, dw[:, part] + rows, db[:, part] + got))
                both = jnp.concatenate([dr_h.astype(F32), dr_l.astype(F32)], axis=0)
                dlat[pl.ds(C, 2 * G), part] = both.astype(BF)
        mine, back = (dkey_0, back_0) if layer == 0 else (dkey_1, back_1)
        drows = mm_nt(edge[pl.ds(0, SELF), :], dlat[pl.ds(0, mine.shape[1]), :])
        mine[...] = drows[:ROWS]
        give_back(7 + 2 * layer, mine, back)
        query_s[...] = drows[ROWS:, :C]
        if layer == 0:
            pos_own_s[...] = drows[ROWS:, C:]

    def collect(own, back):
        return own + mm(pick_back[...], back.astype(BF))

    def returned(layer):
        mine, back = (dkey_0, back_0) if layer == 0 else (dkey_1, back_1)
        arrived(8 + 2 * layer, back, 0, PLANE_PART, 1)
        arrived(7 + 2 * layer, back, PLANE, ZONE_PART, -1)
        return collect(mine[pl.ds(0, A), :], back[...])

    set_pull(1, thrice(mm_nt, dhead, joint[2], joint[3]), thrice(flip, dhead, joint[2], joint[3]))
    backward(1)

    square = vec_s[0] * vec_s[0] + vec_s[1] * vec_s[1]
    square = square[:A] + (square[A : 2 * A] + square[2 * A :])
    energy = jnp.sum(hidden_s[...], axis=1, keepdims=True) + jnp.sum(
        square, axis=1, keepdims=True
    ) * (1.0 / CT)
    en_out[0, 0] = jnp.sum(
        jnp.where(iota((A, A), 0) == iota((A, A), 1), energy, 0.0), axis=0, keepdims=True
    )
    dh = exact(mm_nt, head_s[...], wh[...]) + exact(mm_nt, query_s[...], wq[1])
    dh_s[...] = dh
    dh_h, dh_l = split(FACTOR * dh)
    base_s[...] = mm_nt(dh_h, wm[0]) + mm_nt(dh_l, wm[0])
    base_t[...] = mm_nt(wm[0], dh_h) + mm_nt(wm[0], dh_l)

    own = returned(1)
    set_pull(
        0,
        base_s[...] + thrice(mm_nt, own, joint[0], joint[1]),
        base_t[...] + thrice(flip, own, joint[0], joint[1]),
    )
    own_s[...] = own
    backward(0)

    dh = dh_s[...] + exact(mm_nt, own_s[...], wk[1])
    dh_s[...] = dh + exact(mm_nt, query_s[...], wq[0])
    sent(0, pos_send, 0, PLANE_PART, 1)
    sent_zone(1, pos_face)
    sent_zone(3, face_send)
    for group, side in enumerate(SIDES):
        slots = face_all.at[pl.ds(3 * group, 2 if side == 0 else 3)]

        def wait_given(group=group, slots=slots):
            pltpu.make_async_copy(slots, slots, send_sem.at[4, group]).wait()

        beside(side, wait_given)
    sent(5, key_send, 0, PLANE_PART, 1)
    sent(6, key_send, PLANE, ZONE_PART, -1)
    sent(9, back_1, PLANE, ZONE_PART, 1)
    sent(10, back_1, 0, PLANE_PART, -1)
    sent(7, back_0, PLANE, ZONE_PART, 1)
    sent(8, back_0, 0, PLANE_PART, -1)
    own = returned(0)
    grad_out[0, 0, 0] = dh_s[...] + thrice(mm_nt, own[:, :C], joint[4], joint[5])
    pos_own = own[:, C:] - pos_own_s[...]
    pos_own = jnp.concatenate([pos_own, jnp.zeros((128 - A, 128), F32)], axis=0).T
    pos_own = -(pos_own[0:G, :A] + pos_own[G : 2 * G, :A])
    for q in range(3):
        force_out[q, 0, 0] = pos_own[q : q + 1]


def hand_on(*refs):
    copies = [pltpu.make_async_copy(refs[n], refs[3 + n], refs[6].at[n]) for n in range(3)]
    for copy in copies:
        copy.start()
    for copy in copies:
        copy.wait()


def per_device(*args):
    hbm = pl.BlockSpec(memory_space=pltpu.HBM)
    vmem = pl.BlockSpec(memory_space=pltpu.VMEM)
    args = list(args)
    args[10] = args[10].swapaxes(1, 2)
    args[12] = args[12].reshape(1, C)
    args = [pltpu.with_memory_space_constraint(a, pltpu.HBM) for a in args]
    f32, bf = (lambda *shape: pltpu.VMEM(shape, F32)), (lambda *shape: pltpu.VMEM(shape, BF))
    out_shape = (
        jax.ShapeDtypeStruct((1, 1, 1, A), F32),
        jax.ShapeDtypeStruct((3, 1, 1, 1, A), F32),
        jax.ShapeDtypeStruct((1, 1, 1, A, C), F32),
    )
    results = pl.pallas_call(
        kernel,
        out_shape=tuple(pltpu.VMEM(a.shape, a.dtype) for a in out_shape),
        in_specs=[hbm] * len(args),
        out_specs=(vmem,) * 3,
        scratch_shapes=[pltpu.VMEM(a.shape, a.dtype) for a in args]
        + [
            f32(2 * G, 128), f32(len(MESSAGES), 2 * G, 128), f32(ROWS, 128), f32(PLANE, 128),
            f32(2 * G, 128),
            f32(LAYERS, ROWS, C), f32(BACK, C), f32(2 * G, C), f32(ZONE, C),
            f32(ROWS, C + 128), f32(ROWS, C), f32(DEPTH, C + 128), f32(DEPTH, C),
            bf(FIRST + ZONE, A), bf(A, DEPTH), f32(A, EDGES), f32(8, EDGES), f32(G, EDGES),
            f32(NB, EDGES), bf(DEPTH, EDGES), bf(8 * A, EDGES), bf(LAYERS, C, EDGES),
            f32(LAYERS, C, EDGES), bf(C + 128, EDGES),
            bf(C, DEPTH), bf(LAYERS, C, 8 * A), f32(8, EDGES), f32(NB, EDGES),
            f32(A, C), f32(C, A), f32(A, C), f32(A, C), f32(A, C), f32(A, C), f32(A, C),
            f32(A, 128), f32(LAYERS, DEPTH - ROWS, C), f32(4 * A, C), bf(LAYERS, 4 * A, C),
            bf(6, C, C), f32(LAYERS, 3 * A, CT),
            pltpu.SemaphoreType.DMA((13,)),
            pltpu.SemaphoreType.DMA((11, 3)),
            pltpu.SemaphoreType.DMA((11, 3)),
        ],
        compiler_params=pltpu.CompilerParams(
            collective_id=0, has_side_effects=True, vmem_limit_bytes=32 * 1024 * 1024
        ),
        cost_estimate=pl.CostEstimate(
            flops=2_500_000_000, bytes_accessed=2_000_000, transcendentals=800_000
        ),
    )(*args)
    return pl.pallas_call(
        hand_on,
        out_shape=out_shape,
        in_specs=[vmem] * 3,
        out_specs=(hbm,) * 3,
        scratch_shapes=[pltpu.SemaphoreType.DMA((3,))],
        compiler_params=pltpu.CompilerParams(vmem_limit_bytes=32 * 1024 * 1024),
    )(*[pltpu.with_memory_space_constraint(a, pltpu.VMEM) for a in results])


def solution(mesh):
    return jax.shard_map(
        per_device,
        mesh=mesh,
        in_specs=(
            P(None, "gx", "gy", "gz", None),
            P("gx", "gy", "gz", None, None),
            P("gx", "gy", "gz", None, None, None),
            P("gx", "gy", "gz", None, None),
            P("gx", "gy", "gz", None, None),
            P("gx", "gy", "gz", None),
            P(),
            P(),
            P(),
            P(),
            P(),
            P(),
            P(),
        ),
        out_specs=(
            P("gx", "gy", "gz", None),
            P(None, "gx", "gy", "gz", None),
            P("gx", "gy", "gz", None, None),
        ),
        check_vma=False,
    )
```

```python
import math

import jax
import jax.numpy as jnp
from jax import lax
from jax.experimental import pallas as pl
from jax.experimental.pallas import tpu as pltpu
from jax.sharding import PartitionSpec as P

A, S, C, CT, NB, G = 32, 48, 256, 64, 8, 8
LAYERS = 2
EDGES = A * S
STEP = 256
CHUNKS = EDGES // STEP
CUTOFF, SOFTEN, BOX_SIDE = 6.0, 0.25, 4.0
FACTOR = 1.0 / math.sqrt(S)
F32, BF = jnp.float32, jnp.bfloat16

MESSAGES = (
    (1, 0, ((1, 0), (1, 1))),
    (1, 1, ((1, 1),)),
    (1, -1, ((1, 0),)),
    (-1, 0, ((0, 0), (0, 1))),
    (-1, 1, ((0, 1),)),
    (-1, -1, ((0, 0),)),
    (0, 1, ((0, 1), (1, 1))),
    (0, -1, ((0, 0), (1, 0))),
)
SIDES = (1, -1, 0)
BLOCKS = tuple((dx, dy, a, b) for dx, dy, quads in MESSAGES for a, b in quads)
PLANE = G * len(BLOCKS)
FIRST = A + PLANE
ROWS = FIRST + 2 * G
LABELS = tuple(range(0, A, G)) + tuple(
    A + ((1 - 2 * dx + a) * 4 + 1 - 2 * dy + b) * G for dx, dy, a, b in BLOCKS
) + (A + 16 * G, A + 19 * G)
SELF = ROWS + A
DEPTH = 256
PLACES = tuple((dx, dy) for dx, dy, _ in MESSAGES) + ((0, 0),)
ZONE = 2 * G * len(PLACES)
BACK = PLANE + ZONE
PLANE_PART, ZONE_PART = PLANE // 3, ZONE // 3


def mm(a, b):
    return lax.dot_general(a, b, (((1,), (0,)), ((), ())), preferred_element_type=F32)


def mm_nt(a, b):
    return lax.dot_general(a, b, (((1,), (1,)), ((), ())), preferred_element_type=F32)


def split(x):
    hi = x.astype(BF)
    return hi, (x - hi.astype(F32)).astype(BF)


def split3(x):
    hi, rest = x.astype(BF), x - x.astype(BF).astype(F32)
    mid = rest.astype(BF)
    return hi, mid, (rest - mid.astype(F32)).astype(BF)


def exact(product, a, b):
    ah, al = split(a)
    bh, bl = split(b)
    return product(ah, bh) + (product(ah, bl) + product(al, bh))


def corners_first(place):
    return -abs(place[1][0]) - abs(place[1][1])


def iota(shape, dim):
    return lax.broadcasted_iota(jnp.int32, shape, dim)


def kernel(
    pos_in, feat_in, ps_in, vs_in, nbr_in, cnt_in, wq_in, wk_in, wr_in, wm_in, wv_in, wh_in, we_in,
    en_out, force_out, grad_out,
    pos, feat, ps, vs, nbr, cnt, wq, wk, wr, wm, wv, wh, we,
    face_mine, face_all, pos_tab, pos_send, pos_face,
    key_tab, key_send, face_send, zone_in, dkey_0, dkey_1, back_0, back_1,
    pick_all, pick_back, mine_s, geo, unit_s, dbasis_s, edge, weight, act, slope, dlat,
    mt, mp, dw, db, base_s, base_t, dh_s, own_s, query_s, head_s, hidden_s,
    pos_own_s, rest_s, gather_s, pull_s, joint, vec_s,
    load_sem, send_sem, recv_sem,
):
    ix, iy, iz = (lax.axis_index(n) for n in ("gx", "gy", "gz"))
    nx, ny, nz = (lax.axis_size(n) for n in ("gx", "gy", "gz"))

    near_x = {d: ix + d if d else ix for d in (-1, 0, 1)}
    near_y = {d: lax.rem(iy + (d + ny), ny) if d else iy for d in (-1, 0, 1)}
    near_z = {d: lax.rem(iz + (d + nz), nz) if d else iz for d in (-1, 0, 1)}

    def at(dx, dy, dz):
        return {"gx": near_x[dx], "gy": near_y[dy], "gz": near_z[dz]}

    def beside(side, action):
        if side == 0:
            pl.when(ix >= 0)(action)
        elif side == 1:
            pl.when(ix < nx - 1)(action)
        else:
            pl.when(ix > 0)(action)

    barrier = pltpu.get_barrier_semaphore()

    def greet(where):
        pl.semaphore_signal(barrier, inc=1, device_id=where, device_id_type=pl.DeviceIdType.MESH)

    greet(at(0, 0, -1))
    greet(at(0, 0, 1))
    for side in SIDES:

        def greet_side(side=side):
            for dx, dy, _ in MESSAGES:
                if dx == side:
                    greet(at(dx, dy, 0))

        beside(side, greet_side)
    greeted = 4 + 3 * (ix > 0).astype(jnp.int32) + 3 * (ix < nx - 1).astype(jnp.int32)

    loads = {}
    for n, (name, src, dst) in enumerate(
        (
            ("ps", ps_in, ps),
            ("pos", pos_in, pos),
            ("feat", feat_in, feat),
            ("wk", wk_in, wk),
            ("vs", vs_in, vs),
            ("nbr", nbr_in, nbr),
            ("cnt", cnt_in, cnt),
            ("wr", wr_in, wr),
            ("wq", wq_in, wq),
            ("wm", wm_in, wm),
            ("wv", wv_in, wv),
            ("wh", wh_in, wh),
            ("we", we_in, we),
        )
    ):
        loads[name] = pltpu.make_async_copy(src, dst, load_sem.at[n])
        loads[name].start()

    def remote(stage, group, src, dst, where):
        pltpu.make_async_remote_copy(
            src_ref=src,
            dst_ref=dst,
            send_sem=send_sem.at[stage, group],
            recv_sem=recv_sem.at[stage, group],
            device_id=where,
            device_id_type=pl.DeviceIdType.MESH,
        ).start()

    def plane(stage, src, src_at, dst, dst_at, sign):
        for group, side in enumerate(SIDES):

            def send(group=group, side=side):
                row = 0
                for dx, dy, quads in MESSAGES:
                    rows = G * len(quads)
                    if dx == side:
                        remote(
                            stage,
                            group,
                            src.at[pl.ds(src_at + row, rows)],
                            dst.at[pl.ds(dst_at + row, rows)],
                            at(sign * dx, sign * dy, 0),
                        )
                    row += rows

            beside(sign * side, send)

    def zone(stage, src, src_at, dst, dst_at):
        remote(stage, 0, src.at[pl.ds(src_at, G)], dst.at[pl.ds(dst_at + G, G)], at(0, 0, -1))
        remote(stage, 0, src.at[pl.ds(src_at + G, G)], dst.at[pl.ds(dst_at, G)], at(0, 0, 1))

    def zone_out(stage, src, src_at, dst):
        for group, side in enumerate(SIDES):

            def send(group=group, side=side):
                for m, (dx, dy) in sorted(enumerate(PLACES), key=corners_first):
                    for f, dz in ((0, -1), (1, 1)):
                        if dx == side:
                            remote(
                                stage,
                                group,
                                src.at[pl.ds(src_at + (2 * m + f) * G, G)],
                                dst.at[pl.ds((2 * m + 1 - f) * G, G)],
                                at(-dx, -dy, dz),
                            )

            beside(-side, send)

    def give_back(stage, src, dst):
        for group, side in enumerate(SIDES):

            def send(group=group, side=side):
                for m, (dx, dy) in sorted(enumerate(PLACES), key=corners_first):
                    for b, dz in ((0, -1), (1, 1)):
                        if dx == side:
                            remote(
                                stage,
                                group,
                                src.at[pl.ds(FIRST + b * G, G)],
                                dst.at[pl.ds(PLANE + (2 * m + 1 - b) * G, G)],
                                at(dx, dy, dz),
                            )

            beside(side, send)
        plane(stage + 1, src, A, dst, 0, -1)

    def arrived(stage, buf, row, rows, sign):
        for group, side in enumerate(SIDES):
            part = buf.at[pl.ds(row + rows * group, rows)]

            def wait(group=group, part=part):
                pltpu.make_async_copy(part, part, recv_sem.at[stage, group]).wait()

            beside(sign * side, wait)

    def sent(stage, buf, row, rows, sign):
        for group, side in enumerate(SIDES):
            part = buf.at[pl.ds(row + rows * group, rows)]

            def wait(group=group, part=part):
                pltpu.make_async_copy(part, part, send_sem.at[stage, group]).wait()

            beside(sign * side, wait)

    def arrived_zone(stage, buf):
        part = buf.at[pl.ds(FIRST, 2 * G)]

        @pl.when(ix >= 0)
        def _():
            pltpu.make_async_copy(part, part, recv_sem.at[stage, 0]).wait()

    def sent_zone(stage, buf):
        part = buf.at[pl.ds(0, 2 * G)]
        pltpu.make_async_copy(part, part, send_sem.at[stage, 0]).wait()

    def clear(group):
        def fill(buf, row, rows):
            buf[pl.ds(row, rows)] = jnp.zeros((rows,) + buf.shape[1:], F32)

        fill(pos_tab, A + PLANE_PART * group, PLANE_PART)
        fill(face_all, 3 * group, 3)
        fill(zone_in, ZONE_PART * (1 - group), ZONE_PART)
        for layer in range(LAYERS):
            fill(key_tab.at[layer], A + PLANE_PART * group, PLANE_PART)
        for back in (back_0, back_1):
            fill(back, PLANE + ZONE_PART * group, ZONE_PART)
            fill(back, PLANE_PART * (1 - group), PLANE_PART)

    pl.when(ix == 0)(lambda: clear(0))
    pl.when(ix == nx - 1)(lambda: clear(1))

    sub8, lane8 = iota((G, G), 0), iota((G, G), 1)

    def column(row):
        return jnp.sum(jnp.where(sub8 == lane8, row.astype(F32), 0.0), axis=1, keepdims=True)

    loads["ps"].wait()
    lane32 = iota((G, A), 1).astype(F32)
    quads = {
        (a, b): jnp.where(column(ps[0, 0, 0, a, b : b + 1, :]) == lane32, 1.0, 0.0)
        for a in range(2)
        for b in range(2)
    }
    eye = jnp.where(iota((A, A), 0) == iota((A, A), 1), 1.0, 0.0)
    pick_f = jnp.concatenate([eye] + [quads[a, b] for _, _, a, b in BLOCKS], axis=0)
    pick = pick_f.astype(BF)
    pick_all[pl.ds(0, FIRST), :] = pick

    loads["pos"].wait()
    own_parts = split3(jnp.concatenate([pos[q, 0, 0] for q in range(3)], axis=0))

    def place_rows(part):
        wide = jnp.concatenate([part.astype(F32), jnp.zeros((128 - 3, A), F32)], axis=0)
        return mm_nt(pick, wide.astype(BF))

    place = place_rows(own_parts[0]) + place_rows(own_parts[1]) + place_rows(own_parts[2])
    pos_tab[pl.ds(0, A), :] = place[:A]
    pos_send[...] = place[A:]

    def own_keys(layer, h):
        return exact(mm, h, wk[layer]).astype(BF)

    loads["feat"].wait()
    loads["wk"].wait()
    rows = mm(pick, own_keys(0, feat[0, 0, 0]))
    key_tab[0, pl.ds(0, A), :] = rows[:A]
    key_send[pl.ds(0, PLANE), :] = rows[A:]

    pl.semaphore_wait(barrier, greeted)
    plane(0, pos_send, 0, pos_tab, A, 1)
    plane(2, key_send, 0, key_tab.at[0], A, 1)

    loads["vs"].wait()
    lane_first = iota((1, FIRST), 1)
    label_row = lane_first
    for n in range(A // G, FIRST // G):
        label_row = label_row + jnp.where(lane_first >> 3 == n, LABELS[n] - n * G, 0)
    label_row = label_row.astype(F32)
    face_f = jnp.concatenate(
        [jnp.where(column(vs[0, 0, 0, f : f + 1, :]) == label_row, 1.0, 0.0) for f in range(2)],
        axis=0,
    )
    face = face_f.astype(BF)
    face_mine[...] = face_f
    for group, side in enumerate(SIDES):

        def send_face(group=group, side=side):
            for m, (dx, dy, _) in enumerate(MESSAGES):
                if dx == side:
                    remote(4, group, face_mine, face_all.at[m], at(dx, dy, 0))

        beside(side, send_face)

    mine = (iota((A, EDGES), 1) & (A - 1)) == iota((A, EDGES), 0)
    mine_f = jnp.where(mine, 1.0, 0.0)
    mine_b = mine_f.astype(BF)
    mine_s[...] = mine_f
    edge[pl.ds(ROWS, A), :] = mine_b
    edge[pl.ds(SELF, DEPTH - SELF), :] = jnp.zeros((DEPTH - SELF, EDGES), BF)
    dlat[pl.ds(C, 128), :] = jnp.zeros((128, EDGES), BF)
    for back in (back_0, back_1):
        back[pl.ds(BACK, DEPTH - BACK), :] = jnp.zeros((DEPTH - BACK, back.shape[1]), F32)
    slot_pick = jnp.where((iota((S, EDGES), 1) >> 5) == iota((S, EDGES), 0), 1.0, 0.0).astype(BF)
    loads["nbr"].wait()
    nbr_all = mm(nbr[0, 0, 0].astype(F32).astype(BF), slot_pick)
    nbr_row = jnp.sum(jnp.where(mine, nbr_all, 0.0), axis=0, keepdims=True)
    loads["cnt"].wait()
    cnt_rows = jnp.broadcast_to(cnt[0, 0].astype(F32), (16, A)).astype(BF)
    cnt_row = mm(cnt_rows, mine_b)[0:1]
    live = jnp.where((iota((1, EDGES), 1) >> 5).astype(F32) < cnt_row, 1.0, 0.0)
    def rest(layer, queries):
        radial_h, radial_l = split(wr[layer])
        radial_h, radial_l = radial_h.astype(F32), radial_l.astype(F32)
        zeros = jnp.zeros((DEPTH - SELF - 3 * NB, C), F32)
        rest_s[layer] = jnp.concatenate([queries, radial_h, radial_h, radial_l, zeros], axis=0)

    loads["wq"].wait()
    loads["wr"].wait()
    loads["wm"].wait()
    loads["wv"].wait()
    loads["wh"].wait()
    loads["we"].wait()
    h0 = feat[0, 0, 0]
    rest(0, exact(mm, h0, wq[0]))
    base_s[...] = exact(mm, h0, wk[1])
    joint[4], joint[5] = split(wk[0])
    for n, (mixing, after) in enumerate(((wm[0], wk[1]), (wm[1], wh[...]))):
        after_h, after_l = split(after)
        joint_h, joint_l = split(FACTOR * (mm(mixing, after_h) + mm(mixing, after_l)))
        joint[2 * n] = joint_h
        joint[2 * n + 1] = joint_l
    arrived(0, pos_tab, A, PLANE_PART, -1)
    first = pos_tab[pl.ds(0, FIRST), :]
    rows = sum(mm(face, part) for part in split3(first))
    span = BOX_SIDE * nz
    low_shift = jnp.where(iz == 0, span, 0.0).astype(F32)
    high_shift = jnp.where(iz == nz - 1, -span, 0.0).astype(F32)
    shift = jnp.where(iota((2 * G, 128), 0) < G, low_shift, high_shift)
    pos_face[...] = rows + jnp.where(iota((2 * G, 128), 1) == 2, shift, 0.0)
    zone(1, pos_face, 0, pos_tab, FIRST)

    arrived(2, key_tab.at[0], A, PLANE_PART, -1)
    face_send[...] = mm(face, key_tab[0, pl.ds(0, FIRST), :].astype(BF))
    zone(3, face_send, 0, key_tab.at[0], FIRST)

    tile = iota((16, EDGES), 0)
    for n in range(ROWS // 16):
        low, high = LABELS[2 * n], LABELS[2 * n + 1]
        label = jnp.where(tile < G, tile + low, tile + (high - G)).astype(F32)
        edge[pl.ds(16 * n, 16), :] = jnp.where(nbr_row == label, 1.0, 0.0).astype(BF)

    for group, side in enumerate(SIDES):
        slots = face_all.at[pl.ds(3 * group, 2 if side == 0 else 3)]

        def wait_face(group=group, slots=slots):
            pltpu.make_async_copy(slots, slots, recv_sem.at[4, group]).wait()

        beside(-side, wait_face)
    lane = iota((2 * G, FIRST), 1)
    parts, starts = [], [A]
    for _, _, quads in MESSAGES:
        starts.append(starts[-1] + G * len(quads))
    for m, (dx, dy) in enumerate(PLACES):
        if (dx, dy) == (0, 0):
            parts.append(jnp.where(lane < A, face_f, 0.0))
        else:
            to = PLACES.index((-dx, -dy))
            within = (lane >= starts[to]) & (lane < starts[to + 1])
            parts.append(jnp.where(within, face_all[m], 0.0))
    given = mm(jnp.concatenate(parts, axis=0).astype(BF), pick)
    pick_all[pl.ds(FIRST, ZONE), :] = given.astype(BF)
    pick_back[...] = jnp.concatenate(
        [pick_f[A:], given, jnp.zeros((DEPTH - BACK, A), F32)], axis=0
    ).T.astype(BF)

    arrived_zone(1, pos_tab)
    place = jnp.concatenate(
        [pos_tab[...], -pos_tab[pl.ds(0, A), :], jnp.zeros((DEPTH - SELF, 128), F32)], axis=0
    )
    place_t = place.T[0:G, :]
    parts = [part.astype(F32) for part in split3(place_t)] + [jnp.zeros((G, DEPTH), F32)]
    offset = mm(jnp.concatenate(parts, axis=0).astype(BF), edge[...])
    offset = offset[0:G] + (offset[G : 2 * G] + offset[2 * G : 3 * G])
    dist = jnp.sqrt(jnp.sum(offset * offset, axis=0, keepdims=True) + SOFTEN)
    inv = 1.0 / dist
    scaled = dist * (1.0 / CUTOFF)
    gap = 1.0 - scaled * scaled
    inside = jnp.where(scaled < 1.0, live, 0.0)
    envelope = inside * gap * gap
    unit = offset * inv
    order = (iota((NB, EDGES), 0) + 1).astype(F32)
    turn = order * scaled
    whole = jnp.floor(turn + 0.5)
    angle = (turn - whole) * math.pi
    sign = 1.0 - 2.0 * (whole - 2.0 * jnp.floor(0.5 * whole))
    sq = angle * angle
    sine, cosine = jnp.zeros_like(sq), jnp.zeros_like(sq)
    for n in range(6, -1, -1):
        sine = sine * sq + (-1.0) ** n / math.factorial(2 * n + 1)
        cosine = cosine * sq + (-1.0) ** n / math.factorial(2 * n)
    inv_scaled = CUTOFF * inv
    basis = sign * sine * angle * inv_scaled
    dbasis_s[...] = (order * math.pi * sign * cosine - basis) * inv_scaled
    unit_s[...] = unit
    geo[...] = jnp.concatenate(
        [envelope, inv, -4.0 * inside * gap * scaled, jnp.zeros((5, EDGES), F32)], axis=0
    )
    basis_h, basis_l = split(basis)
    basis_h, basis_l = basis_h.astype(F32), basis_l.astype(F32)
    edge[pl.ds(SELF, 32), :] = jnp.concatenate(
        [basis_h, basis_l, basis_h, jnp.zeros_like(basis)], axis=0
    ).astype(BF)
    for q in range(4):
        row = envelope if q == 0 else envelope * unit[q - 1 : q]
        w_h, w_l = split(row * mine_s[...])
        weight[pl.ds(A * q, A), :] = w_h
        weight[pl.ds(4 * A + A * q, A), :] = w_l

    def near_keys(layer):
        mt[:, pl.ds(0, FIRST)] = (0.5 * key_tab[layer, pl.ds(0, FIRST), :]).T.astype(BF)

    def forward(layer, zone_rows):
        rows = jnp.concatenate([zone_rows, rest_s[layer]], axis=0)
        mt[:, pl.ds(FIRST, DEPTH - FIRST)] = (0.5 * rows).T.astype(BF)
        for n in range(CHUNKS):
            part = pl.ds(n * STEP, STEP)
            half = mm(mt[...], edge[:, part])
            turned = jnp.tanh(half)
            more = 1.0 + turned
            active = (half * more).astype(BF)
            act[layer, :, part] = active
            slope[layer, :, part] = more * (1.0 + half * (1.0 - turned))
        total = mm_nt(weight[...], act[layer])
        total = total[: 4 * A] + total[4 * A :]
        gather_s[...] = total
        return total

    def vectors(layer):
        vec_h, vec_l = split(gather_s[pl.ds(A, 3 * A), :])
        vector = FACTOR * (mm_nt(vec_h, wv[layer]) + mm_nt(vec_l, wv[layer]))
        vec_s[layer] = vector
        dv_h, dv_l = split(vector * (2.0 / CT))
        gx = FACTOR * (mm(dv_h, wv[layer]) + mm(dv_l, wv[layer]))
        pull_s[layer, pl.ds(A, 3 * A), :] = gx.astype(BF)
        flipped = jnp.concatenate([jnp.zeros((A, C), F32), 0.5 * gx], axis=0).T.astype(BF)
        mp[layer, :, pl.ds(0, 4 * A)] = flipped
        mp[layer, :, pl.ds(4 * A, 4 * A)] = flipped

    def thrice(product, a, b_h, b_l):
        return product(a.astype(BF), b_h)

    near_keys(0)

    arrived_zone(3, key_tab.at[0])
    total = forward(0, key_tab[0, pl.ds(FIRST, 2 * G), :])
    keys = base_s[...] + thrice(mm, total[:A], joint[0], joint[1])
    rows = mm(pick_all[...], keys.astype(BF))
    key_tab[1, pl.ds(0, A), :] = rows[:A]
    sent(2, key_send, 0, PLANE_PART, 1)
    key_send[...] = rows[A:]
    zone_out(6, key_send, PLANE, zone_in)
    plane(5, key_send, 0, key_tab.at[1], A, 1)

    gather_h, gather_l = split(gather_s[pl.ds(0, A), :])
    h1 = feat[0, 0, 0] + FACTOR * (mm(gather_h, wm[0]) + mm(gather_l, wm[0]))
    rest(1, exact(mm, h1, wq[1]))
    base_s[...] = exact(mm, h1, wh[...])
    vectors(0)
    arrived(5, key_tab.at[1], A, PLANE_PART, -1)
    near_keys(1)
    arrived(6, zone_in, 0, ZONE_PART, 1)
    zone_rows = zone_in[pl.ds(0, 2 * G), :]
    for m in range(1, len(PLACES)):
        zone_rows = zone_rows + zone_in[pl.ds(2 * G * m, 2 * G), :]
    total = forward(1, zone_rows)

    lat = base_s[...] + thrice(mm, total[:A], joint[2], joint[3])
    gate = 0.5 * jnp.tanh(0.5 * lat) + 0.5
    hidden = lat * gate
    readout = we[...]
    dhead = readout * (gate + hidden * (1.0 - gate))
    head_s[...] = dhead
    hidden_s[...] = hidden * readout
    vectors(1)

    def set_pull(layer, g0, g0_t):
        pull_s[layer, pl.ds(0, A), :] = g0.astype(BF)
        half = (0.5 * g0_t).astype(BF)
        mp[layer, :, pl.ds(0, A)] = half
        mp[layer, :, pl.ds(4 * A, A)] = half

    def flip(a, b):
        return mm_nt(b, a)

    def places(part, du, dbasis):
        unit, inv = unit_s[:, part], geo[1:2, part]
        along = jnp.sum(du * unit, axis=0, keepdims=True)
        dscaled = geo[2:3, part] * (du[3:4] + along) + jnp.sum(
            dbasis * dbasis_s[:, part], axis=0, keepdims=True
        )
        spread = geo[0:1, part] * inv
        return du * spread + unit * (dscaled * (1.0 / CUTOFF) - spread * along)

    def backward(layer):
        radial_h, radial_l = split(wr[layer])
        radial = jnp.concatenate([radial_h.astype(F32), radial_l.astype(F32)], axis=0).astype(BF)
        for n in range(CHUNKS):
            part = pl.ds(n * STEP, STEP)
            dl = (mm(mp[layer], weight[:, part]) * slope[layer, :, part]).astype(BF)
            dlat[pl.ds(0, C), part] = dl
            cross = mm(pull_s[layer], act[layer, :, part])
            rows = [
                jnp.sum(cross[A * q : A * q + A] * mine_s[:, :STEP], axis=0, keepdims=True)
                for q in range(4)
            ]
            rows = jnp.concatenate(rows[1:] + rows[:1] + [jnp.zeros((4, STEP), F32)], axis=0)
            got = mm(radial, dl)
            got = got[:NB] + got[NB:]
            if layer == LAYERS - 1:
                dw[:, part] = rows
                db[:, part] = got
            else:
                dr_h, dr_l = split(places(part, dw[:, part] + rows, db[:, part] + got))
                both = jnp.concatenate([dr_h.astype(F32), dr_l.astype(F32)], axis=0)
                dlat[pl.ds(C, 2 * G), part] = both.astype(BF)
        mine, back = (dkey_0, back_0) if layer == 0 else (dkey_1, back_1)
        drows = mm_nt(edge[pl.ds(0, SELF), :], dlat[pl.ds(0, mine.shape[1]), :])
        mine[...] = drows[:ROWS]
        give_back(7 + 2 * layer, mine, back)
        query_s[...] = drows[ROWS:, :C]
        if layer == 0:
            pos_own_s[...] = drows[ROWS:, C:]

    def collect(own, back):
        return own + mm(pick_back[...], back.astype(BF))

    def returned(layer):
        mine, back = (dkey_0, back_0) if layer == 0 else (dkey_1, back_1)
        arrived(8 + 2 * layer, back, 0, PLANE_PART, 1)
        arrived(7 + 2 * layer, back, PLANE, ZONE_PART, -1)
        return collect(mine[pl.ds(0, A), :], back[...])

    set_pull(1, thrice(mm_nt, dhead, joint[2], joint[3]), thrice(flip, dhead, joint[2], joint[3]))
    backward(1)

    square = vec_s[0] * vec_s[0] + vec_s[1] * vec_s[1]
    square = square[:A] + (square[A : 2 * A] + square[2 * A :])
    energy = jnp.sum(hidden_s[...], axis=1, keepdims=True) + jnp.sum(
        square, axis=1, keepdims=True
    ) * (1.0 / CT)
    en_out[0, 0] = jnp.sum(
        jnp.where(iota((A, A), 0) == iota((A, A), 1), energy, 0.0), axis=0, keepdims=True
    )
    dh = exact(mm_nt, head_s[...], wh[...]) + exact(mm_nt, query_s[...], wq[1])
    dh_s[...] = dh
    dh_h, dh_l = split(FACTOR * dh)
    base_s[...] = mm_nt(dh_h, wm[0]) + mm_nt(dh_l, wm[0])
    base_t[...] = mm_nt(wm[0], dh_h) + mm_nt(wm[0], dh_l)

    own = returned(1)
    set_pull(
        0,
        base_s[...] + thrice(mm_nt, own, joint[0], joint[1]),
        base_t[...] + thrice(flip, own, joint[0], joint[1]),
    )
    own_s[...] = own
    backward(0)

    dh = dh_s[...] + exact(mm_nt, own_s[...], wk[1])
    dh_s[...] = dh + exact(mm_nt, query_s[...], wq[0])
    sent(0, pos_send, 0, PLANE_PART, 1)
    sent_zone(1, pos_face)
    sent_zone(3, face_send)
    for group, side in enumerate(SIDES):
        slots = face_all.at[pl.ds(3 * group, 2 if side == 0 else 3)]

        def wait_given(group=group, slots=slots):
            pltpu.make_async_copy(slots, slots, send_sem.at[4, group]).wait()

        beside(side, wait_given)
    sent(5, key_send, 0, PLANE_PART, 1)
    sent(6, key_send, PLANE, ZONE_PART, -1)
    sent(9, back_1, PLANE, ZONE_PART, 1)
    sent(10, back_1, 0, PLANE_PART, -1)
    sent(7, back_0, PLANE, ZONE_PART, 1)
    sent(8, back_0, 0, PLANE_PART, -1)
    own = returned(0)
    grad_out[0, 0, 0] = dh_s[...] + thrice(mm_nt, own[:, :C], joint[4], joint[5])
    pos_own = own[:, C:] - pos_own_s[...]
    pos_own = jnp.concatenate([pos_own, jnp.zeros((128 - A, 128), F32)], axis=0).T
    pos_own = -(pos_own[0:G, :A] + pos_own[G : 2 * G, :A])
    for q in range(3):
        force_out[q, 0, 0] = pos_own[q : q + 1]


def hand_on(*refs):
    copies = [pltpu.make_async_copy(refs[n], refs[3 + n], refs[6].at[n]) for n in range(3)]
    for copy in copies:
        copy.start()
    for copy in copies:
        copy.wait()


def per_device(*args):
    hbm = pl.BlockSpec(memory_space=pltpu.HBM)
    vmem = pl.BlockSpec(memory_space=pltpu.VMEM)
    args = list(args)
    args[10] = args[10].swapaxes(1, 2)
    args[12] = args[12].reshape(1, C)
    args = [pltpu.with_memory_space_constraint(a, pltpu.HBM) for a in args]
    f32, bf = (lambda *shape: pltpu.VMEM(shape, F32)), (lambda *shape: pltpu.VMEM(shape, BF))
    out_shape = (
        jax.ShapeDtypeStruct((1, 1, 1, A), F32),
        jax.ShapeDtypeStruct((3, 1, 1, 1, A), F32),
        jax.ShapeDtypeStruct((1, 1, 1, A, C), F32),
    )
    results = pl.pallas_call(
        kernel,
        out_shape=tuple(pltpu.VMEM(a.shape, a.dtype) for a in out_shape),
        in_specs=[hbm] * len(args),
        out_specs=(vmem,) * 3,
        scratch_shapes=[pltpu.VMEM(a.shape, a.dtype) for a in args]
        + [
            f32(2 * G, 128), f32(len(MESSAGES), 2 * G, 128), f32(ROWS, 128), f32(PLANE, 128),
            f32(2 * G, 128),
            f32(LAYERS, ROWS, C), f32(BACK, C), f32(2 * G, C), f32(ZONE, C),
            f32(ROWS, C + 128), f32(ROWS, C), f32(DEPTH, C + 128), f32(DEPTH, C),
            bf(FIRST + ZONE, A), bf(A, DEPTH), f32(A, EDGES), f32(8, EDGES), f32(G, EDGES),
            f32(NB, EDGES), bf(DEPTH, EDGES), bf(8 * A, EDGES), bf(LAYERS, C, EDGES),
            f32(LAYERS, C, EDGES), bf(C + 128, EDGES),
            bf(C, DEPTH), bf(LAYERS, C, 8 * A), f32(8, EDGES), f32(NB, EDGES),
            f32(A, C), f32(C, A), f32(A, C), f32(A, C), f32(A, C), f32(A, C), f32(A, C),
            f32(A, 128), f32(LAYERS, DEPTH - ROWS, C), f32(4 * A, C), bf(LAYERS, 4 * A, C),
            bf(6, C, C), f32(LAYERS, 3 * A, CT),
            pltpu.SemaphoreType.DMA((13,)),
            pltpu.SemaphoreType.DMA((11, 3)),
            pltpu.SemaphoreType.DMA((11, 3)),
        ],
        compiler_params=pltpu.CompilerParams(
            collective_id=0, has_side_effects=True, vmem_limit_bytes=32 * 1024 * 1024
        ),
        cost_estimate=pl.CostEstimate(
            flops=2_500_000_000, bytes_accessed=2_000_000, transcendentals=800_000
        ),
    )(*args)
    return pl.pallas_call(
        hand_on,
        out_shape=out_shape,
        in_specs=[vmem] * 3,
        out_specs=(hbm,) * 3,
        scratch_shapes=[pltpu.SemaphoreType.DMA((3,))],
        compiler_params=pltpu.CompilerParams(vmem_limit_bytes=32 * 1024 * 1024),
    )(*[pltpu.with_memory_space_constraint(a, pltpu.VMEM) for a in results])


def solution(mesh):
    return jax.shard_map(
        per_device,
        mesh=mesh,
        in_specs=(
            P(None, "gx", "gy", "gz", None),
            P("gx", "gy", "gz", None, None),
            P("gx", "gy", "gz", None, None, None),
            P("gx", "gy", "gz", None, None),
            P("gx", "gy", "gz", None, None),
            P("gx", "gy", "gz", None),
            P(),
            P(),
            P(),
            P(),
            P(),
            P(),
            P(),
        ),
        out_specs=(
            P("gx", "gy", "gz", None),
            P(None, "gx", "gy", "gz", None),
            P("gx", "gy", "gz", None, None),
        ),
        check_vma=False,
    )
```

```python
import math

import jax
import jax.numpy as jnp
from jax import lax
from jax.experimental import pallas as pl
from jax.experimental.pallas import tpu as pltpu
from jax.sharding import PartitionSpec as P

A, S, C, CT, NB, G = 32, 48, 256, 64, 8, 8
LAYERS = 2
EDGES = A * S
STEP = 256
CHUNKS = EDGES // STEP
CUTOFF, SOFTEN, BOX_SIDE = 6.0, 0.25, 4.0
FACTOR = 1.0 / math.sqrt(S)
F32, BF = jnp.float32, jnp.bfloat16

MESSAGES = (
    (1, 0, ((1, 0), (1, 1))),
    (1, 1, ((1, 1),)),
    (1, -1, ((1, 0),)),
    (-1, 0, ((0, 0), (0, 1))),
    (-1, 1, ((0, 1),)),
    (-1, -1, ((0, 0),)),
    (0, 1, ((0, 1), (1, 1))),
    (0, -1, ((0, 0), (1, 0))),
)
SIDES = (1, -1, 0)
BLOCKS = tuple((dx, dy, a, b) for dx, dy, quads in MESSAGES for a, b in quads)
PLANE = G * len(BLOCKS)
FIRST = A + PLANE
ROWS = FIRST + 2 * G
LABELS = tuple(range(0, A, G)) + tuple(
    A + ((1 - 2 * dx + a) * 4 + 1 - 2 * dy + b) * G for dx, dy, a, b in BLOCKS
) + (A + 16 * G, A + 19 * G)
SELF = ROWS + A
DEPTH = 256
PLACES = tuple((dx, dy) for dx, dy, _ in MESSAGES) + ((0, 0),)
ZONE = 2 * G * len(PLACES)
BACK = PLANE + ZONE
PLANE_PART, ZONE_PART = PLANE // 3, ZONE // 3


def mm(a, b):
    return lax.dot_general(a, b, (((1,), (0,)), ((), ())), preferred_element_type=F32)


def mm_nt(a, b):
    return lax.dot_general(a, b, (((1,), (1,)), ((), ())), preferred_element_type=F32)


def split(x):
    hi = x.astype(BF)
    return hi, (x - hi.astype(F32)).astype(BF)


def split3(x):
    hi, rest = x.astype(BF), x - x.astype(BF).astype(F32)
    mid = rest.astype(BF)
    return hi, mid, (rest - mid.astype(F32)).astype(BF)


def exact(product, a, b):
    ah, al = split(a)
    bh, bl = split(b)
    return product(ah, bh) + (product(ah, bl) + product(al, bh))


def corners_first(place):
    return -abs(place[1][0]) - abs(place[1][1])


def iota(shape, dim):
    return lax.broadcasted_iota(jnp.int32, shape, dim)


def kernel(
    pos_in, feat_in, ps_in, vs_in, nbr_in, cnt_in, wq_in, wk_in, wr_in, wm_in, wv_in, wh_in, we_in,
    en_out, force_out, grad_out,
    pos, feat, ps, vs, nbr, cnt, wq, wk, wr, wm, wv, wh, we,
    face_mine, face_all, pos_tab, pos_send, pos_face,
    key_tab, key_send, face_send, zone_in, dkey_0, dkey_1, back_0, back_1,
    pick_all, pick_back, mine_s, geo, unit_s, dbasis_s, edge, weight, act, slope, dlat,
    mt, mp, dw, db, base_s, base_t, dh_s, own_s, query_s, head_s, hidden_s,
    pos_own_s, rest_s, gather_s, pull_s, joint, vec_s,
    load_sem, send_sem, recv_sem,
):
    ix, iy, iz = (lax.axis_index(n) for n in ("gx", "gy", "gz"))
    nx, ny, nz = (lax.axis_size(n) for n in ("gx", "gy", "gz"))

    near_x = {d: ix + d if d else ix for d in (-1, 0, 1)}
    near_y = {d: lax.rem(iy + (d + ny), ny) if d else iy for d in (-1, 0, 1)}
    near_z = {d: lax.rem(iz + (d + nz), nz) if d else iz for d in (-1, 0, 1)}

    def at(dx, dy, dz):
        return {"gx": near_x[dx], "gy": near_y[dy], "gz": near_z[dz]}

    def beside(side, action):
        if side == 0:
            pl.when(ix >= 0)(action)
        elif side == 1:
            pl.when(ix < nx - 1)(action)
        else:
            pl.when(ix > 0)(action)

    barrier = pltpu.get_barrier_semaphore()

    def greet(where):
        pl.semaphore_signal(barrier, inc=1, device_id=where, device_id_type=pl.DeviceIdType.MESH)

    greet(at(0, 0, -1))
    greet(at(0, 0, 1))
    for side in SIDES:

        def greet_side(side=side):
            for dx, dy, _ in MESSAGES:
                if dx == side:
                    greet(at(dx, dy, 0))

        beside(side, greet_side)
    greeted = 4 + 3 * (ix > 0).astype(jnp.int32) + 3 * (ix < nx - 1).astype(jnp.int32)

    loads = {}
    for n, (name, src, dst) in enumerate(
        (
            ("ps", ps_in, ps),
            ("pos", pos_in, pos),
            ("feat", feat_in, feat),
            ("wk", wk_in, wk),
            ("vs", vs_in, vs),
            ("nbr", nbr_in, nbr),
            ("cnt", cnt_in, cnt),
            ("wr", wr_in, wr),
            ("wq", wq_in, wq),
            ("wm", wm_in, wm),
            ("wv", wv_in, wv),
            ("wh", wh_in, wh),
            ("we", we_in, we),
        )
    ):
        loads[name] = pltpu.make_async_copy(src, dst, load_sem.at[n])
        loads[name].start()

    def remote(stage, group, src, dst, where):
        pltpu.make_async_remote_copy(
            src_ref=src,
            dst_ref=dst,
            send_sem=send_sem.at[stage, group],
            recv_sem=recv_sem.at[stage, group],
            device_id=where,
            device_id_type=pl.DeviceIdType.MESH,
        ).start()

    def plane(stage, src, src_at, dst, dst_at, sign):
        for group, side in enumerate(SIDES):

            def send(group=group, side=side):
                row = 0
                for dx, dy, quads in MESSAGES:
                    rows = G * len(quads)
                    if dx == side:
                        remote(
                            stage,
                            group,
                            src.at[pl.ds(src_at + row, rows)],
                            dst.at[pl.ds(dst_at + row, rows)],
                            at(sign * dx, sign * dy, 0),
                        )
                    row += rows

            send() if side == 0 else beside(sign * side, send)

    def zone(stage, src, src_at, dst, dst_at):
        remote(stage, 0, src.at[pl.ds(src_at, G)], dst.at[pl.ds(dst_at + G, G)], at(0, 0, -1))
        remote(stage, 0, src.at[pl.ds(src_at + G, G)], dst.at[pl.ds(dst_at, G)], at(0, 0, 1))

    def zone_out(stage, src, src_at, dst):
        for group, side in enumerate(SIDES):

            def send(group=group, side=side):
                for m, (dx, dy) in sorted(enumerate(PLACES), key=corners_first):
                    for f, dz in ((0, -1), (1, 1)):
                        if dx == side:
                            remote(
                                stage,
                                group,
                                src.at[pl.ds(src_at + (2 * m + f) * G, G)],
                                dst.at[pl.ds((2 * m + 1 - f) * G, G)],
                                at(-dx, -dy, dz),
                            )

            send() if side == 0 else beside(-side, send)

    def give_back(stage, src, dst):
        for group, side in enumerate(SIDES):

            def send(group=group, side=side):
                for m, (dx, dy) in sorted(enumerate(PLACES), key=corners_first):
                    for b, dz in ((0, -1), (1, 1)):
                        if dx == side:
                            remote(
                                stage,
                                group,
                                src.at[pl.ds(FIRST + b * G, G)],
                                dst.at[pl.ds(PLANE + (2 * m + 1 - b) * G, G)],
                                at(dx, dy, dz),
                            )

            send() if side == 0 else beside(side, send)
        plane(stage + 1, src, A, dst, 0, -1)

    def arrived(stage, buf, row, rows, sign):
        for group, side in enumerate(SIDES):
            part = buf.at[pl.ds(row + rows * group, rows)]

            def wait(group=group, part=part):
                pltpu.make_async_copy(part, part, recv_sem.at[stage, group]).wait()

            beside(sign * side, wait)

    def sent(stage, buf, row, rows, sign):
        for group, side in enumerate(SIDES):
            part = buf.at[pl.ds(row + rows * group, rows)]

            def wait(group=group, part=part):
                pltpu.make_async_copy(part, part, send_sem.at[stage, group]).wait()

            beside(sign * side, wait)

    def arrived_zone(stage, buf):
        part = buf.at[pl.ds(FIRST, 2 * G)]

        @pl.when(ix >= 0)
        def _():
            pltpu.make_async_copy(part, part, recv_sem.at[stage, 0]).wait()

    def sent_zone(stage, buf):
        part = buf.at[pl.ds(0, 2 * G)]
        pltpu.make_async_copy(part, part, send_sem.at[stage, 0]).wait()

    def clear(group):
        def fill(buf, row, rows):
            buf[pl.ds(row, rows)] = jnp.zeros((rows,) + buf.shape[1:], F32)

        fill(pos_tab, A + PLANE_PART * group, PLANE_PART)
        fill(face_all, 3 * group, 3)
        fill(zone_in, ZONE_PART * (1 - group), ZONE_PART)
        for layer in range(LAYERS):
            fill(key_tab.at[layer], A + PLANE_PART * group, PLANE_PART)
        for back in (back_0, back_1):
            fill(back, PLANE + ZONE_PART * group, ZONE_PART)
            fill(back, PLANE_PART * (1 - group), PLANE_PART)

    sub8, lane8 = iota((G, G), 0), iota((G, G), 1)

    def column(row):
        return jnp.sum(jnp.where(sub8 == lane8, row.astype(F32), 0.0), axis=1, keepdims=True)

    loads["ps"].wait()
    lane32 = iota((G, A), 1).astype(F32)
    quads = {
        (a, b): jnp.where(column(ps[0, 0, 0, a, b : b + 1, :]) == lane32, 1.0, 0.0)
        for a in range(2)
        for b in range(2)
    }
    eye = jnp.where(iota((A, A), 0) == iota((A, A), 1), 1.0, 0.0)
    pick_f = jnp.concatenate([eye] + [quads[a, b] for _, _, a, b in BLOCKS], axis=0)
    pick = pick_f.astype(BF)
    pick_all[pl.ds(0, FIRST), :] = pick

    loads["pos"].wait()
    own_parts = split3(jnp.concatenate([pos[q, 0, 0] for q in range(3)], axis=0))

    def place_rows(part):
        wide = jnp.concatenate([part.astype(F32), jnp.zeros((128 - 3, A), F32)], axis=0)
        return mm_nt(pick, wide.astype(BF))

    place = place_rows(own_parts[0]) + place_rows(own_parts[1]) + place_rows(own_parts[2])
    pos_tab[pl.ds(0, A), :] = place[:A]
    pos_send[...] = place[A:]

    def own_keys(layer, h):
        return exact(mm, h, wk[layer]).astype(BF)

    loads["feat"].wait()
    loads["wk"].wait()
    rows = mm(pick, own_keys(0, feat[0, 0, 0]))
    key_tab[0, pl.ds(0, A), :] = rows[:A]
    key_send[pl.ds(0, PLANE), :] = rows[A:]

    pl.semaphore_wait(barrier, greeted)
    plane(0, pos_send, 0, pos_tab, A, 1)
    plane(2, key_send, 0, key_tab.at[0], A, 1)

    loads["vs"].wait()
    lane_first = iota((1, FIRST), 1)
    label_row = lane_first
    for n in range(A // G, FIRST // G):
        label_row = label_row + jnp.where(lane_first >> 3 == n, LABELS[n] - n * G, 0)
    label_row = label_row.astype(F32)
    face_f = jnp.concatenate(
        [jnp.where(column(vs[0, 0, 0, f : f + 1, :]) == label_row, 1.0, 0.0) for f in range(2)],
        axis=0,
    )
    face = face_f.astype(BF)
    face_mine[...] = face_f
    for group, side in enumerate(SIDES):

        def send_face(group=group, side=side):
            for m, (dx, dy, _) in enumerate(MESSAGES):
                if dx == side:
                    remote(4, group, face_mine, face_all.at[m], at(dx, dy, 0))

        beside(side, send_face)

    pl.when(ix == 0)(lambda: clear(0))
    pl.when(ix == nx - 1)(lambda: clear(1))

    mine = (iota((A, EDGES), 1) & (A - 1)) == iota((A, EDGES), 0)
    mine_f = jnp.where(mine, 1.0, 0.0)
    mine_b = mine_f.astype(BF)
    mine_s[...] = mine_f
    edge[pl.ds(ROWS, A), :] = mine_b
    edge[pl.ds(SELF, DEPTH - SELF), :] = jnp.zeros((DEPTH - SELF, EDGES), BF)
    dlat[pl.ds(C, 128), :] = jnp.zeros((128, EDGES), BF)
    for back in (back_0, back_1):
        back[pl.ds(BACK, DEPTH - BACK), :] = jnp.zeros((DEPTH - BACK, back.shape[1]), F32)
    slot_pick = jnp.where((iota((S, EDGES), 1) >> 5) == iota((S, EDGES), 0), 1.0, 0.0).astype(BF)
    loads["nbr"].wait()
    nbr_all = mm(nbr[0, 0, 0].astype(F32).astype(BF), slot_pick)
    nbr_row = jnp.sum(jnp.where(mine, nbr_all, 0.0), axis=0, keepdims=True)
    loads["cnt"].wait()
    cnt_rows = jnp.broadcast_to(cnt[0, 0].astype(F32), (16, A)).astype(BF)
    cnt_row = mm(cnt_rows, mine_b)[0:1]
    live = jnp.where((iota((1, EDGES), 1) >> 5).astype(F32) < cnt_row, 1.0, 0.0)
    def rest(layer, queries):
        radial_h, radial_l = split(wr[layer])
        radial_h, radial_l = radial_h.astype(F32), radial_l.astype(F32)
        zeros = jnp.zeros((DEPTH - SELF - 3 * NB, C), F32)
        rest_s[layer] = jnp.concatenate([queries, radial_h, radial_h, radial_l, zeros], axis=0)

    loads["wq"].wait()
    loads["wr"].wait()
    loads["wm"].wait()
    loads["wv"].wait()
    loads["wh"].wait()
    loads["we"].wait()
    h0 = feat[0, 0, 0]
    rest(0, exact(mm, h0, wq[0]))
    base_s[...] = exact(mm, h0, wk[1])
    joint[4], joint[5] = split(wk[0])
    for n, (mixing, after) in enumerate(((wm[0], wk[1]), (wm[1], wh[...]))):
        after_h, after_l = split(after)
        joint_h, joint_l = split(FACTOR * (mm(mixing, after_h) + mm(mixing, after_l)))
        joint[2 * n] = joint_h
        joint[2 * n + 1] = joint_l
    arrived(0, pos_tab, A, PLANE_PART, -1)
    first = pos_tab[pl.ds(0, FIRST), :]
    rows = sum(mm(face, part) for part in split3(first))
    span = BOX_SIDE * nz
    low_shift = jnp.where(iz == 0, span, 0.0).astype(F32)
    high_shift = jnp.where(iz == nz - 1, -span, 0.0).astype(F32)
    shift = jnp.where(iota((2 * G, 128), 0) < G, low_shift, high_shift)
    pos_face[...] = rows + jnp.where(iota((2 * G, 128), 1) == 2, shift, 0.0)
    zone(1, pos_face, 0, pos_tab, FIRST)

    arrived(2, key_tab.at[0], A, PLANE_PART, -1)
    face_send[...] = mm(face, key_tab[0, pl.ds(0, FIRST), :].astype(BF))
    zone(3, face_send, 0, key_tab.at[0], FIRST)

    tile = iota((16, EDGES), 0)
    for n in range(ROWS // 16):
        low, high = LABELS[2 * n], LABELS[2 * n + 1]
        label = jnp.where(tile < G, tile + low, tile + (high - G)).astype(F32)
        edge[pl.ds(16 * n, 16), :] = jnp.where(nbr_row == label, 1.0, 0.0).astype(BF)

    for group, side in enumerate(SIDES):
        slots = face_all.at[pl.ds(3 * group, 2 if side == 0 else 3)]

        def wait_face(group=group, slots=slots):
            pltpu.make_async_copy(slots, slots, recv_sem.at[4, group]).wait()

        beside(-side, wait_face)
    lane = iota((2 * G, FIRST), 1)
    parts, starts = [], [A]
    for _, _, quads in MESSAGES:
        starts.append(starts[-1] + G * len(quads))
    for m, (dx, dy) in enumerate(PLACES):
        if (dx, dy) == (0, 0):
            parts.append(jnp.where(lane < A, face_f, 0.0))
        else:
            to = PLACES.index((-dx, -dy))
            within = (lane >= starts[to]) & (lane < starts[to + 1])
            parts.append(jnp.where(within, face_all[m], 0.0))
    given = mm(jnp.concatenate(parts, axis=0).astype(BF), pick)
    pick_all[pl.ds(FIRST, ZONE), :] = given.astype(BF)
    pick_back[...] = jnp.concatenate(
        [pick_f[A:], given, jnp.zeros((DEPTH - BACK, A), F32)], axis=0
    ).T.astype(BF)

    arrived_zone(1, pos_tab)
    place = jnp.concatenate(
        [pos_tab[...], -pos_tab[pl.ds(0, A), :], jnp.zeros((DEPTH - SELF, 128), F32)], axis=0
    )
    place_t = place.T[0:G, :]
    parts = [part.astype(F32) for part in split3(place_t)] + [jnp.zeros((G, DEPTH), F32)]
    offset = mm(jnp.concatenate(parts, axis=0).astype(BF), edge[...])
    offset = offset[0:G] + (offset[G : 2 * G] + offset[2 * G : 3 * G])
    dist = jnp.sqrt(jnp.sum(offset * offset, axis=0, keepdims=True) + SOFTEN)
    inv = 1.0 / dist
    scaled = dist * (1.0 / CUTOFF)
    gap = 1.0 - scaled * scaled
    inside = jnp.where(scaled < 1.0, live, 0.0)
    envelope = inside * gap * gap
    unit = offset * inv
    order = (iota((NB, EDGES), 0) + 1).astype(F32)
    turn = order * scaled
    whole = jnp.floor(turn + 0.5)
    angle = (turn - whole) * math.pi
    sign = 1.0 - 2.0 * (whole - 2.0 * jnp.floor(0.5 * whole))
    sq = angle * angle
    sine, cosine = jnp.zeros_like(sq), jnp.zeros_like(sq)
    for n in range(6, -1, -1):
        sine = sine * sq + (-1.0) ** n / math.factorial(2 * n + 1)
        cosine = cosine * sq + (-1.0) ** n / math.factorial(2 * n)
    inv_scaled = CUTOFF * inv
    basis = sign * sine * angle * inv_scaled
    dbasis_s[...] = (order * math.pi * sign * cosine - basis) * inv_scaled
    unit_s[...] = unit
    geo[...] = jnp.concatenate(
        [envelope, inv, -4.0 * inside * gap * scaled, jnp.zeros((5, EDGES), F32)], axis=0
    )
    basis_h, basis_l = split(basis)
    basis_h, basis_l = basis_h.astype(F32), basis_l.astype(F32)
    edge[pl.ds(SELF, 32), :] = jnp.concatenate(
        [basis_h, basis_l, basis_h, jnp.zeros_like(basis)], axis=0
    ).astype(BF)
    for q in range(4):
        row = envelope if q == 0 else envelope * unit[q - 1 : q]
        w_h, w_l = split(row * mine_s[...])
        weight[pl.ds(A * q, A), :] = w_h
        weight[pl.ds(4 * A + A * q, A), :] = w_l

    def near_keys(layer):
        mt[:, pl.ds(0, FIRST)] = (0.5 * key_tab[layer, pl.ds(0, FIRST), :]).astype(BF).T

    def forward(layer, zone_rows):
        rows = jnp.concatenate([zone_rows, rest_s[layer]], axis=0)
        mt[:, pl.ds(FIRST, DEPTH - FIRST)] = (0.5 * rows).astype(BF).T
        for n in range(CHUNKS):
            part = pl.ds(n * STEP, STEP)
            half = mm(mt[...], edge[:, part])
            turned = jnp.tanh(half)
            more = 1.0 + turned
            active = (half * more).astype(BF)
            act[layer, :, part] = active
            slope[layer, :, part] = more * (1.0 + half * (1.0 - turned))
        total = mm_nt(weight[...], act[layer])
        total = total[: 4 * A] + total[4 * A :]
        gather_s[...] = total
        return total

    def vectors(layer):
        vec_h, vec_l = split(gather_s[pl.ds(A, 3 * A), :])
        vector = FACTOR * (mm_nt(vec_h, wv[layer]) + mm_nt(vec_l, wv[layer]))
        vec_s[layer] = vector
        gx = FACTOR * mm((vector * (2.0 / CT)).astype(BF), wv[layer])
        pull_s[layer, pl.ds(A, 3 * A), :] = gx.astype(BF)
        flipped = jnp.concatenate([jnp.zeros((A, C), F32), 0.5 * gx], axis=0).astype(BF).T
        mp[layer, :, pl.ds(0, 4 * A)] = flipped
        mp[layer, :, pl.ds(4 * A, 4 * A)] = flipped

    def thrice(product, a, b_h, b_l):
        return product(a.astype(BF), b_h)

    near_keys(0)

    arrived_zone(3, key_tab.at[0])
    total = forward(0, key_tab[0, pl.ds(FIRST, 2 * G), :])
    keys = base_s[...] + thrice(mm, total[:A], joint[0], joint[1])
    rows = mm(pick_all[...], keys.astype(BF))
    key_tab[1, pl.ds(0, A), :] = rows[:A]
    sent(2, key_send, 0, PLANE_PART, 1)
    key_send[...] = rows[A:]
    zone_out(6, key_send, PLANE, zone_in)
    plane(5, key_send, 0, key_tab.at[1], A, 1)

    gather_h, gather_l = split(gather_s[pl.ds(0, A), :])
    h1 = feat[0, 0, 0] + FACTOR * (mm(gather_h, wm[0]) + mm(gather_l, wm[0]))
    rest(1, exact(mm, h1, wq[1]))
    base_s[...] = exact(mm, h1, wh[...])
    vectors(0)
    arrived(5, key_tab.at[1], A, PLANE_PART, -1)
    near_keys(1)
    arrived(6, zone_in, 0, ZONE_PART, 1)
    zone_rows = zone_in[pl.ds(0, 2 * G), :]
    for m in range(1, len(PLACES)):
        zone_rows = zone_rows + zone_in[pl.ds(2 * G * m, 2 * G), :]
    total = forward(1, zone_rows)

    lat = base_s[...] + thrice(mm, total[:A], joint[2], joint[3])
    gate = 0.5 * jnp.tanh(0.5 * lat) + 0.5
    hidden = lat * gate
    readout = we[...]
    dhead = readout * (gate + hidden * (1.0 - gate))
    head_s[...] = dhead
    hidden_s[...] = hidden * readout
    vectors(1)

    def set_pull(layer, g0, g0_t):
        pull_s[layer, pl.ds(0, A), :] = g0.astype(BF)
        half = (0.5 * g0_t).astype(BF)
        mp[layer, :, pl.ds(0, A)] = half
        mp[layer, :, pl.ds(4 * A, A)] = half

    def flip(a, b):
        return mm_nt(b, a)

    def places(part, du, dbasis):
        unit, inv = unit_s[:, part], geo[1:2, part]
        along = jnp.sum(du * unit, axis=0, keepdims=True)
        dscaled = geo[2:3, part] * (du[3:4] + along) + jnp.sum(
            dbasis * dbasis_s[:, part], axis=0, keepdims=True
        )
        spread = geo[0:1, part] * inv
        return du * spread + unit * (dscaled * (1.0 / CUTOFF) - spread * along)

    def backward(layer):
        radial_h, radial_l = split(wr[layer])
        radial = jnp.concatenate([radial_h.astype(F32), radial_l.astype(F32)], axis=0).astype(BF)
        for n in range(CHUNKS):
            part = pl.ds(n * STEP, STEP)
            dl = (mm(mp[layer], weight[:, part]) * slope[layer, :, part]).astype(BF)
            dlat[pl.ds(0, C), part] = dl
            cross = mm(pull_s[layer], act[layer, :, part])
            rows = [
                jnp.sum(cross[A * q : A * q + A] * mine_s[:, :STEP], axis=0, keepdims=True)
                for q in range(4)
            ]
            rows = jnp.concatenate(rows[1:] + rows[:1] + [jnp.zeros((4, STEP), F32)], axis=0)
            got = mm(radial, dl)
            got = got[:NB] + got[NB:]
            if layer == LAYERS - 1:
                dw[:, part] = rows
                db[:, part] = got
            else:
                dr_h, dr_l = split(places(part, dw[:, part] + rows, db[:, part] + got))
                both = jnp.concatenate([dr_h.astype(F32), dr_l.astype(F32)], axis=0)
                dlat[pl.ds(C, 2 * G), part] = both.astype(BF)
        mine, back = (dkey_0, back_0) if layer == 0 else (dkey_1, back_1)
        drows = mm_nt(edge[pl.ds(0, SELF), :], dlat[pl.ds(0, mine.shape[1]), :])
        mine[...] = drows[:ROWS]
        give_back(7 + 2 * layer, mine, back)
        query_s[...] = drows[ROWS:, :C]
        if layer == 0:
            pos_own_s[...] = drows[ROWS:, C:]

    def collect(own, back):
        return own + mm(pick_back[...], back.astype(BF))

    def returned(layer):
        mine, back = (dkey_0, back_0) if layer == 0 else (dkey_1, back_1)
        arrived(8 + 2 * layer, back, 0, PLANE_PART, 1)
        arrived(7 + 2 * layer, back, PLANE, ZONE_PART, -1)
        return collect(mine[pl.ds(0, A), :], back[...])

    set_pull(1, thrice(mm_nt, dhead, joint[2], joint[3]), thrice(flip, dhead, joint[2], joint[3]))
    backward(1)

    square = vec_s[0] * vec_s[0] + vec_s[1] * vec_s[1]
    square = square[:A] + (square[A : 2 * A] + square[2 * A :])
    energy = jnp.sum(hidden_s[...], axis=1, keepdims=True) + jnp.sum(
        square, axis=1, keepdims=True
    ) * (1.0 / CT)
    en_out[0, 0] = jnp.sum(
        jnp.where(iota((A, A), 0) == iota((A, A), 1), energy, 0.0), axis=0, keepdims=True
    )
    dh = exact(mm_nt, head_s[...], wh[...]) + exact(mm_nt, query_s[...], wq[1])
    dh_s[...] = dh
    dh_h, dh_l = split(FACTOR * dh)
    base_s[...] = mm_nt(dh_h, wm[0]) + mm_nt(dh_l, wm[0])
    base_t[...] = mm_nt(wm[0], dh_h) + mm_nt(wm[0], dh_l)

    own = returned(1)
    set_pull(
        0,
        base_s[...] + thrice(mm_nt, own, joint[0], joint[1]),
        base_t[...] + thrice(flip, own, joint[0], joint[1]),
    )
    own_s[...] = own
    backward(0)

    dh = dh_s[...] + exact(mm_nt, own_s[...], wk[1])
    dh_s[...] = dh + exact(mm_nt, query_s[...], wq[0])
    sent(0, pos_send, 0, PLANE_PART, 1)
    sent_zone(1, pos_face)
    sent_zone(3, face_send)
    for group, side in enumerate(SIDES):
        slots = face_all.at[pl.ds(3 * group, 2 if side == 0 else 3)]

        def wait_given(group=group, slots=slots):
            pltpu.make_async_copy(slots, slots, send_sem.at[4, group]).wait()

        beside(side, wait_given)
    sent(5, key_send, 0, PLANE_PART, 1)
    sent(6, key_send, PLANE, ZONE_PART, -1)
    sent(9, back_1, PLANE, ZONE_PART, 1)
    sent(10, back_1, 0, PLANE_PART, -1)
    sent(7, back_0, PLANE, ZONE_PART, 1)
    sent(8, back_0, 0, PLANE_PART, -1)
    own = returned(0)
    grad_out[0, 0, 0] = dh_s[...] + thrice(mm_nt, own[:, :C], joint[4], joint[5])
    pos_own = own[:, C:] - pos_own_s[...]
    pos_own = jnp.concatenate([pos_own, jnp.zeros((128 - A, 128), F32)], axis=0).T
    pos_own = -(pos_own[0:G, :A] + pos_own[G : 2 * G, :A])
    for q in range(3):
        force_out[q, 0, 0] = pos_own[q : q + 1]


def hand_on(*refs):
    copies = [pltpu.make_async_copy(refs[n], refs[3 + n], refs[6].at[n]) for n in range(3)]
    for copy in copies:
        copy.start()
    for copy in copies:
        copy.wait()


def per_device(*args):
    hbm = pl.BlockSpec(memory_space=pltpu.HBM)
    vmem = pl.BlockSpec(memory_space=pltpu.VMEM)
    args = list(args)
    args[10] = args[10].swapaxes(1, 2)
    args[12] = args[12].reshape(1, C)
    args = [pltpu.with_memory_space_constraint(a, pltpu.HBM) for a in args]
    f32, bf = (lambda *shape: pltpu.VMEM(shape, F32)), (lambda *shape: pltpu.VMEM(shape, BF))
    out_shape = (
        jax.ShapeDtypeStruct((1, 1, 1, A), F32),
        jax.ShapeDtypeStruct((3, 1, 1, 1, A), F32),
        jax.ShapeDtypeStruct((1, 1, 1, A, C), F32),
    )
    results = pl.pallas_call(
        kernel,
        out_shape=tuple(pltpu.VMEM(a.shape, a.dtype) for a in out_shape),
        in_specs=[hbm] * len(args),
        out_specs=(vmem,) * 3,
        scratch_shapes=[pltpu.VMEM(a.shape, a.dtype) for a in args]
        + [
            f32(2 * G, 128), f32(len(MESSAGES), 2 * G, 128), f32(ROWS, 128), f32(PLANE, 128),
            f32(2 * G, 128),
            f32(LAYERS, ROWS, C), f32(BACK, C), f32(2 * G, C), f32(ZONE, C),
            f32(ROWS, C + 128), f32(ROWS, C), f32(DEPTH, C + 128), f32(DEPTH, C),
            bf(FIRST + ZONE, A), bf(A, DEPTH), f32(A, EDGES), f32(8, EDGES), f32(G, EDGES),
            f32(NB, EDGES), bf(DEPTH, EDGES), bf(8 * A, EDGES), bf(LAYERS, C, EDGES),
            f32(LAYERS, C, EDGES), bf(C + 128, EDGES),
            bf(C, DEPTH), bf(LAYERS, C, 8 * A), f32(8, EDGES), f32(NB, EDGES),
            f32(A, C), f32(C, A), f32(A, C), f32(A, C), f32(A, C), f32(A, C), f32(A, C),
            f32(A, 128), f32(LAYERS, DEPTH - ROWS, C), f32(4 * A, C), bf(LAYERS, 4 * A, C),
            bf(6, C, C), f32(LAYERS, 3 * A, CT),
            pltpu.SemaphoreType.DMA((13,)),
            pltpu.SemaphoreType.DMA((11, 3)),
            pltpu.SemaphoreType.DMA((11, 3)),
        ],
        compiler_params=pltpu.CompilerParams(
            collective_id=0, has_side_effects=True, vmem_limit_bytes=32 * 1024 * 1024
        ),
        cost_estimate=pl.CostEstimate(
            flops=2_500_000_000, bytes_accessed=2_000_000, transcendentals=800_000
        ),
    )(*args)
    return pl.pallas_call(
        hand_on,
        out_shape=out_shape,
        in_specs=[vmem] * 3,
        out_specs=(hbm,) * 3,
        scratch_shapes=[pltpu.SemaphoreType.DMA((3,))],
        compiler_params=pltpu.CompilerParams(vmem_limit_bytes=32 * 1024 * 1024),
    )(*[pltpu.with_memory_space_constraint(a, pltpu.VMEM) for a in results])


def solution(mesh):
    return jax.shard_map(
        per_device,
        mesh=mesh,
        in_specs=(
            P(None, "gx", "gy", "gz", None),
            P("gx", "gy", "gz", None, None),
            P("gx", "gy", "gz", None, None, None),
            P("gx", "gy", "gz", None, None),
            P("gx", "gy", "gz", None, None),
            P("gx", "gy", "gz", None),
            P(),
            P(),
            P(),
            P(),
            P(),
            P(),
            P(),
        ),
        out_specs=(
            P("gx", "gy", "gz", None),
            P(None, "gx", "gy", "gz", None),
            P("gx", "gy", "gz", None, None),
        ),
        check_vma=False,
    )
```
